32 devices in a mesh: row: 8 (over y, x, core), col: 4 (over z).
Axes of the slice: x: 2, y: 2, z: 4, core: 2. Of those that a mesh axis runs over, the one named last changes fastest.
Arguments:
- a_vals: float32 [128, 512, 128], P('row', 'col'), may hold values from -6 to 6
- a_code: int32 [128, 4], P('row', 'col'), may hold values from -1 to 63, as said below
- b_vals: float32 [96, 512, 128], P('row', 'col'), may hold values from -0.25 to 0.25
- b_code: int32 [96, 4], P('row', 'col'), may hold values from -1 to 255, as said below
- panels: int32 [4], replicated, may hold values from 0 to 3, as said below
Outputs:
- c_band: float32 [1024, 4096], P('row', 'col')
The draws below stay inside these ranges and needn't reach their ends.
Inputs may be any that keep to these rules, and one draw needn't show every extreme that they name: `a_code`: used slots of each device come first and name distinct block columns; empty slots hold -1; every device uses half or more of its 16 slots and some device uses all of them. `b_code`: used slots of each device come first and name distinct blocks; empty slots hold -1; every device uses half or more of its 12 slots and some device uses all of them. `panels`: each panel number appears once.
All inputs are finite; a program needn't handle non-finite values.
Results may differ from the reference program's by a relative error of at most 0.0003.
Values sent between devices are 32-bit elements; how exact they have to be, the bound alone decides.
No kernel may reach another device: no remote copies, remote signals or barrier semaphores. Data moves between devices by JAX's collectives and lax.ppermute only.
A program may use at most 64 MiB of HBM per device.

```python
import jax
import jax.numpy as jnp
from jax import lax

BLK = 128
KPB = 64
STEPS = 2
SA = 16
SB = 12
JB = 8
NBROW = 8
NPANEL = 4
KROWS = 32


def slot_codes(key, capacity, cells):
    devices = NBROW * NPANEL
    keys = jax.random.split(key, devices + 1)
    full_device = jax.random.randint(keys[devices], (), 0, devices)

    def one_device(dev_key, dev_id):
        perm_key, count_key = jax.random.split(dev_key)
        chosen = jax.random.permutation(perm_key, cells)[:capacity]
        used = jax.random.randint(count_key, (), capacity // 2, capacity + 1)
        used = jnp.where(dev_id == full_device, capacity, used)
        slots = jnp.arange(capacity)
        return jnp.where(slots < used, chosen, -1).astype(jnp.int32)
    codes = jax.vmap(one_device)(keys[:devices], jnp.arange(devices))
    codes = codes.reshape(NBROW, NPANEL, capacity).transpose(0, 2, 1)
    return codes.reshape(NBROW * capacity, NPANEL)


def draw_a_code(key, part):
    return slot_codes(jax.random.fold_in(key, 11), SA, KPB)


def draw_b_code(key, part):
    return slot_codes(jax.random.fold_in(key, 23), SB, KROWS * JB)


def draw_panels(key, part):
    return jax.random.permutation(jax.random.fold_in(key, 37), NPANEL).astype(jnp.int32)


def levels(stream_key, shape, cuts, smallest, largest):
    def one(axis_at, shards_of):
        heights = jax.random.uniform(jax.random.fold_in(jax.random.fold_in(stream_key, 6), axis_at), (shards_of,), jnp.float32, smallest / len(cuts), largest / len(cuts))
        return jnp.repeat(jnp.exp(heights), shape[axis_at] // shards_of).reshape((-1,) + (1,) * (len(shape) - axis_at - 1))

    loudness = one(*cuts[0])
    for cut in cuts[1:]:
        loudness = loudness * one(*cut)
    return loudness


def noise(key, shape, spread, limit, pieces=(), held_as=jnp.bfloat16):
    values = spread * jax.random.normal(key, shape, jnp.float32)
    if pieces:
        values = values * levels(key, shape, pieces, -0.22, 0.18)
    return jnp.clip(values, -limit, limit).astype(held_as)


def setup_inputs(seed: int = 0) -> dict:
    key_list = jax.random.split(jax.random.key(seed), 6)
    return {
        "a_vals": noise(key_list[0], (NBROW * SA, NPANEL * BLK, BLK), 1.0, 6.0, ((0, 8), (1, 4)), jnp.float32),
        "a_code": draw_a_code(jax.random.fold_in(key_list[5], 71), 0),
        "b_vals": noise(key_list[2], (NBROW * SB, NPANEL * BLK, BLK), (4 * BLK) ** -0.5, 0.25, ((0, 8), (1, 4)), jnp.float32),
        "b_code": draw_b_code(jax.random.fold_in(key_list[5], 71), 0),
        "panels": draw_panels(jax.random.fold_in(key_list[5], 71), 0),
    }


def panel_product(left_vals, left_cols, right_vals, right_codes, per_dev, k_rows):
    slots = right_vals.shape[0]
    blk = right_vals.shape[1]
    valid = right_codes >= 0
    offset = (jnp.arange(slots, dtype=jnp.int32) // per_dev) * k_rows
    k_need = jnp.where(valid, offset + right_codes // JB, -1)
    j_need = right_codes % JB
    match = (k_need[:, None] == left_cols[None, :]) & (left_cols >= 0)[None, :] & valid[:, None]
    found = jnp.any(match, axis=1)
    index = jnp.argmax(match, axis=1).astype(jnp.int32)
    left = jnp.take(left_vals, index, axis=0) * found.astype(left_vals.dtype)[:, None, None]
    prods = jnp.einsum("txy,tyz->txz", left, right_vals, precision=lax.Precision.HIGHEST)
    select = ((j_need[None, :] == jnp.arange(JB, dtype=jnp.int32)[:, None]) & valid[None, :]).astype(left_vals.dtype)
    placed = jnp.einsum("jt,txz->xjz", select, prods, precision=lax.Precision.HIGHEST)
    return placed.reshape(blk, JB * blk)


def reference(a_vals, a_code, b_vals, b_code, panels):
    group = NBROW // NPANEL
    k_rows = KPB // group
    a_blocks = a_vals.reshape(NBROW, SA, NPANEL, BLK, BLK)
    a_keys = a_code.reshape(NBROW, SA, NPANEL)
    b_blocks = b_vals.reshape(NBROW, SB, NPANEL, BLK, BLK)
    b_keys = b_code.reshape(NBROW, SB, NPANEL)
    zero = jnp.zeros((), jnp.int32)

    def one_device(flat):
        row_id = (flat // NPANEL).astype(jnp.int32)
        col_id = (flat % NPANEL).astype(jnp.int32)
        total = jnp.zeros((BLK, JB * BLK), jnp.float32)
        for step in range(STEPS):
            root = panels[step].astype(jnp.int32)
            left_vals = lax.dynamic_slice(a_blocks, (row_id, zero, root, zero, zero), (1, SA, 1, BLK, BLK)).reshape(SA, BLK, BLK)
            left_cols = lax.dynamic_slice(a_keys, (row_id, zero, root), (1, SA, 1)).reshape(SA)
            start = (root * group).astype(jnp.int32)
            right_vals = lax.dynamic_slice(b_blocks, (start, zero, col_id, zero, zero), (group, SB, 1, BLK, BLK)).reshape(group * SB, BLK, BLK)
            right_codes = lax.dynamic_slice(b_keys, (start, zero, col_id), (group, SB, 1)).reshape(group * SB)
            total = total + panel_product(left_vals, left_cols, right_vals, right_codes, SB, k_rows)
        return total

    bands = lax.map(one_device, jnp.arange(NBROW * NPANEL, dtype=jnp.int32))
    bands = bands.reshape(NBROW, NPANEL, BLK, JB * BLK).transpose(0, 2, 1, 3)
    return bands.reshape(NBROW * BLK, NPANEL * JB * BLK)
```

```python
import functools

import jax
import jax.numpy as jnp
import numpy as np
from jax import lax
from jax.experimental import pallas as pl
from jax.experimental.pallas import tpu as pltpu
from jax.sharding import PartitionSpec as P

KPB = 64
STEPS = 2
JB = 8
FIELDS = 5
CHUNKS = 2


def plan_kernel(group, per_dev, cs, route, a_codes, b_codes, plan, table):
    sa = a_codes.shape[1]
    k_rows = KPB // group
    count = jnp.int32(0)
    for step in range(STEPS):
        base = step * (2 + group)
        panel, a_array = route[base], route[base + 1]

        for k in range(KPB):
            table[k] = jnp.int32(-1)
        for slot in range(sa):
            code = a_codes[panel, slot]

            @pl.when(code >= 0)
            def _():
                table[code] = jnp.int32(slot)

        for g in range(group):
            b_array = route[base + 2 + g]

            def one(slot, count):
                code = b_codes[panel * group + g, slot]
                k = jnp.where(code >= 0, g * k_rows + code // JB, 0)
                a_slot = table[k]
                ok = (code >= 0) & (a_slot >= 0)

                @pl.when(ok)
                def _():
                    at = 1 + count * FIELDS
                    chunked = a_array > 0
                    plan[at] = jnp.where(chunked, a_array + a_slot // cs, 0)
                    plan[at + 1] = jnp.where(chunked, a_slot % cs, a_slot)
                    plan[at + 2] = b_array
                    plan[at + 3] = slot
                    plan[at + 4] = code % JB

                return count + ok.astype(jnp.int32)

            count = lax.fori_loop(0, per_dev, one, count)
    plan[0] = count


def make_plan(route, a_codes, b_codes, group, cs):
    per_dev = b_codes.shape[1]
    most = STEPS * group * per_dev
    smem = pl.BlockSpec(memory_space=pltpu.SMEM)
    return pl.pallas_call(
        functools.partial(plan_kernel, group, per_dev, cs),
        out_shape=jax.ShapeDtypeStruct((1 + most * FIELDS,), jnp.int32),
        in_specs=[smem] * 3,
        out_specs=smem,
        scratch_shapes=[pltpu.SMEM((KPB,), jnp.int32)],
        name="plan",
    )(route, a_codes, b_codes)


def split(x):
    high = x.astype(jnp.bfloat16)
    low = (x - high.astype(jnp.float32)).astype(jnp.bfloat16)
    return high, low


def dot(x, y):
    return jnp.dot(x, y, preferred_element_type=jnp.float32)


def product_kernel(n_a, n_b, plan, *refs):
    a_refs, b_refs = refs[:n_a], refs[n_a : n_a + n_b]
    c_ref, a_buf, b_buf, sems = refs[n_a + n_b :]
    blk = a_buf.shape[1]
    count = plan[0]

    def fetch(m, carry):
        at = 1 + m * FIELDS
        for which, (sources, buf) in enumerate(((a_refs, a_buf), (b_refs, b_buf))):
            array, slot = plan[at + 2 * which], plan[at + 2 * which + 1]
            for i, source in enumerate(sources):

                @pl.when(array == i)
                def _():
                    pltpu.make_async_copy(source.at[slot], buf.at[m], sems.at[which, m]).start()

        return carry

    lax.fori_loop(0, count, fetch, 0)
    c_ref[...] = jnp.zeros_like(c_ref)

    def multiply(m, carry):
        for which, buf in enumerate((a_buf, b_buf)):
            pltpu.make_async_copy(buf.at[m], buf.at[m], sems.at[which, m]).wait()
        a_high, a_low = split(a_buf[m])
        b_high, b_low = split(b_buf[m])
        prod = dot(a_high, b_high) + (dot(a_high, b_low) + dot(a_low, b_high))
        j = plan[1 + m * FIELDS + 4]
        columns = pl.ds(pl.multiple_of(j * blk, blk), blk)
        c_ref[:, columns] += prod
        return carry

    lax.fori_loop(0, count, multiply, 0)


def multiply_all(plan, a_arrays, b_arrays):
    most = (plan.shape[0] - 1) // FIELDS
    blk = a_arrays[0].shape[1]
    anywhere = pl.BlockSpec(memory_space=pl.ANY)
    return pl.pallas_call(
        functools.partial(product_kernel, len(a_arrays), len(b_arrays)),
        out_shape=jax.ShapeDtypeStruct((blk, JB * blk), jnp.float32),
        in_specs=[pl.BlockSpec(memory_space=pltpu.SMEM)] + [anywhere] * (len(a_arrays) + len(b_arrays)),
        out_specs=pl.BlockSpec(memory_space=pltpu.VMEM),
        scratch_shapes=[
            pltpu.VMEM((most, blk, blk), jnp.float32),
            pltpu.VMEM((most, blk, blk), jnp.float32),
            pltpu.SemaphoreType.DMA((2, most)),
        ],
        compiler_params=pltpu.CompilerParams(vmem_limit_bytes=24 * 2**20),
        cost_estimate=pl.CostEstimate(flops=2 * 3 * 8 * blk**3, bytes_accessed=2**21, transcendentals=0),
        name="products",
    )(plan, *a_arrays, *b_arrays)


def gathered(a_vals, a_code, b_vals, b_code, panels, group):
    sa, sb = a_vals.shape[0], b_vals.shape[0]
    a_codes = lax.all_gather(a_code[:, 0], "col")
    b_codes = lax.all_gather(b_code[:, 0], "row")
    a_all = lax.all_gather(a_vals, "col")
    b_all = lax.all_gather(b_vals, "row")
    a_arrays, b_arrays, route = [], [], []
    for step in range(STEPS):
        a_arrays.append(lax.dynamic_index_in_dim(a_all, panels[step], 0, keepdims=False))
        route += [panels[step], step]
        for g in range(group):
            b_arrays.append(lax.dynamic_index_in_dim(b_all, panels[step] * group + g, 0, keepdims=False))
            route.append(step * group + g)
    route = jnp.stack([jnp.int32(x) for x in route])
    plan = make_plan(route, a_codes, b_codes, group, sa)
    return multiply_all(plan, a_arrays, b_arrays)


def pair_branch(roots, n, a_vals, a_code, b_vals, b_code):
    group = 2
    cs = a_vals.shape[0] // CHUNKS
    z = lax.axis_index("col")
    row = lax.axis_index("row")
    chip, core = row // group, row % group

    pieces = [a_vals[i * cs : (i + 1) * cs] for i in range(CHUNKS)]
    a_arrays = [a_vals]
    a_table = np.zeros((n, STEPS), np.int32)
    for sign in (1, -1):
        held = pieces
        for d in range(1, n):
            pairs = [(p + sign * (d - 1), p + sign * d) for p in roots if 0 <= p + sign * d < n]
            if not pairs:
                break
            held = [lax.ppermute(x, "col", pairs) for x in held]
            for s, p in enumerate(roots):
                if 0 <= p + sign * d < n:
                    a_table[p + sign * d, s] = len(a_arrays)
            a_arrays += held

    def rows(pairs):
        return [(x * group + c, y * group + c) for x, y in pairs for c in range(group)]

    def swapped(chips):
        return [(q * group + c, q * group + 1 - c) for q in chips for c in range(group)]

    others = [q for q in range(n) if q not in roots]
    rounds = [[(roots[0], roots[1]), (roots[1], roots[0])]]
    for i in range(len(others)):
        rounds.append([(roots[s], others[(i + s) % len(others)]) for s in range(STEPS)])
    b_arrays = [b_vals, lax.ppermute(b_vals, "row", swapped(roots))]
    b_table = np.zeros((n, STEPS, 2), np.int32)
    for s, p in enumerate(roots):
        b_table[p, s] = (0, 1)
    for pairs in rounds:
        straight = lax.ppermute(b_vals, "row", rows(pairs))
        across = lax.ppermute(straight, "row", swapped([q for _, q in pairs]))
        for p, q in pairs:
            b_table[q, roots.index(p)] = (len(b_arrays), len(b_arrays) + 1)
        b_arrays += [straight, across]

    a_at = jnp.asarray(a_table)[z]
    b_at = jnp.asarray(b_table)[chip]
    route = []
    for s, p in enumerate(roots):
        route += [jnp.int32(p), a_at[s]]
        route += [jnp.where(core == g, b_at[s, 0], b_at[s, 1]) for g in range(group)]
    a_codes = lax.all_gather(a_code[:, 0], "col")
    b_codes = lax.all_gather(b_code[:, 0], "row")
    plan = make_plan(jnp.stack(route), a_codes, b_codes, group, cs)
    return multiply_all(plan, a_arrays, b_arrays)


def shards(a_vals, a_code, b_vals, b_code, panels):
    n = lax.axis_size("col")
    group = lax.axis_size("row") // n
    if group != 2 or n != 4:
        return gathered(a_vals, a_code, b_vals, b_code, panels, group)
    pairs = [(lo, hi) for lo in range(n) for hi in range(lo + 1, n)]
    lo = jnp.minimum(panels[0], panels[1])
    hi = jnp.maximum(panels[0], panels[1])
    which = lo * n - lo * (lo + 1) // 2 + hi - lo - 1
    branches = [functools.partial(pair_branch, pair, n) for pair in pairs]
    return lax.switch(which, branches, a_vals, a_code, b_vals, b_code)


def solution(mesh):
    return jax.shard_map(
        shards,
        mesh=mesh,
        in_specs=(
            P("row", "col", None),
            P("row", "col"),
            P("row", "col", None),
            P("row", "col"),
            P(),
        ),
        out_specs=P("row", "col"),
        check_vma=False,
    )
```

```python
import functools

import jax
import jax.numpy as jnp
import numpy as np
from jax import lax
from jax.experimental import pallas as pl
from jax.experimental.pallas import tpu as pltpu
from jax.sharding import PartitionSpec as P

KPB = 64
STEPS = 2
JB = 8
FIELDS = 5


def plan_kernel(group, per_dev, route, a_codes, b_codes, plan, table):
    sa = a_codes.shape[1]
    k_rows = KPB // group
    count = jnp.int32(0)
    for step in range(STEPS):
        base = step * (1 + group)
        a_source = route[base]

        for k in range(KPB):
            table[k] = jnp.int32(-1)
        for slot in range(sa):
            code = a_codes[a_source, slot]

            @pl.when(code >= 0)
            def _():
                table[code] = jnp.int32(slot)

        for g in range(group):
            b_source = route[base + 1 + g]

            def one(slot, count):
                code = b_codes[b_source, slot]
                k = jnp.where(code >= 0, g * k_rows + code // JB, 0)
                a_slot = table[k]
                ok = (code >= 0) & (a_slot >= 0)

                @pl.when(ok)
                def _():
                    at = 1 + count * FIELDS
                    plan[at] = a_source
                    plan[at + 1] = a_slot
                    plan[at + 2] = b_source
                    plan[at + 3] = slot
                    plan[at + 4] = code % JB

                return count + ok.astype(jnp.int32)

            count = lax.fori_loop(0, per_dev, one, count)
    plan[0] = count


def make_plan(route, a_codes, b_codes, group):
    per_dev = b_codes.shape[1]
    most = STEPS * group * per_dev
    smem = pl.BlockSpec(memory_space=pltpu.SMEM)
    return pl.pallas_call(
        functools.partial(plan_kernel, group, per_dev),
        out_shape=jax.ShapeDtypeStruct((1 + most * FIELDS,), jnp.int32),
        in_specs=[smem] * 3,
        out_specs=smem,
        scratch_shapes=[pltpu.SMEM((KPB,), jnp.int32)],
        name="plan",
    )(route, a_codes, b_codes)


def split(x):
    high = x.astype(jnp.bfloat16)
    low = (x - high.astype(jnp.float32)).astype(jnp.bfloat16)
    return high, low


def dot(x, y):
    return jnp.dot(x, y, preferred_element_type=jnp.float32)


def product_kernel(a_arrays, n_b, plan, *refs):
    n_a = sum(len(arrays) for arrays in a_arrays)
    a_refs, b_refs = refs[:n_a], refs[n_a : n_a + n_b]
    c_ref, a_buf, b_buf, sems = refs[n_a + n_b :]
    blk = a_buf.shape[1]
    count = plan[0]

    def rows(slot):
        return pl.ds(pl.multiple_of(slot * blk, blk), blk)

    def fetch(m, carry):
        at = 1 + m * FIELDS
        source, slot = plan[at], plan[at + 1]
        i = 0
        for which, arrays in enumerate(a_arrays):
            for first, end in arrays:

                @pl.when((source == which) & (slot >= first) & (slot < end))
                def _():
                    pltpu.make_async_copy(a_refs[i].at[rows(slot - first)], a_buf.at[m], sems.at[0, m]).start()

                i += 1
        source, slot = plan[at + 2], plan[at + 3]
        for which in range(n_b):

            @pl.when(source == which)
            def _():
                pltpu.make_async_copy(b_refs[which].at[rows(slot)], b_buf.at[m], sems.at[1, m]).start()

        return carry

    lax.fori_loop(0, count, fetch, 0)
    c_ref[...] = jnp.zeros_like(c_ref)

    def multiply(m, carry):
        for which, buf in enumerate((a_buf, b_buf)):
            pltpu.make_async_copy(buf.at[m], buf.at[m], sems.at[which, m]).wait()
        a_high, a_low = split(a_buf[m])
        b_high, b_low = split(b_buf[m])
        prod = dot(a_high, b_high) + (dot(a_high, b_low) + dot(a_low, b_high))
        j = plan[1 + m * FIELDS + 4]
        columns = pl.ds(pl.multiple_of(j * blk, blk), blk)
        c_ref[:, columns] += prod
        return carry

    lax.fori_loop(0, count, multiply, 0)


def multiply_all(plan, a_sources, b_sources):
    most = (plan.shape[0] - 1) // FIELDS
    blk = b_sources[0].shape[1]
    a_flat = [x for arrays in a_sources for _, _, x in arrays]
    in_hbm = pl.BlockSpec(memory_space=pltpu.HBM)
    return pl.pallas_call(
        functools.partial(product_kernel, [[(f, e) for f, e, _ in arrays] for arrays in a_sources], len(b_sources)),
        out_shape=jax.ShapeDtypeStruct((blk, JB * blk), jnp.float32),
        in_specs=[pl.BlockSpec(memory_space=pltpu.SMEM)] + [in_hbm] * (len(a_flat) + len(b_sources)),
        out_specs=pl.BlockSpec(memory_space=pltpu.VMEM),
        scratch_shapes=[
            pltpu.VMEM((most, blk, blk), jnp.float32),
            pltpu.VMEM((most, blk, blk), jnp.float32),
            pltpu.SemaphoreType.DMA((2, most)),
        ],
        compiler_params=pltpu.CompilerParams(vmem_limit_bytes=24 * 2**20),
        cost_estimate=pl.CostEstimate(flops=2 * 3 * 8 * blk**3, bytes_accessed=2**21, transcendentals=0),
        name="products",
    )(plan, *a_flat, *b_sources)


def as_rows(x):
    return x.reshape(-1, x.shape[-1])


def gathered(a_vals, a_code, b_vals, b_code, panels, group):
    sa = a_vals.shape[0]
    codes = (lax.all_gather(a_code[:, 0], "col"), lax.all_gather(b_code[:, 0], "row"))
    a_all = lax.all_gather(a_vals, "col")
    b_all = lax.all_gather(b_vals, "row")
    a_sources, a_codes, b_sources, b_codes, route = [], [], [], [], []
    for step in range(STEPS):
        panel = panels[step]
        route.append(step)
        a_sources.append([(0, sa, as_rows(lax.dynamic_index_in_dim(a_all, panel, 0, keepdims=False)))])
        a_codes.append(codes[0][panel])
        for g in range(group):
            route.append(step * group + g)
            b_sources.append(as_rows(lax.dynamic_index_in_dim(b_all, panel * group + g, 0, keepdims=False)))
            b_codes.append(codes[1][panel * group + g])
    plan = make_plan(jnp.array(route, jnp.int32), jnp.stack(a_codes), jnp.stack(b_codes), group)
    return multiply_all(plan, a_sources, b_sources)


CHUNKS = ((0, 8), (8, 16))
UP = {
    (0, 1): [(None, ((0, 1), (1, 2)), {1: 0, 2: 1}), (0, ((1, 2), (2, 3)), {2: 0, 3: 1}), (1, ((2, 3),), {3: 0})],
    (0, 2): [
        (None, ((0, 1), (1, 2)), {1: 0}),
        (None, ((2, 3),), {3: 2}),
        (0, ((0, 1), (1, 2)), {2: 0}),
        (2, ((2, 3),), {3: 0}),
    ],
    (0, 3): [(None, ((0, 1), (1, 2)), {1: 0}), (0, ((0, 1), (1, 2)), {2: 0}), (1, ((2, 3),), {3: 0})],
    (1, 2): [(None, ((1, 2), (2, 3)), {2: 1, 3: 2}), (0, ((2, 3),), {3: 1})],
    (1, 3): [(None, ((1, 2), (2, 3)), {2: 1}), (0, ((2, 3),), {3: 1})],
    (2, 3): [(None, ((2, 3),), {3: 2})],
}


def chain_steps(roots, n):
    def flip(x):
        return n - 1 - x

    down = [
        (src, tuple((flip(x), flip(y)) for x, y in pairs), {flip(at): flip(p) for at, p in got.items()})
        for src, pairs, got in UP[tuple(sorted(map(flip, roots)))]
    ]
    return UP[roots], down


def with_codes(rows, code):
    code = code[:, 0].astype(jnp.float32)
    tail = jnp.pad(code[None, :], ((0, 7), (0, rows.shape[1] - code.shape[0])))
    return jnp.concatenate([rows, tail])


def codes_in(x, count):
    return x[x.shape[0] - 8, :count].astype(jnp.int32)


def pair_branch(roots, n, a_vals, a_code, b_vals, b_code):
    group = 2
    sa, blk = a_vals.shape[:2]
    sb = b_vals.shape[0]
    z = lax.axis_index("col")
    row = lax.axis_index("row")
    chip, core = row >> 1, row & 1

    a_rows, b_rows = as_rows(a_vals), as_rows(b_vals)
    pieces = [a_rows[f * blk : e * blk] for f, e in CHUNKS]
    pieces[0] = with_codes(pieces[0], a_code)
    b_own = with_codes(b_rows, b_code)

    a_sources = [[(0, sa, a_rows)]]
    a_codes = [a_code[:, 0]]
    a_table = np.zeros((n, STEPS), np.int32)
    for steps in chain_steps(roots, n):
        results = []
        for src, pairs, got in steps:
            sent = pieces if src is None else results[src]
            results.append([lax.ppermute(x, "col", pairs) for x in sent])
            for at, p in got.items():
                a_table[at, roots.index(p)] = len(a_sources)
            a_sources.append([(f, e, x) for (f, e), x in zip(CHUNKS, results[-1])])
            a_codes.append(codes_in(results[-1][0], sa))

    def exchange(x, bit):
        return lax.ppermute(x, "row", [(r, r ^ bit) for r in range(n * group)])

    straight = [b_own] + [exchange(b_own, q * group) for q in range(1, n)]
    b_sources = [b_rows] + straight[1:] + [exchange(x, 1) for x in straight]
    b_codes = [b_code[:, 0]] + [codes_in(x, sb) for x in b_sources[1:]]

    a_at = jnp.asarray(a_table)[z]
    route = []
    for s, p in enumerate(roots):
        route.append(a_at[s])
        route += [(chip ^ p) + jnp.where(core == g, 0, n) for g in range(group)]
    plan = make_plan(jnp.stack(route), jnp.stack(a_codes), jnp.stack(b_codes), group)
    return multiply_all(plan, a_sources, b_sources)


def shards(a_vals, a_code, b_vals, b_code, panels):
    n = lax.axis_size("col")
    group = lax.axis_size("row") // n
    if group != 2 or n != 4:
        return gathered(a_vals, a_code, b_vals, b_code, panels, group)
    lo = jnp.minimum(panels[0], panels[1])
    hi = jnp.maximum(panels[0], panels[1])
    which = jnp.where(lo == 0, 0, lo + 1) + hi - 1
    branches = [functools.partial(pair_branch, pair, n) for pair in sorted(UP)]
    return lax.switch(which, branches, a_vals, a_code, b_vals, b_code)


def solution(mesh):
    return jax.shard_map(
        shards,
        mesh=mesh,
        in_specs=(
            P("row", "col", None),
            P("row", "col"),
            P("row", "col", None),
            P("row", "col"),
            P(),
        ),
        out_specs=P("row", "col"),
        check_vma=False,
    )
```

```python
import functools

import jax
import jax.numpy as jnp
from jax import lax
from jax.experimental import pallas as pl
from jax.experimental.pallas import tpu as pltpu
from jax.sharding import PartitionSpec as P

KPB = 64
STEPS = 2
JB = 8
TAIL = 8
MIB = 2**20

SMEM = pl.BlockSpec(memory_space=pltpu.SMEM)
VMEM = pl.BlockSpec(memory_space=pltpu.VMEM)
ANY = pl.BlockSpec(memory_space=pl.ANY)


def rows_of(slot, blk):
    return pl.ds(pl.multiple_of(slot * blk, blk), blk)


def prepare_kernel(chunks, a_code, b_code, panels, a_rows, b_rows, which, *refs):
    pieces, b_own = refs[: len(chunks)], refs[len(chunks)]
    tails, sems = refs[len(chunks) + 1 :]
    blk = a_rows.shape[1]
    copies = [
        pltpu.make_async_copy(a_rows.at[pl.ds(f * blk, (e - f) * blk)], piece.at[pl.ds(0, (e - f) * blk)], sems.at[i])
        for i, ((f, e), piece) in enumerate(zip(chunks, pieces))
    ]
    copies.append(pltpu.make_async_copy(b_rows, b_own.at[pl.ds(0, b_rows.shape[0])], sems.at[len(chunks)]))
    for copy in copies:
        copy.start()
    tails[...] = jnp.zeros_like(tails)
    for i, (code, into) in enumerate(((a_code, pieces[0]), (b_code, b_own))):
        tails[i, 0:1, 0 : code.shape[1]] = code[...].astype(jnp.float32)
        last = into.shape[0] - TAIL
        copy = pltpu.make_async_copy(tails.at[i], into.at[pl.ds(last, TAIL)], sems.at[len(chunks) + 1 + i])
        copy.start()
        copies.append(copy)
    lo = jnp.minimum(panels[0], panels[1])
    hi = jnp.maximum(panels[0], panels[1])
    which[0] = jnp.where(lo == 0, 0, lo + 1) + hi - 1
    for copy in copies:
        copy.wait()


def prepare(chunks, a_code, b_code, panels, a_rows, b_rows):
    blk = a_rows.shape[1]
    sizes = [(e - f) * blk for f, e in chunks]
    sizes[0] += TAIL
    sizes.append(b_rows.shape[0] + TAIL)
    return pl.pallas_call(
        functools.partial(prepare_kernel, chunks),
        out_shape=[jax.ShapeDtypeStruct((1,), jnp.int32)] + [jax.ShapeDtypeStruct((x, blk), jnp.float32) for x in sizes],
        in_specs=[VMEM, VMEM, SMEM, ANY, ANY],
        out_specs=[SMEM] + [ANY] * len(sizes),
        scratch_shapes=[pltpu.VMEM((2, TAIL, blk), jnp.float32), pltpu.SemaphoreType.DMA((len(chunks) + 3,))],
        name="prepare",
    )(a_code.T, b_code.T, panels, a_rows, b_rows)


def split(x):
    high = x.astype(jnp.bfloat16)
    low = (x - high.astype(jnp.float32)).astype(jnp.bfloat16)
    return high, low


def dot(x, y):
    return jnp.dot(x, y, preferred_element_type=jnp.float32)


def add_products(count, column, a_buf, b_buf, sems, c_ref):
    blk = a_buf.shape[1]

    def one(m, carry):
        for which, buf in enumerate((a_buf, b_buf)):
            pltpu.make_async_copy(buf.at[m], buf.at[m], sems.at[which, m]).wait()
        a_high, a_low = split(a_buf[m])
        b_high, b_low = split(b_buf[m])
        prod = dot(a_high, b_high) + (dot(a_high, b_low) + dot(a_low, b_high))
        c_ref[:, rows_of(column(m), blk)] += prod
        return carry

    lax.fori_loop(0, count, one, 0)


def start_from(refs, source, rows, into, sem):
    for i, ref in enumerate(refs):

        @pl.when(source == i)
        def _():
            pltpu.make_async_copy(ref.at[rows], into, sem).start()


def early_kernel(chunks, n_a, slots, a_at, b_at, *refs):
    group, sb = slots
    parts = len(chunks)
    n_b = len(refs) - n_a * parts - 13
    a_refs = [refs[i * parts : (i + 1) * parts] for i in range(n_a)]
    b_refs = refs[n_a * parts : n_a * parts + n_b]
    late, c_ref, b_late, tails, ints, codes, table, plan, a_buf, b_buf, sems, late_sems, tail_sems = refs[n_a * parts + n_b :]
    sa = chunks[-1][1]
    last_first = chunks[-1][0]
    blk = a_buf.shape[1]
    k_rows = KPB // group
    sources = [[a_at(s)] + [b_at(s, g) for g in range(group)] for s in range(STEPS)]
    sources = [x for step in sources for x in step]

    for t, source in enumerate(sources):
        holders = b_refs if t % (1 + group) else [arrays[0] for arrays in a_refs]
        start_from(holders, source, pl.ds(holders[0].shape[0] - TAIL, TAIL), tails.at[t], tail_sems.at[t])
    for s in range(STEPS):
        for k in range(KPB):
            table[s, k] = jnp.int32(-1)
    c_ref[...] = jnp.zeros_like(c_ref)
    ints[...] = jnp.zeros_like(ints)
    for t in range(len(sources)):
        pltpu.make_async_copy(tails.at[t], tails.at[t], tail_sems.at[t]).wait()
        ints[t : t + 1, :] = tails[t, 0:1, :].astype(jnp.int32)
    copy = pltpu.make_async_copy(ints, codes, tail_sems.at[len(sources)])
    copy.start()
    copy.wait()

    counts = (jnp.int32(0), jnp.int32(0))
    for s in range(STEPS):
        row_a = s * (1 + group)
        for slot in range(sa):
            code = codes[row_a, slot]

            @pl.when(code >= 0)
            def _():
                table[s, code] = jnp.int32(slot)

        for g in range(group):

            def one(slot, counts):
                n_early, n_late = counts
                code = codes[row_a + 1 + g, slot]
                k = jnp.where(code >= 0, g * k_rows + code // JB, 0)
                a_slot = table[s, k]
                ok = (code >= 0) & (a_slot >= 0)
                is_late = a_slot >= last_first

                @pl.when(ok & jnp.logical_not(is_late))
                def _():
                    plan[n_early] = code % JB
                    for i, arrays in enumerate(a_refs):

                        @pl.when(sources[row_a] == i)
                        def _():
                            for (f, e), ref in list(zip(chunks, arrays))[:-1]:

                                @pl.when((a_slot >= f) & (a_slot < e))
                                def _():
                                    rows = rows_of(a_slot - f, blk)
                                    pltpu.make_async_copy(ref.at[rows], a_buf.at[n_early], sems.at[0, n_early]).start()

                    start_from(b_refs, sources[row_a + 1 + g], rows_of(slot, blk), b_buf.at[n_early], sems.at[1, n_early])

                @pl.when(ok & is_late)
                def _():
                    late[1 + 3 * n_late] = sources[row_a]
                    late[2 + 3 * n_late] = a_slot - last_first
                    late[3 + 3 * n_late] = code % JB
                    into = b_late.at[rows_of(n_late, blk)]
                    start_from(b_refs, sources[row_a + 1 + g], rows_of(slot, blk), into, late_sems.at[n_late])

                is_late = is_late.astype(jnp.int32)
                ok = ok.astype(jnp.int32)
                return n_early + ok * (1 - is_late), n_late + ok * is_late

            counts = lax.fori_loop(0, sb, one, counts)
    late[0] = counts[1]
    add_products(counts[0], lambda m: plan[m], a_buf, b_buf, sems, c_ref)

    def wait(m, carry):
        into = b_late.at[rows_of(m, blk)]
        pltpu.make_async_copy(into, into, late_sems.at[m]).wait()
        return carry

    lax.fori_loop(0, counts[1], wait, 0)


def late_kernel(n_a, late, c_in, b_late, *refs):
    a_refs, (c_ref, a_buf, b_buf, sems) = refs[:n_a], refs[n_a:]
    blk = a_buf.shape[1]

    def fetch(m, carry):
        start_from(a_refs, late[1 + 3 * m], rows_of(late[2 + 3 * m], blk), a_buf.at[m], sems.at[0, m])
        pltpu.make_async_copy(b_late.at[rows_of(m, blk)], b_buf.at[m], sems.at[1, m]).start()
        return carry

    lax.fori_loop(0, late[0], fetch, 0)
    c_ref[...] = c_in[...]
    add_products(late[0], lambda m: late[3 + 3 * m], a_buf, b_buf, sems, c_ref)


def multiply(chunks, a_sources, b_sources, slots, a_at, b_at):
    group, sb = slots
    blk = b_sources[0].shape[1]
    most = STEPS * group * sb
    tails = STEPS * (1 + group)
    n_a = len(a_sources)
    buffers = [pltpu.VMEM((most, blk, blk), jnp.float32)] * 2 + [pltpu.SemaphoreType.DMA((2, most))]
    band = jax.ShapeDtypeStruct((blk, JB * blk), jnp.float32)
    late, c_early, b_late = pl.pallas_call(
        functools.partial(early_kernel, chunks, n_a, slots, a_at, b_at),
        out_shape=[
            jax.ShapeDtypeStruct((1 + 3 * most,), jnp.int32),
            band,
            jax.ShapeDtypeStruct((most * blk, blk), jnp.float32),
        ],
        in_specs=[ANY] * (n_a * len(chunks) + len(b_sources)),
        out_specs=[SMEM, VMEM, ANY],
        scratch_shapes=[
            pltpu.VMEM((tails, TAIL, blk), jnp.float32),
            pltpu.VMEM((TAIL, blk), jnp.int32),
            pltpu.SMEM((TAIL, blk), jnp.int32),
            pltpu.SMEM((STEPS, KPB), jnp.int32),
            pltpu.SMEM((most,), jnp.int32),
            *buffers,
            pltpu.SemaphoreType.DMA((most,)),
            pltpu.SemaphoreType.DMA((tails + 1,)),
        ],
        compiler_params=pltpu.CompilerParams(vmem_limit_bytes=24 * MIB),
        cost_estimate=pl.CostEstimate(flops=6 * 8 * blk**3, bytes_accessed=8 * MIB, transcendentals=0),
        name="early",
    )(*[x for arrays in a_sources for x in arrays], *b_sources)
    return pl.pallas_call(
        functools.partial(late_kernel, n_a),
        out_shape=band,
        in_specs=[SMEM, VMEM, ANY] + [ANY] * n_a,
        out_specs=VMEM,
        scratch_shapes=buffers,
        compiler_params=pltpu.CompilerParams(vmem_limit_bytes=24 * MIB),
        cost_estimate=pl.CostEstimate(flops=6 * 2 * blk**3, bytes_accessed=2 * MIB, transcendentals=0),
        name="late",
    )(late, c_early, b_late, *[arrays[-1] for arrays in a_sources])


def as_rows(x):
    return x.reshape(-1, x.shape[-1])


def gathered(a_vals, a_code, b_vals, b_code, panels, group):
    chunks = [(0, a_vals.shape[0])]
    _, a_own, b_own = prepare(chunks, a_code, b_code, panels, as_rows(a_vals), as_rows(b_vals))
    a_all = lax.all_gather(a_own, "col")
    b_all = lax.all_gather(b_own, "row")
    a_sources, b_sources = [], []
    for step in range(STEPS):
        a_sources.append([lax.dynamic_index_in_dim(a_all, panels[step], 0, keepdims=False)])
        for g in range(group):
            b_sources.append(lax.dynamic_index_in_dim(b_all, panels[step] * group + g, 0, keepdims=False))
    slots = (group, b_vals.shape[0])
    return multiply(chunks, a_sources, b_sources, slots, lambda s: s, lambda s, g: s * group + g)


CHUNKS = [(0, 4), (4, 8), (8, 12), (12, 16)]
UP = {
    (0, 1): [(None, ((0, 1), (1, 2)), {1: 0, 2: 1}), (0, ((1, 2), (2, 3)), {2: 0, 3: 1}), (1, ((2, 3),), {3: 0})],
    (0, 2): [
        (None, ((0, 1), (1, 2)), {1: 0}),
        (None, ((2, 3),), {3: 2}),
        (0, ((0, 1), (1, 2)), {2: 0}),
        (2, ((2, 3),), {3: 0}),
    ],
    (0, 3): [(None, ((0, 1), (1, 2)), {1: 0}), (0, ((0, 1), (1, 2)), {2: 0}), (1, ((2, 3),), {3: 0})],
    (1, 2): [(None, ((1, 2), (2, 3)), {2: 1, 3: 2}), (0, ((2, 3),), {3: 1})],
    (1, 3): [(None, ((1, 2), (2, 3)), {2: 1}), (0, ((2, 3),), {3: 1})],
    (2, 3): [(None, ((2, 3),), {3: 2})],
}


def chain_steps(roots, n):
    def flip(x):
        return n - 1 - x

    down = [
        (src, tuple((flip(x), flip(y)) for x, y in pairs), {flip(at): flip(p) for at, p in got.items()})
        for src, pairs, got in UP[tuple(sorted(map(flip, roots)))]
    ]
    return UP[roots], down


def pick(values, index):
    out = jnp.int32(values[0])
    for i, value in enumerate(values[1:], 1):
        out = jnp.where(index == i, jnp.int32(value), out)
    return out


def pair_branch(roots, n, slots, pieces, b_own):
    group, _ = slots
    a_sources = [pieces]
    a_table = [[0] * n for _ in roots]
    for steps in chain_steps(roots, n):
        results = []
        for src, pairs, got in steps:
            sent = pieces if src is None else results[src]
            results.append([lax.ppermute(x, "col", pairs) for x in sent])
            for at, p in got.items():
                a_table[roots.index(p)][at] = len(a_sources)
            a_sources.append(results[-1])

    def exchange(x, bit):
        return lax.ppermute(x, "row", [(r, r ^ bit) for r in range(n * group)])

    straight = [b_own] + [exchange(b_own, q * group) for q in range(1, n)]
    b_sources = straight + [exchange(x, 1) for x in straight]

    def a_at(s):
        return pick(a_table[s], lax.axis_index("col"))

    def b_at(s, g):
        row = lax.axis_index("row")
        return ((row >> 1) ^ roots[s]) + jnp.where((row & 1) == g, 0, n)

    return multiply(CHUNKS, a_sources, b_sources, slots, a_at, b_at)


def shards(a_vals, a_code, b_vals, b_code, panels):
    n = lax.axis_size("col")
    group = lax.axis_size("row") // n
    if group != 2 or n != 4:
        return gathered(a_vals, a_code, b_vals, b_code, panels, group)
    which, *pieces, b_own = prepare(CHUNKS, a_code, b_code, panels, as_rows(a_vals), as_rows(b_vals))
    slots = (group, b_vals.shape[0])
    branches = [functools.partial(pair_branch, pair, n, slots) for pair in sorted(UP)]
    return lax.switch(which[0], branches, pieces, b_own)


def solution(mesh):
    return jax.shard_map(
        shards,
        mesh=mesh,
        in_specs=(
            P("row", "col", None),
            P("row", "col"),
            P("row", "col", None),
            P("row", "col"),
            P(),
        ),
        out_specs=P("row", "col"),
        check_vma=False,
    )
```

```python
import functools

import jax
import jax.numpy as jnp
from jax import lax
from jax.experimental import pallas as pl
from jax.experimental.pallas import tpu as pltpu
from jax.sharding import PartitionSpec as P

KPB = 64
STEPS = 2
JB = 8
TAIL = 8
MIB = 2**20

SMEM = pl.BlockSpec(memory_space=pltpu.SMEM)
VMEM = pl.BlockSpec(memory_space=pltpu.VMEM)
ANY = pl.BlockSpec(memory_space=pl.ANY)


def rows_of(slot, blk):
    return pl.ds(pl.multiple_of(slot * blk, blk), blk)


def prepare_kernel(chunks, a_code, b_code, panels, a_rows, b_rows, which, *refs):
    pieces, b_own = refs[: len(chunks)], refs[len(chunks)]
    tails, sems = refs[len(chunks) + 1 :]
    blk = a_rows.shape[1]
    copies = [
        pltpu.make_async_copy(a_rows.at[pl.ds(f * blk, (e - f) * blk)], piece.at[pl.ds(0, (e - f) * blk)], sems.at[i])
        for i, ((f, e), piece) in enumerate(zip(chunks, pieces))
    ]
    copies.append(pltpu.make_async_copy(b_rows, b_own.at[pl.ds(0, b_rows.shape[0])], sems.at[len(chunks)]))
    for copy in copies:
        copy.start()
    tails[...] = jnp.zeros_like(tails)
    for i, (code, into) in enumerate(((a_code, pieces[0]), (b_code, b_own))):
        tails[i, 0:1, 0 : code.shape[1]] = code[...].astype(jnp.float32)
        last = into.shape[0] - TAIL
        copy = pltpu.make_async_copy(tails.at[i], into.at[pl.ds(last, TAIL)], sems.at[len(chunks) + 1 + i])
        copy.start()
        copies.append(copy)
    lo = jnp.minimum(panels[0], panels[1])
    hi = jnp.maximum(panels[0], panels[1])
    which[0] = jnp.where(lo == 0, 0, lo + 1) + hi - 1
    for copy in copies:
        copy.wait()


def prepare(chunks, a_code, b_code, panels, a_rows, b_rows):
    blk = a_rows.shape[1]
    sizes = [(e - f) * blk for f, e in chunks]
    sizes[0] += TAIL
    sizes.append(b_rows.shape[0] + TAIL)
    return pl.pallas_call(
        functools.partial(prepare_kernel, chunks),
        out_shape=[jax.ShapeDtypeStruct((1,), jnp.int32)] + [jax.ShapeDtypeStruct((x, blk), jnp.float32) for x in sizes],
        in_specs=[VMEM, VMEM, SMEM, ANY, ANY],
        out_specs=[SMEM] + [ANY] * len(sizes),
        scratch_shapes=[pltpu.VMEM((2, TAIL, blk), jnp.float32), pltpu.SemaphoreType.DMA((len(chunks) + 3,))],
        name="prepare",
    )(a_code.T, b_code.T, panels, a_rows, b_rows)


def split(x):
    high = x.astype(jnp.bfloat16)
    low = (x - high.astype(jnp.float32)).astype(jnp.bfloat16)
    return high, low


def dot(x, y):
    return jnp.dot(x, y, preferred_element_type=jnp.float32)


def add_products(count, column, a_buf, b_buf, sems, c_ref):
    blk = a_buf.shape[1]

    def one(m, carry):
        for which, buf in enumerate((a_buf, b_buf)):
            pltpu.make_async_copy(buf.at[m], buf.at[m], sems.at[which, m]).wait()
        a_high, a_low = split(a_buf[m])
        b_high, b_low = split(b_buf[m])
        prod = dot(a_high, b_high) + (dot(a_high, b_low) + dot(a_low, b_high))
        c_ref[:, rows_of(column(m), blk)] += prod
        return carry

    lax.fori_loop(0, count, one, 0)


def start_from(refs, source, rows, into, sem):
    for i, ref in enumerate(refs):

        @pl.when(source == i)
        def _():
            pltpu.make_async_copy(ref.at[rows], into, sem).start()


def early_kernel(chunks, n_a, slots, a_at, b_at, *refs):
    group, sb = slots
    parts = max(1, len(chunks) - 1)
    n_b = len(refs) - n_a * parts - 13
    a_refs = [refs[i * parts : (i + 1) * parts] for i in range(n_a)]
    b_refs = refs[n_a * parts : n_a * parts + n_b]
    late, c_ref, b_late, tails, ints, codes, table, plan, a_buf, b_buf, sems, late_sems, tail_sems = refs[n_a * parts + n_b :]
    sa = chunks[-1][1]
    last_first = chunks[-1][0]
    blk = a_buf.shape[1]
    k_rows = KPB // group
    sources = [[a_at(s)] + [b_at(s, g) for g in range(group)] for s in range(STEPS)]
    sources = [x for step in sources for x in step]

    for t, source in enumerate(sources):
        holders = b_refs if t % (1 + group) else [arrays[0] for arrays in a_refs]
        start_from(holders, source, pl.ds(holders[0].shape[0] - TAIL, TAIL), tails.at[t], tail_sems.at[t])
    for s in range(STEPS):
        for k in range(KPB):
            table[s, k] = jnp.int32(-1)
    c_ref[...] = jnp.zeros_like(c_ref)
    ints[...] = jnp.zeros_like(ints)
    for t in range(len(sources)):
        pltpu.make_async_copy(tails.at[t], tails.at[t], tail_sems.at[t]).wait()
        ints[t : t + 1, :] = tails[t, 0:1, :].astype(jnp.int32)
    copy = pltpu.make_async_copy(ints, codes, tail_sems.at[len(sources)])
    copy.start()
    copy.wait()

    counts = (jnp.int32(0), jnp.int32(0))
    for s in range(STEPS):
        row_a = s * (1 + group)
        for slot in range(sa):
            code = codes[row_a, slot]

            @pl.when(code >= 0)
            def _():
                table[s, code] = jnp.int32(slot)

        for g in range(group):

            def one(slot, counts):
                n_early, n_late = counts
                code = codes[row_a + 1 + g, slot]
                k = jnp.where(code >= 0, g * k_rows + code // JB, 0)
                a_slot = table[s, k]
                ok = (code >= 0) & (a_slot >= 0)
                is_late = a_slot >= last_first

                @pl.when(ok & jnp.logical_not(is_late))
                def _():
                    plan[n_early] = code % JB
                    for i, arrays in enumerate(a_refs):

                        @pl.when(sources[row_a] == i)
                        def _():
                            for (f, e), ref in zip(chunks[:-1], arrays):

                                @pl.when((a_slot >= f) & (a_slot < e))
                                def _():
                                    rows = rows_of(a_slot - f, blk)
                                    pltpu.make_async_copy(ref.at[rows], a_buf.at[n_early], sems.at[0, n_early]).start()

                    start_from(b_refs, sources[row_a + 1 + g], rows_of(slot, blk), b_buf.at[n_early], sems.at[1, n_early])

                @pl.when(ok & is_late)
                def _():
                    late[1 + 3 * n_late] = sources[row_a]
                    late[2 + 3 * n_late] = a_slot - last_first
                    late[3 + 3 * n_late] = code % JB
                    into = b_late.at[rows_of(n_late, blk)]
                    start_from(b_refs, sources[row_a + 1 + g], rows_of(slot, blk), into, late_sems.at[n_late])

                is_late = is_late.astype(jnp.int32)
                ok = ok.astype(jnp.int32)
                return n_early + ok * (1 - is_late), n_late + ok * is_late

            counts = lax.fori_loop(0, sb, one, counts)
    late[0] = counts[1]
    add_products(counts[0], lambda m: plan[m], a_buf, b_buf, sems, c_ref)

    def wait(m, carry):
        into = b_late.at[rows_of(m, blk)]
        pltpu.make_async_copy(into, into, late_sems.at[m]).wait()
        return carry

    lax.fori_loop(0, counts[1], wait, 0)


def late_kernel(n_a, late, c_in, b_late, *refs):
    a_refs, (c_ref, a_buf, b_buf, sems) = refs[:n_a], refs[n_a:]
    blk = a_buf.shape[1]

    def fetch(m, carry):
        start_from(a_refs, late[1 + 3 * m], rows_of(late[2 + 3 * m], blk), a_buf.at[m], sems.at[0, m])
        pltpu.make_async_copy(b_late.at[rows_of(m, blk)], b_buf.at[m], sems.at[1, m]).start()
        return carry

    lax.fori_loop(0, late[0], fetch, 0)
    c_ref[...] = c_in[...]
    add_products(late[0], lambda m: late[3 + 3 * m], a_buf, b_buf, sems, c_ref)


def multiply(chunks, a_sources, b_sources, slots, a_at, b_at):
    group, sb = slots
    blk = b_sources[0].shape[1]
    most = STEPS * group * sb
    tails = STEPS * (1 + group)
    n_a = len(a_sources)
    first = chunks[:-1] or chunks
    buffers = [pltpu.VMEM((most, blk, blk), jnp.float32)] * 2 + [pltpu.SemaphoreType.DMA((2, most))]
    band = jax.ShapeDtypeStruct((blk, JB * blk), jnp.float32)
    late, c_early, b_late = pl.pallas_call(
        functools.partial(early_kernel, chunks, n_a, slots, a_at, b_at),
        out_shape=[
            jax.ShapeDtypeStruct((1 + 3 * most,), jnp.int32),
            band,
            jax.ShapeDtypeStruct((most * blk, blk), jnp.float32),
        ],
        in_specs=[ANY] * (n_a * len(first) + len(b_sources)),
        out_specs=[SMEM, VMEM, ANY],
        scratch_shapes=[
            pltpu.VMEM((tails, TAIL, blk), jnp.float32),
            pltpu.VMEM((TAIL, blk), jnp.int32),
            pltpu.SMEM((TAIL, blk), jnp.int32),
            pltpu.SMEM((STEPS, KPB), jnp.int32),
            pltpu.SMEM((most,), jnp.int32),
            *buffers,
            pltpu.SemaphoreType.DMA((most,)),
            pltpu.SemaphoreType.DMA((tails + 1,)),
        ],
        compiler_params=pltpu.CompilerParams(vmem_limit_bytes=24 * MIB),
        cost_estimate=pl.CostEstimate(flops=6 * 8 * blk**3, bytes_accessed=8 * MIB, transcendentals=0),
        name="early",
    )(*[x for arrays in a_sources for x in arrays[: len(first)]], *b_sources)
    return pl.pallas_call(
        functools.partial(late_kernel, n_a),
        out_shape=band,
        in_specs=[SMEM, VMEM, ANY] + [ANY] * n_a,
        out_specs=VMEM,
        scratch_shapes=buffers,
        compiler_params=pltpu.CompilerParams(vmem_limit_bytes=24 * MIB),
        cost_estimate=pl.CostEstimate(flops=6 * 2 * blk**3, bytes_accessed=2 * MIB, transcendentals=0),
        name="late",
    )(late, c_early, b_late, *[arrays[-1] for arrays in a_sources])


def as_rows(x):
    return x.reshape(-1, x.shape[-1])


def gathered(a_vals, a_code, b_vals, b_code, panels, group):
    chunks = [(0, a_vals.shape[0])]
    _, a_own, b_own = prepare(chunks, a_code, b_code, panels, as_rows(a_vals), as_rows(b_vals))
    a_all = lax.all_gather(a_own, "col")
    b_all = lax.all_gather(b_own, "row")
    a_sources, b_sources = [], []
    for step in range(STEPS):
        a_sources.append([lax.dynamic_index_in_dim(a_all, panels[step], 0, keepdims=False)])
        for g in range(group):
            b_sources.append(lax.dynamic_index_in_dim(b_all, panels[step] * group + g, 0, keepdims=False))
    slots = (group, b_vals.shape[0])
    return multiply(chunks, a_sources, b_sources, slots, lambda s: s, lambda s, g: s * group + g)


CHUNKS = [(0, 8), (8, 16)]
WINDOW = 5
UP = {
    (0, 1): [(None, ((0, 1), (1, 2)), {1: 0, 2: 1}), (0, ((1, 2), (2, 3)), {2: 0, 3: 1}), (1, ((2, 3),), {3: 0})],
    (0, 2): [(None, ((0, 1), (2, 3)), {1: 0, 3: 2}), (0, ((1, 2),), {2: 0}), (1, ((2, 3),), {3: 0})],
    (0, 3): [(None, ((0, 1),), {1: 0}), (0, ((1, 2),), {2: 0}), (1, ((2, 3),), {3: 0})],
    (1, 2): [(None, ((1, 2), (2, 3)), {2: 1, 3: 2}), (0, ((2, 3),), {3: 1})],
    (1, 3): [(None, ((1, 2),), {2: 1}), (0, ((2, 3),), {3: 1})],
    (2, 3): [(None, ((2, 3),), {3: 2})],
}


def chain_steps(roots, n):
    def flip(x):
        return n - 1 - x

    down = [
        (src, tuple((flip(x), flip(y)) for x, y in pairs), {flip(at): flip(p) for at, p in got.items()})
        for src, pairs, got in UP[tuple(sorted(map(flip, roots)))]
    ]
    return UP[roots], down


def pick(values, index):
    out = jnp.int32(values[0])
    for i, value in enumerate(values[1:], 1):
        out = jnp.where(index == i, jnp.int32(value), out)
    return out


def after(x, *earlier):
    return lax.optimization_barrier((x, *earlier))[0]


ORDER = {
    (0, 1): [
        "u0a", "x", "d0b", "u0b", "y", "u1a", "g", "so", "u1b", "u2a", "d0a", "sg", "sx", "u2b", "sy",
    ],
    (0, 2): [
        "u0a", "d0a", "x", "y", "d0b", "u0b", "u1a", "sx", "g", "u1b", "d1a", "u2a", "sy", "d1b", "u2b", "sg", "so",
    ],
    (0, 3): [
        "d0a", "u0a", "y", "x", "d0b", "u0b", "u1a", "d1a", "sy", "u1b", "g", "d1b", "u2a", "d2a", "sx", "u2b", "d2b",
        "so", "sg",
    ],
    (1, 2): [
        "u0b", "d0a", "y", "x", "so", "d0b", "u0a", "d1a", "sy", "g", "u1a", "u1b", "d1b", "sx", "sg",
    ],
}


def mirrored(name):
    return {"u": "d", "d": "u"}.get(name[0], name[0]) + name[1:]


def order_of(roots, n):
    if roots in ORDER:
        return ORDER[roots]
    return [mirrored(name) for name in ORDER[tuple(sorted(n - 1 - p for p in roots))]]


def pair_branch(roots, n, slots, pieces, b_own):
    group, _ = slots
    parts = "abcdefgh"[: len(pieces)]

    def exchange(bit):
        return "row", [(r, r ^ bit) for r in range(n * group)]

    moves = {"so": ("o", *exchange(1))}
    for q, name in enumerate("xyg", 1):
        moves[name] = ("o", *exchange(q * group))
        moves["s" + name] = (name, *exchange(1))
    held = dict(zip(parts, pieces), o=b_own)
    a_names = [list(parts)]
    a_table = [[0] * n for _ in roots]
    for way, steps in zip("ud", chain_steps(roots, n)):
        for number, (src, pairs, got) in enumerate(steps):
            for at, p in got.items():
                a_table[roots.index(p)][at] = len(a_names)
            for part in parts:
                moves[f"{way}{number}{part}"] = (part if src is None else f"{way}{src}{part}", "col", pairs)
            a_names.append([f"{way}{number}{part}" for part in parts])

    order = order_of(roots, n)
    ended = 0
    for i, name in enumerate(order):
        source, axis, pairs = moves.pop(name)
        x = held[source]
        ended = max(ended, i + 1 - WINDOW, order.index(source) + 1 if source in order else 0)
        if ended:
            x = lax.optimization_barrier((x, *[held[e] for e in order[max(0, ended - WINDOW) : ended] if e != source]))[0]
        held[name] = lax.ppermute(x, axis, pairs)
    assert not moves

    a_sources = [[held[name] for name in names] for names in a_names]
    b_sources = [held[name] for name in ("o", "x", "y", "g", "so", "sx", "sy", "sg")]

    def a_at(s):
        return pick(a_table[s], lax.axis_index("col"))

    def b_at(s, g):
        row = lax.axis_index("row")
        return ((row >> 1) ^ roots[s]) + jnp.where((row & 1) == g, 0, n)

    return multiply(CHUNKS, a_sources, b_sources, slots, a_at, b_at)


def shards(a_vals, a_code, b_vals, b_code, panels):
    n = lax.axis_size("col")
    group = lax.axis_size("row") // n
    if group != 2 or n != 4:
        return gathered(a_vals, a_code, b_vals, b_code, panels, group)
    which, *pieces, b_own = prepare(CHUNKS, a_code, b_code, panels, as_rows(a_vals), as_rows(b_vals))
    slots = (group, b_vals.shape[0])
    branches = [functools.partial(pair_branch, pair, n, slots) for pair in sorted(UP)]
    return lax.switch(which[0], branches, pieces, b_own)


def solution(mesh):
    return jax.shard_map(
        shards,
        mesh=mesh,
        in_specs=(
            P("row", "col", None),
            P("row", "col"),
            P("row", "col", None),
            P("row", "col"),
            P(),
        ),
        out_specs=P("row", "col"),
        check_vma=False,
    )
```

```python
import functools
import itertools

import jax
import jax.numpy as jnp
from jax import lax
from jax.experimental import pallas as pl
from jax.experimental.pallas import tpu as pltpu
from jax.sharding import PartitionSpec as P

KPB = 64
STEPS = 2
JB = 8
TAIL = 8
MIB = 2**20

SMEM = pl.BlockSpec(memory_space=pltpu.SMEM)
VMEM = pl.BlockSpec(memory_space=pltpu.VMEM)
ANY = pl.BlockSpec(memory_space=pl.ANY)


def rows_of(slot, blk):
    return pl.ds(pl.multiple_of(slot * blk, blk), blk)


def prepare_kernel(chunks, a_code, b_code, panels, a_rows, b_rows, which, *refs):
    pieces, b_own = refs[: len(chunks)], refs[len(chunks)]
    tails, sems = refs[len(chunks) + 1 :]
    blk = a_rows.shape[1]
    copies = [
        pltpu.make_async_copy(a_rows.at[pl.ds(f * blk, (e - f) * blk)], piece.at[pl.ds(0, (e - f) * blk)], sems.at[i])
        for i, ((f, e), piece) in enumerate(zip(chunks, pieces))
    ]
    copies.append(pltpu.make_async_copy(b_rows, b_own.at[pl.ds(0, b_rows.shape[0])], sems.at[len(chunks)]))
    for copy in copies:
        copy.start()
    tails[...] = jnp.zeros_like(tails)
    for i, (code, into) in enumerate(((a_code, pieces[0]), (b_code, b_own))):
        tails[i, 0:1, 0 : code.shape[1]] = code[...].astype(jnp.float32)
        last = into.shape[0] - TAIL
        copy = pltpu.make_async_copy(tails.at[i], into.at[pl.ds(last, TAIL)], sems.at[len(chunks) + 1 + i])
        copy.start()
        copies.append(copy)
    lo = jnp.minimum(panels[0], panels[1])
    hi = jnp.maximum(panels[0], panels[1])
    which[0] = jnp.where(lo == 0, 0, lo + 1) + hi - 1
    for copy in copies:
        copy.wait()


def prepare(chunks, a_code, b_code, panels, a_rows, b_rows):
    blk = a_rows.shape[1]
    sizes = [(e - f) * blk for f, e in chunks]
    sizes[0] += TAIL
    sizes.append(b_rows.shape[0] + TAIL)
    return pl.pallas_call(
        functools.partial(prepare_kernel, chunks),
        out_shape=[jax.ShapeDtypeStruct((1,), jnp.int32)] + [jax.ShapeDtypeStruct((x, blk), jnp.float32) for x in sizes],
        in_specs=[VMEM, VMEM, SMEM, ANY, ANY],
        out_specs=[SMEM] + [ANY] * len(sizes),
        scratch_shapes=[pltpu.VMEM((2, TAIL, blk), jnp.float32), pltpu.SemaphoreType.DMA((len(chunks) + 3,))],
        name="prepare",
    )(a_code.T, b_code.T, panels, a_rows, b_rows)


def split(x):
    high = x.astype(jnp.bfloat16)
    low = (x - high.astype(jnp.float32)).astype(jnp.bfloat16)
    return high, low


def dot(x, y):
    return jnp.dot(x, y, preferred_element_type=jnp.float32)


def add_products(count, column, a_buf, b_buf, sems, c_ref):
    blk = a_buf.shape[1]

    def one(m, carry):
        for which, buf in enumerate((a_buf, b_buf)):
            pltpu.make_async_copy(buf.at[m], buf.at[m], sems.at[which, m]).wait()
        a_high, a_low = split(a_buf[m])
        b_high, b_low = split(b_buf[m])
        prod = dot(a_high, b_high) + (dot(a_high, b_low) + dot(a_low, b_high))
        c_ref[:, rows_of(column(m), blk)] += prod
        return carry

    lax.fori_loop(0, count, one, 0)


def start_from(refs, source, rows, into, sem):
    for i, ref in enumerate(refs):

        @pl.when(source == i)
        def _():
            pltpu.make_async_copy(ref.at[rows], into, sem).start()


def early_kernel(chunks, n_a, slots, a_at, b_at, *refs):
    group, sb = slots
    parts = max(1, len(chunks) - 1)
    n_b = len(refs) - n_a * parts - 13
    a_refs = [refs[i * parts : (i + 1) * parts] for i in range(n_a)]
    b_refs = refs[n_a * parts : n_a * parts + n_b]
    late, c_ref, b_late, tails, ints, codes, table, plan, a_buf, b_buf, sems, late_sems, tail_sems = refs[n_a * parts + n_b :]
    sa = chunks[-1][1]
    last_first = chunks[-1][0]
    blk = a_buf.shape[1]
    k_rows = KPB // group
    sources = [[a_at(s)] + [b_at(s, g) for g in range(group)] for s in range(STEPS)]
    sources = [x for step in sources for x in step]

    for t, source in enumerate(sources):
        holders = b_refs if t % (1 + group) else [arrays[0] for arrays in a_refs]
        start_from(holders, source, pl.ds(holders[0].shape[0] - TAIL, TAIL), tails.at[t], tail_sems.at[t])
    for s in range(STEPS):
        for k in range(KPB):
            table[s, k] = jnp.int32(-1)
    c_ref[...] = jnp.zeros_like(c_ref)
    ints[...] = jnp.zeros_like(ints)
    for t in range(len(sources)):
        pltpu.make_async_copy(tails.at[t], tails.at[t], tail_sems.at[t]).wait()
        ints[t : t + 1, :] = tails[t, 0:1, :].astype(jnp.int32)
    copy = pltpu.make_async_copy(ints, codes, tail_sems.at[len(sources)])
    copy.start()
    copy.wait()

    counts = (jnp.int32(0), jnp.int32(0))
    for s in range(STEPS):
        row_a = s * (1 + group)
        for slot in range(sa):
            code = codes[row_a, slot]

            @pl.when(code >= 0)
            def _():
                table[s, code] = jnp.int32(slot)

        for g in range(group):

            def one(slot, counts):
                n_early, n_late = counts
                code = codes[row_a + 1 + g, slot]
                k = jnp.where(code >= 0, g * k_rows + code // JB, 0)
                a_slot = table[s, k]
                ok = (code >= 0) & (a_slot >= 0)
                is_late = a_slot >= last_first

                @pl.when(ok & jnp.logical_not(is_late))
                def _():
                    plan[n_early] = code % JB
                    for i, arrays in enumerate(a_refs):

                        @pl.when(sources[row_a] == i)
                        def _():
                            for (f, e), ref in zip(chunks[:-1], arrays):

                                @pl.when((a_slot >= f) & (a_slot < e))
                                def _():
                                    rows = rows_of(a_slot - f, blk)
                                    pltpu.make_async_copy(ref.at[rows], a_buf.at[n_early], sems.at[0, n_early]).start()

                    start_from(b_refs, sources[row_a + 1 + g], rows_of(slot, blk), b_buf.at[n_early], sems.at[1, n_early])

                @pl.when(ok & is_late)
                def _():
                    late[1 + 3 * n_late] = sources[row_a]
                    late[2 + 3 * n_late] = a_slot - last_first
                    late[3 + 3 * n_late] = code % JB
                    into = b_late.at[rows_of(n_late, blk)]
                    start_from(b_refs, sources[row_a + 1 + g], rows_of(slot, blk), into, late_sems.at[n_late])

                is_late = is_late.astype(jnp.int32)
                ok = ok.astype(jnp.int32)
                return n_early + ok * (1 - is_late), n_late + ok * is_late

            counts = lax.fori_loop(0, sb, one, counts)
    late[0] = counts[1]
    add_products(counts[0], lambda m: plan[m], a_buf, b_buf, sems, c_ref)

    def wait(m, carry):
        into = b_late.at[rows_of(m, blk)]
        pltpu.make_async_copy(into, into, late_sems.at[m]).wait()
        return carry

    lax.fori_loop(0, counts[1], wait, 0)


def late_kernel(n_a, late, c_in, b_late, *refs):
    a_refs, (c_ref, a_buf, b_buf, sems) = refs[:n_a], refs[n_a:]
    blk = a_buf.shape[1]

    def fetch(m, carry):
        start_from(a_refs, late[1 + 3 * m], rows_of(late[2 + 3 * m], blk), a_buf.at[m], sems.at[0, m])
        pltpu.make_async_copy(b_late.at[rows_of(m, blk)], b_buf.at[m], sems.at[1, m]).start()
        return carry

    lax.fori_loop(0, late[0], fetch, 0)
    c_ref[...] = c_in[...]
    add_products(late[0], lambda m: late[3 + 3 * m], a_buf, b_buf, sems, c_ref)


def multiply(chunks, a_sources, b_sources, slots, a_at, b_at):
    group, sb = slots
    blk = b_sources[0].shape[1]
    most = STEPS * group * sb
    tails = STEPS * (1 + group)
    n_a = len(a_sources)
    first = chunks[:-1] or chunks
    buffers = [pltpu.VMEM((most, blk, blk), jnp.float32)] * 2 + [pltpu.SemaphoreType.DMA((2, most))]
    band = jax.ShapeDtypeStruct((blk, JB * blk), jnp.float32)
    late, c_early, b_late = pl.pallas_call(
        functools.partial(early_kernel, chunks, n_a, slots, a_at, b_at),
        out_shape=[
            jax.ShapeDtypeStruct((1 + 3 * most,), jnp.int32),
            band,
            jax.ShapeDtypeStruct((most * blk, blk), jnp.float32),
        ],
        in_specs=[ANY] * (n_a * len(first) + len(b_sources)),
        out_specs=[SMEM, VMEM, ANY],
        scratch_shapes=[
            pltpu.VMEM((tails, TAIL, blk), jnp.float32),
            pltpu.VMEM((TAIL, blk), jnp.int32),
            pltpu.SMEM((TAIL, blk), jnp.int32),
            pltpu.SMEM((STEPS, KPB), jnp.int32),
            pltpu.SMEM((most,), jnp.int32),
            *buffers,
            pltpu.SemaphoreType.DMA((most,)),
            pltpu.SemaphoreType.DMA((tails + 1,)),
        ],
        compiler_params=pltpu.CompilerParams(vmem_limit_bytes=24 * MIB),
        cost_estimate=pl.CostEstimate(flops=6 * 8 * blk**3, bytes_accessed=8 * MIB, transcendentals=0),
        name="early",
    )(*[x for arrays in a_sources for x in arrays[: len(first)]], *b_sources)
    return pl.pallas_call(
        functools.partial(late_kernel, n_a),
        out_shape=band,
        in_specs=[SMEM, VMEM, ANY] + [ANY] * n_a,
        out_specs=VMEM,
        scratch_shapes=buffers,
        compiler_params=pltpu.CompilerParams(vmem_limit_bytes=24 * MIB),
        cost_estimate=pl.CostEstimate(flops=6 * 2 * blk**3, bytes_accessed=2 * MIB, transcendentals=0),
        name="late",
    )(late, c_early, b_late, *[arrays[-1] for arrays in a_sources])


def as_rows(x):
    return x.reshape(-1, x.shape[-1])


def gathered(a_vals, a_code, b_vals, b_code, panels, group):
    chunks = [(0, a_vals.shape[0])]
    _, a_own, b_own = prepare(chunks, a_code, b_code, panels, as_rows(a_vals), as_rows(b_vals))
    a_all = lax.all_gather(a_own, "col")
    b_all = lax.all_gather(b_own, "row")
    a_sources, b_sources = [], []
    for step in range(STEPS):
        a_sources.append([lax.dynamic_index_in_dim(a_all, panels[step], 0, keepdims=False)])
        for g in range(group):
            b_sources.append(lax.dynamic_index_in_dim(b_all, panels[step] * group + g, 0, keepdims=False))
    slots = (group, b_vals.shape[0])
    return multiply(chunks, a_sources, b_sources, slots, lambda s: s, lambda s, g: s * group + g)


CHUNKS = [(0, 8), (8, 16)]
ROUTES = {
    (0, 1): [(None, ((0, 1), (1, 2))), (0, ((1, 2), (2, 3))), (1, ((2, 3), (3, 0)))],
    (0, 2): [(None, ((0, 1), (2, 3))), (0, ((1, 2), (3, 1))), (1, ((1, 0), (2, 3)))],
    (0, 3): [(None, ((0, 1), (3, 2))), (0, ((1, 2), (2, 1))), (1, ((2, 3), (1, 0)))],
    (1, 2): [(None, ((1, 0), (2, 3))), (None, ((1, 2), (2, 1))), (1, ((1, 0), (2, 3)))],
}
WRITTEN = ("0a", "1a", "0b", "1b", "x", "y", "g", "2a", "2b", "sx", "sy", "so", "sg")
WAITS = {
    (0, 1): {
        "sy": ("2a", "g", "sg"),
    },
    (0, 2): {
        "1a": ("0a",), "sx": ("y", "x"), "2b": ("sx", "1b"), "sg": ("1b", "2a"),
    },
    (0, 3): {
        "sx": ("y", "x"), "1b": ("x", "0b"), "2a": ("0b", "1a"), "sy": ("1a", "g"), "2b": ("sx", "1b"),
        "sg": ("1b", "2a"), "so": ("1a",),
    },
    (1, 2): {
        "0b": ("0a",), "2a": ("0a",), "2b": ("0b",), "sg": ("2a",), "so": ("1b",), "g": ("1a",),
    },
}


def route_of(roots, n):
    mirror = roots not in ROUTES
    key = tuple(sorted(n - 1 - p for p in roots)) if mirror else roots
    steps, brings = [], []
    for source, pairs in ROUTES[key]:
        if mirror:
            pairs = tuple((n - 1 - x, n - 1 - y) for x, y in pairs)
        steps.append((source, pairs))
        brings.append({y: x if source is None else brings[source][x] for x, y in pairs})
    return steps, brings, WAITS[key]


def pick(values, index):
    out = jnp.int32(values[0])
    for i, value in enumerate(values[1:], 1):
        out = jnp.where(index == i, jnp.int32(value), out)
    return out


def after(x, *earlier):
    return lax.optimization_barrier((x, *earlier))[0]


def pair_branch(roots, n, slots, pieces, b_own):
    group, _ = slots
    parts = "abcdefgh"[: len(pieces)]

    def exchange(bit):
        return "row", [(r, r ^ bit) for r in range(n * group)]

    moves = {"so": ("o", *exchange(1))}
    for q, name in enumerate("xyg", 1):
        moves[name] = ("o", *exchange(q * group))
        moves["s" + name] = (name, *exchange(1))
    held = dict(zip(parts, pieces), o=b_own)
    a_names = [list(parts)]
    a_table = [[0] * n for _ in roots]
    steps, brings, waits = route_of(roots, n)
    for number, (source, pairs) in enumerate(steps):
        for at, p in brings[number].items():
            a_table[roots.index(p)][at] = len(a_names)
        for part in parts:
            moves[f"{number}{part}"] = (part if source is None else f"{source}{part}", "col", pairs)
        a_names.append([f"{number}{part}" for part in parts])

    while moves:
        for name in [name for name in WRITTEN if name in moves]:
            source, axis, pairs = moves[name]
            if all(e in held for e in (source, *waits.get(name, ()))):
                x = held[source]
                if name in waits:
                    x = lax.optimization_barrier((x, *[held[e] for e in waits[name]]))[0]
                held[name] = lax.ppermute(x, axis, pairs)
                del moves[name]

    a_sources = [[held[name] for name in names] for names in a_names]
    b_sources = [held[name] for name in ("o", "x", "y", "g", "so", "sx", "sy", "sg")]

    def a_at(s):
        return pick(a_table[s], lax.axis_index("col"))

    def b_at(s, g):
        row = lax.axis_index("row")
        return ((row >> 1) ^ roots[s]) + jnp.where((row & 1) == g, 0, n)

    return multiply(CHUNKS, a_sources, b_sources, slots, a_at, b_at)


def shards(a_vals, a_code, b_vals, b_code, panels):
    n = lax.axis_size("col")
    group = lax.axis_size("row") // n
    if group != 2 or n != 4:
        return gathered(a_vals, a_code, b_vals, b_code, panels, group)
    which, *pieces, b_own = prepare(CHUNKS, a_code, b_code, panels, as_rows(a_vals), as_rows(b_vals))
    slots = (group, b_vals.shape[0])
    branches = [functools.partial(pair_branch, pair, n, slots) for pair in itertools.combinations(range(n), 2)]
    return lax.switch(which[0], branches, pieces, b_own)


def solution(mesh):
    return jax.shard_map(
        shards,
        mesh=mesh,
        in_specs=(
            P("row", "col", None),
            P("row", "col"),
            P("row", "col", None),
            P("row", "col"),
            P(),
        ),
        out_specs=P("row", "col"),
        check_vma=False,
    )
```

```python
import functools
import itertools

import jax
import jax.numpy as jnp
from jax import lax
from jax.experimental import pallas as pl
from jax.experimental.pallas import tpu as pltpu
from jax.sharding import PartitionSpec as P

KPB = 64
STEPS = 2
JB = 8
TAIL = 8
MIB = 2**20

SMEM = pl.BlockSpec(memory_space=pltpu.SMEM)
VMEM = pl.BlockSpec(memory_space=pltpu.VMEM)
ANY = pl.BlockSpec(memory_space=pl.ANY)


def rows_of(slot, blk):
    return pl.ds(pl.multiple_of(slot * blk, blk), blk)


def prepare_kernel(chunks, a_code, b_code, panels, a_rows, b_rows, which, *refs):
    pieces, b_own = refs[: len(chunks)], refs[len(chunks)]
    tails, sems = refs[len(chunks) + 1 :]
    blk = a_rows.shape[1]
    copies = [
        pltpu.make_async_copy(a_rows.at[pl.ds(f * blk, (e - f) * blk)], piece.at[pl.ds(0, (e - f) * blk)], sems.at[i])
        for i, ((f, e), piece) in enumerate(zip(chunks, pieces))
    ]
    copies.append(pltpu.make_async_copy(b_rows, b_own.at[pl.ds(0, b_rows.shape[0])], sems.at[len(chunks)]))
    for copy in copies:
        copy.start()
    tails[...] = jnp.zeros_like(tails)
    for i, (code, into) in enumerate(((a_code, pieces[0]), (b_code, b_own))):
        tails[i, 0:1, 0 : code.shape[1]] = code[...].astype(jnp.float32)
        last = into.shape[0] - TAIL
        copy = pltpu.make_async_copy(tails.at[i], into.at[pl.ds(last, TAIL)], sems.at[len(chunks) + 1 + i])
        copy.start()
        copies.append(copy)
    lo = jnp.minimum(panels[0], panels[1])
    hi = jnp.maximum(panels[0], panels[1])
    which[0] = jnp.where(lo == 0, 0, lo + 1) + hi - 1
    for copy in copies:
        copy.wait()


def prepare(chunks, a_code, b_code, panels, a_rows, b_rows):
    blk = a_rows.shape[1]
    sizes = [(e - f) * blk for f, e in chunks]
    sizes[0] += TAIL
    sizes.append(b_rows.shape[0] + TAIL)
    return pl.pallas_call(
        functools.partial(prepare_kernel, chunks),
        out_shape=[jax.ShapeDtypeStruct((1,), jnp.int32)] + [jax.ShapeDtypeStruct((x, blk), jnp.float32) for x in sizes],
        in_specs=[VMEM, VMEM, SMEM, ANY, ANY],
        out_specs=[SMEM] + [ANY] * len(sizes),
        scratch_shapes=[pltpu.VMEM((2, TAIL, blk), jnp.float32), pltpu.SemaphoreType.DMA((len(chunks) + 3,))],
        name="prepare",
    )(a_code.T, b_code.T, panels, a_rows, b_rows)


def split(x):
    high = x.astype(jnp.bfloat16)
    low = (x - high.astype(jnp.float32)).astype(jnp.bfloat16)
    return high, low


def product(a, b):
    a_high, a_low = split(a)
    b_high, b_low = split(b)
    left = jnp.concatenate([a_high, a_high, a_low], axis=1)
    right = jnp.concatenate([b_high, b_low, b_high], axis=0)
    return jnp.dot(left, right, preferred_element_type=jnp.float32)


def add_products(count, column, a_buf, b_buf, sems, c_ref):
    blk = a_buf.shape[1]

    def one(m, carry):
        for which, buf in enumerate((a_buf, b_buf)):
            pltpu.make_async_copy(buf.at[m], buf.at[m], sems.at[which, m]).wait()
        c_ref[:, rows_of(column(m), blk)] += product(a_buf[m], b_buf[m])
        return carry

    lax.fori_loop(0, count, one, 0)


def start_from(refs, source, rows, into, sem):
    for i, ref in enumerate(refs):

        @pl.when(source == i)
        def _():
            pltpu.make_async_copy(ref.at[rows], into, sem).start()


def early_kernel(chunks, n_a, slots, a_at, b_at, *refs):
    group, sb = slots
    parts = max(1, len(chunks) - 1)
    n_b = len(refs) - n_a * parts - 12
    a_refs = [refs[i * parts : (i + 1) * parts] for i in range(n_a)]
    b_refs = refs[n_a * parts : n_a * parts + n_b]
    late, c_ref, b_late, tails, found, found_s, plan, a_buf, b_buf, sems, late_sems, tail_sems = refs[n_a * parts + n_b :]
    sa = chunks[-1][1]
    last_first = chunks[-1][0]
    blk = a_buf.shape[1]
    k_rows = KPB // group
    sources = [[a_at(s)] + [b_at(s, g) for g in range(group)] for s in range(STEPS)]

    def tail(s, i):
        return s * (1 + group) + i

    for s in range(STEPS):
        for i, source in enumerate(sources[s]):
            holders = b_refs if i else [arrays[0] for arrays in a_refs]
            rows = pl.ds(holders[0].shape[0] - TAIL, TAIL)
            start_from(holders, source, rows, tails.at[tail(s, i)], tail_sems.at[tail(s, i)])
    c_ref[...] = jnp.zeros_like(c_ref)
    found[...] = jnp.full_like(found, -1)
    for i in range(STEPS * (1 + group)):
        pltpu.make_async_copy(tails.at[i], tails.at[i], tail_sems.at[i]).wait()

    for s in range(STEPS):
        a_codes = tails[tail(s, 0), 0:1, :].astype(jnp.int32)
        for g in range(group):
            b_codes = tails[tail(s, 1 + g), 0:1, :].astype(jnp.int32)
            used = (b_codes >= 0) & (lax.broadcasted_iota(jnp.int32, b_codes.shape, 1) < sb)
            k = jnp.where(used, g * k_rows + b_codes // JB, -2)
            hit = jnp.full_like(k, -1)
            for slot in range(sa):
                hit = jnp.where(a_codes[:, slot : slot + 1] == k, slot, hit)
            found[s * group + g : s * group + g + 1, :] = jnp.where(hit >= 0, hit * JB + b_codes % JB, -1)
    copy = pltpu.make_async_copy(found, found_s, tail_sems.at[STEPS * (1 + group)])
    copy.start()
    copy.wait()

    counts = (jnp.int32(0), jnp.int32(0))
    for s in range(STEPS):
        for g in range(group):

            def one(slot, counts):
                n_early, n_late = counts
                hit = found_s[s * group + g, slot]
                a_slot = hit // JB
                early = (hit >= 0) & (a_slot < last_first)
                is_late = a_slot >= last_first

                @pl.when(early)
                def _():
                    plan[n_early] = hit % JB
                    for i, arrays in enumerate(a_refs):

                        @pl.when(sources[s][0] == i)
                        def _():
                            for (f, e), ref in zip(chunks[:-1], arrays):

                                @pl.when((a_slot >= f) & (a_slot < e))
                                def _():
                                    rows = rows_of(a_slot - f, blk)
                                    pltpu.make_async_copy(ref.at[rows], a_buf.at[n_early], sems.at[0, n_early]).start()

                    start_from(b_refs, sources[s][1 + g], rows_of(slot, blk), b_buf.at[n_early], sems.at[1, n_early])

                @pl.when(is_late)
                def _():
                    late[1 + 3 * n_late] = sources[s][0]
                    late[2 + 3 * n_late] = a_slot - last_first
                    late[3 + 3 * n_late] = hit % JB
                    into = b_late.at[rows_of(n_late, blk)]
                    start_from(b_refs, sources[s][1 + g], rows_of(slot, blk), into, late_sems.at[n_late])

                return n_early + early.astype(jnp.int32), n_late + is_late.astype(jnp.int32)

            counts = lax.fori_loop(0, sb, one, counts)
    late[0] = counts[1]
    add_products(counts[0], lambda m: plan[m], a_buf, b_buf, sems, c_ref)

    def wait(m, carry):
        into = b_late.at[rows_of(m, blk)]
        pltpu.make_async_copy(into, into, late_sems.at[m]).wait()
        return carry

    lax.fori_loop(0, counts[1], wait, 0)


def late_kernel(n_a, late, c_in, b_late, *refs):
    a_refs, (c_ref, a_buf, b_buf, sems) = refs[:n_a], refs[n_a:]
    blk = a_buf.shape[1]

    def fetch(m, carry):
        start_from(a_refs, late[1 + 3 * m], rows_of(late[2 + 3 * m], blk), a_buf.at[m], sems.at[0, m])
        pltpu.make_async_copy(b_late.at[rows_of(m, blk)], b_buf.at[m], sems.at[1, m]).start()
        return carry

    lax.fori_loop(0, late[0], fetch, 0)
    c_ref[...] = c_in[...]
    add_products(late[0], lambda m: late[3 + 3 * m], a_buf, b_buf, sems, c_ref)


def add_early(chunks, a_sources, b_sources, slots, a_at, b_at):
    group, sb = slots
    blk = b_sources[0].shape[1]
    most = STEPS * group * sb
    tails = STEPS * (1 + group)
    n_a = len(a_sources)
    first = chunks[:-1] or chunks
    buffers = [pltpu.VMEM((most, blk, blk), jnp.float32)] * 2 + [pltpu.SemaphoreType.DMA((2, most))]
    band = jax.ShapeDtypeStruct((blk, JB * blk), jnp.float32)
    late, c_early, b_late = pl.pallas_call(
        functools.partial(early_kernel, chunks, n_a, slots, a_at, b_at),
        out_shape=[
            jax.ShapeDtypeStruct((1 + 3 * most,), jnp.int32),
            band,
            jax.ShapeDtypeStruct((most * blk, blk), jnp.float32),
        ],
        in_specs=[ANY] * (n_a * len(first) + len(b_sources)),
        out_specs=[SMEM, VMEM, ANY],
        scratch_shapes=[
            pltpu.VMEM((tails, TAIL, blk), jnp.float32),
            pltpu.VMEM((max(8, STEPS * group), blk), jnp.int32),
            pltpu.SMEM((max(8, STEPS * group), blk), jnp.int32),
            pltpu.SMEM((most,), jnp.int32),
            *buffers,
            pltpu.SemaphoreType.DMA((most,)),
            pltpu.SemaphoreType.DMA((tails + 1,)),
        ],
        compiler_params=pltpu.CompilerParams(vmem_limit_bytes=24 * MIB),
        cost_estimate=pl.CostEstimate(flops=6 * 8 * blk**3, bytes_accessed=8 * MIB, transcendentals=0),
        name="early",
    )(*[x for arrays in a_sources for x in arrays[: len(first)]], *b_sources)
    return late, c_early, b_late


def add_late(late, c_early, b_late, a_last):
    blk = a_last[0].shape[1]
    most = (late.shape[0] - 1) // 3
    buffers = [pltpu.VMEM((most, blk, blk), jnp.float32)] * 2 + [pltpu.SemaphoreType.DMA((2, most))]
    return pl.pallas_call(
        functools.partial(late_kernel, len(a_last)),
        out_shape=jax.ShapeDtypeStruct(c_early.shape, c_early.dtype),
        in_specs=[SMEM, VMEM, ANY] + [ANY] * len(a_last),
        out_specs=VMEM,
        scratch_shapes=buffers,
        compiler_params=pltpu.CompilerParams(vmem_limit_bytes=24 * MIB),
        cost_estimate=pl.CostEstimate(flops=6 * 2 * blk**3, bytes_accessed=2 * MIB, transcendentals=0),
        name="late",
    )(late, c_early, b_late, *a_last)


def as_rows(x):
    return x.reshape(-1, x.shape[-1])


def gathered(a_vals, a_code, b_vals, b_code, panels, group):
    chunks = [(0, a_vals.shape[0])]
    _, a_own, b_own = prepare(chunks, a_code, b_code, panels, as_rows(a_vals), as_rows(b_vals))
    a_all = lax.all_gather(a_own, "col")
    b_all = lax.all_gather(b_own, "row")
    a_sources, b_sources = [], []
    for step in range(STEPS):
        a_sources.append([lax.dynamic_index_in_dim(a_all, panels[step], 0, keepdims=False)])
        for g in range(group):
            b_sources.append(lax.dynamic_index_in_dim(b_all, panels[step] * group + g, 0, keepdims=False))
    slots = (group, b_vals.shape[0])
    early = add_early(chunks, a_sources, b_sources, slots, lambda s: s, lambda s, g: s * group + g)
    return add_late(*early, [arrays[-1] for arrays in a_sources])


CHUNKS = [(0, 8), (8, 16)]
ROUTES = {
    (0, 1): [(None, ((0, 1), (1, 2))), (0, ((1, 2), (2, 3))), (1, ((2, 3), (3, 0)))],
    (0, 2): [(None, ((0, 1), (2, 3))), (0, ((1, 2), (3, 1))), (1, ((1, 0), (2, 3)))],
    (0, 3): [(None, ((0, 1), (3, 2))), (0, ((1, 2), (2, 1))), (1, ((2, 3), (1, 0)))],
    (1, 2): [(None, ((1, 0), (2, 3))), (None, ((1, 2), (2, 1))), (1, ((1, 0), (2, 3)))],
}
WRITTEN = ("0a", "1a", "0b", "1b", "x", "y", "g", "2a", "2b", "sx", "sy", "so", "sg")
WAITS = {
    (0, 1): {
        "sy": ("2a", "g", "sg"),
    },
    (0, 2): {
        "1a": ("0a",), "sx": ("y", "x"), "2b": ("sx", "1b"), "sg": ("1b", "2a", "g"), "sy": ("1b",),
    },
    (0, 3): {
        "sx": ("y", "x"), "1b": ("x", "0b"), "2a": ("0b", "1a"), "sy": ("1a", "g"), "2b": ("sx", "1b"),
        "sg": ("1b", "2a"), "so": ("1a",),
    },
    (1, 2): {
        "0b": ("0a",), "2a": ("0a",), "2b": ("0b",), "sg": ("2a",), "so": ("1b",), "g": ("1a",),
    },
}


def route_of(roots, n):
    mirror = roots not in ROUTES
    key = tuple(sorted(n - 1 - p for p in roots)) if mirror else roots
    steps, brings = [], []
    for source, pairs in ROUTES[key]:
        if mirror:
            pairs = tuple((n - 1 - x, n - 1 - y) for x, y in pairs)
        steps.append((source, pairs))
        brings.append({y: x if source is None else brings[source][x] for x, y in pairs})
    return steps, brings, WAITS[key]


def pick(values, index):
    out = jnp.int32(values[0])
    for i, value in enumerate(values[1:], 1):
        out = jnp.where(index == i, jnp.int32(value), out)
    return out


def after(x, *earlier):
    return lax.optimization_barrier((x, *earlier))[0]


def pair_branch(roots, n, slots, pieces, b_own):
    group, _ = slots
    parts = "abcdefgh"[: len(pieces)]

    def exchange(bit):
        return "row", [(r, r ^ bit) for r in range(n * group)]

    moves = {"so": ("o", *exchange(1))}
    for q, name in enumerate("xyg", 1):
        moves[name] = ("o", *exchange(q * group))
        moves["s" + name] = (name, *exchange(1))
    held = dict(zip(parts, pieces), o=b_own)
    a_names = [list(parts)]
    a_table = [[0] * n for _ in roots]
    steps, brings, waits = route_of(roots, n)
    for number, (source, pairs) in enumerate(steps):
        for at, p in brings[number].items():
            a_table[roots.index(p)][at] = len(a_names)
        for part in parts:
            moves[f"{number}{part}"] = (part if source is None else f"{source}{part}", "col", pairs)
        a_names.append([f"{number}{part}" for part in parts])

    while moves:
        for name in [name for name in WRITTEN if name in moves]:
            source, axis, pairs = moves[name]
            if all(e in held for e in (source, *waits.get(name, ()))):
                x = held[source]
                if name in waits:
                    x = lax.optimization_barrier((x, *[held[e] for e in waits[name]]))[0]
                held[name] = lax.ppermute(x, axis, pairs)
                del moves[name]

    a_sources = [[held[name] for name in names] for names in a_names]
    b_sources = [held[name] for name in ("o", "x", "y", "g", "so", "sx", "sy", "sg")]

    def a_at(s):
        return pick(a_table[s], lax.axis_index("col"))

    def b_at(s, g):
        row = lax.axis_index("row")
        return ((row >> 1) ^ roots[s]) + jnp.where((row & 1) == g, 0, n)

    early = add_early(CHUNKS, a_sources, b_sources, slots, a_at, b_at)
    return early, [arrays[-1] for arrays in a_sources[1:]]


def shards(a_vals, a_code, b_vals, b_code, panels):
    n = lax.axis_size("col")
    group = lax.axis_size("row") // n
    if group != 2 or n != 4:
        return gathered(a_vals, a_code, b_vals, b_code, panels, group)
    which, *pieces, b_own = prepare(CHUNKS, a_code, b_code, panels, as_rows(a_vals), as_rows(b_vals))
    slots = (group, b_vals.shape[0])
    branches = [functools.partial(pair_branch, pair, n, slots) for pair in itertools.combinations(range(n), 2)]
    early, a_last = lax.switch(which[0], branches, pieces, b_own)
    return add_late(*early, [pieces[-1], *a_last])


def solution(mesh):
    return jax.shard_map(
        shards,
        mesh=mesh,
        in_specs=(
            P("row", "col", None),
            P("row", "col"),
            P("row", "col", None),
            P("row", "col"),
            P(),
        ),
        out_specs=P("row", "col"),
        check_vma=False,
    )
```

```python
import functools
import itertools

import jax
import jax.numpy as jnp
from jax import lax
from jax.experimental import pallas as pl
from jax.experimental.pallas import tpu as pltpu
from jax.sharding import PartitionSpec as P

KPB = 64
STEPS = 2
JB = 8
TAIL = 8
MIB = 2**20

SMEM = pl.BlockSpec(memory_space=pltpu.SMEM)
VMEM = pl.BlockSpec(memory_space=pltpu.VMEM)
ANY = pl.BlockSpec(memory_space=pl.ANY)


def rows_of(slot, blk):
    return pl.ds(pl.multiple_of(slot * blk, blk), blk)


def prepare_kernel(chunks, a_code, b_code, panels, a_rows, b_rows, which, *refs):
    pieces, b_own = refs[: len(chunks)], refs[len(chunks)]
    tails, sems = refs[len(chunks) + 1 :]
    blk = a_rows.shape[1]
    copies = [
        pltpu.make_async_copy(a_rows.at[pl.ds(f * blk, (e - f) * blk)], piece.at[pl.ds(0, (e - f) * blk)], sems.at[i])
        for i, ((f, e), piece) in enumerate(zip(chunks, pieces))
    ]
    copies.append(pltpu.make_async_copy(b_rows, b_own.at[pl.ds(0, b_rows.shape[0])], sems.at[len(chunks)]))
    for copy in copies:
        copy.start()
    tails[...] = jnp.zeros_like(tails)
    for i, (code, into) in enumerate(((a_code, pieces[0]), (b_code, b_own))):
        tails[i, 0:1, 0 : code.shape[1]] = code[...].astype(jnp.float32)
        last = into.shape[0] - TAIL
        copy = pltpu.make_async_copy(tails.at[i], into.at[pl.ds(last, TAIL)], sems.at[len(chunks) + 1 + i])
        copy.start()
        copies.append(copy)
    lo = jnp.minimum(panels[0], panels[1])
    hi = jnp.maximum(panels[0], panels[1])
    which[0] = jnp.where(lo == 0, 0, lo + 1) + hi - 1
    for copy in copies:
        copy.wait()


def prepare(chunks, a_code, b_code, panels, a_rows, b_rows):
    blk = a_rows.shape[1]
    sizes = [(e - f) * blk for f, e in chunks]
    sizes[0] += TAIL
    sizes.append(b_rows.shape[0] + TAIL)
    return pl.pallas_call(
        functools.partial(prepare_kernel, chunks),
        out_shape=[jax.ShapeDtypeStruct((1,), jnp.int32)] + [jax.ShapeDtypeStruct((x, blk), jnp.float32) for x in sizes],
        in_specs=[VMEM, VMEM, SMEM, ANY, ANY],
        out_specs=[SMEM] + [ANY] * len(sizes),
        scratch_shapes=[pltpu.VMEM((2, TAIL, blk), jnp.float32), pltpu.SemaphoreType.DMA((len(chunks) + 3,))],
        name="prepare",
    )(a_code.T, b_code.T, panels, a_rows, b_rows)


def split(x):
    high = x.astype(jnp.bfloat16)
    low = (x - high.astype(jnp.float32)).astype(jnp.bfloat16)
    return high, low


def product(a, b):
    a_high, a_low = split(a)
    b_high, b_low = split(b)
    left = jnp.concatenate([a_high, a_high, a_low], axis=1)
    right = jnp.concatenate([b_high, b_low, b_high], axis=0)
    return jnp.dot(left, right, preferred_element_type=jnp.float32)


def add_products(count, column, a_buf, b_buf, sems, c_ref):
    blk = a_buf.shape[1]

    def one(m, carry):
        for which, buf in enumerate((a_buf, b_buf)):
            pltpu.make_async_copy(buf.at[m], buf.at[m], sems.at[which, m]).wait()
        c_ref[:, rows_of(column(m), blk)] += product(a_buf[m], b_buf[m])
        return carry

    lax.fori_loop(0, count, one, 0)


def start_from(refs, source, rows, into, sem):
    for i, ref in enumerate(refs):

        @pl.when(source == i)
        def _():
            pltpu.make_async_copy(ref.at[rows], into, sem).start()


def early_kernel(chunks, n_a, b_parts, slots, a_at, b_at, *refs):
    group, sb = slots
    parts = max(1, len(chunks) - 1)
    n_b = sum(len(firsts) for firsts in b_parts)
    a_refs = [refs[i * parts : (i + 1) * parts] for i in range(n_a)]
    flat = iter(refs[n_a * parts : n_a * parts + n_b])
    b_refs = [[(first, next(flat)) for first in firsts] for firsts in b_parts]
    late, c_ref, b_late, tails, found, found_s, plan, a_buf, b_buf, sems, late_sems, tail_sems = refs[n_a * parts + n_b :]
    sa = chunks[-1][1]
    last_first = chunks[-1][0]
    blk = a_buf.shape[1]
    k_rows = KPB // group
    sources = [[a_at(s)] + [b_at(s, g) for g in range(group)] for s in range(STEPS)]

    def tail(s, i):
        return s * (1 + group) + i

    for s in range(STEPS):
        for i, source in enumerate(sources[s]):
            for j, holder in enumerate([held[-1][1] for held in b_refs] if i else [arrays[0] for arrays in a_refs]):

                @pl.when(source == j)
                def _():
                    rows = pl.ds(holder.shape[0] - TAIL, TAIL)
                    pltpu.make_async_copy(holder.at[rows], tails.at[tail(s, i)], tail_sems.at[tail(s, i)]).start()

    c_ref[...] = jnp.zeros_like(c_ref)
    found[...] = jnp.full_like(found, -1)
    for i in range(STEPS * (1 + group)):
        pltpu.make_async_copy(tails.at[i], tails.at[i], tail_sems.at[i]).wait()

    for s in range(STEPS):
        a_codes = tails[tail(s, 0), 0:1, :].astype(jnp.int32)
        for g in range(group):
            b_codes = tails[tail(s, 1 + g), 0:1, :].astype(jnp.int32)
            used = (b_codes >= 0) & (lax.broadcasted_iota(jnp.int32, b_codes.shape, 1) < sb)
            k = jnp.where(used, g * k_rows + b_codes // JB, -2)
            hit = jnp.full_like(k, -1)
            for slot in range(sa):
                hit = jnp.where(a_codes[:, slot : slot + 1] == k, slot, hit)
            found[s * group + g : s * group + g + 1, :] = jnp.where(hit >= 0, hit * JB + b_codes % JB, -1)
    copy = pltpu.make_async_copy(found, found_s, tail_sems.at[STEPS * (1 + group)])
    copy.start()
    copy.wait()

    def start_b(source, slot, into, sem):
        for i, held in enumerate(b_refs):

            @pl.when(source == i)
            def _():
                for j, (first, ref) in enumerate(held):
                    end = held[j + 1][0] if j + 1 < len(held) else sb

                    @pl.when((slot >= first) & (slot < end))
                    def _():
                        pltpu.make_async_copy(ref.at[rows_of(slot - first, blk)], into, sem).start()

    counts = (jnp.int32(0), jnp.int32(0))
    for s in range(STEPS):
        for g in range(group):

            def one(slot, counts):
                n_early, n_late = counts
                hit = found_s[s * group + g, slot]
                a_slot = hit // JB
                early = (hit >= 0) & (a_slot < last_first)
                is_late = a_slot >= last_first

                @pl.when(early)
                def _():
                    plan[n_early] = hit % JB
                    for i, arrays in enumerate(a_refs):

                        @pl.when(sources[s][0] == i)
                        def _():
                            for (f, e), ref in zip(chunks[:-1], arrays):

                                @pl.when((a_slot >= f) & (a_slot < e))
                                def _():
                                    rows = rows_of(a_slot - f, blk)
                                    pltpu.make_async_copy(ref.at[rows], a_buf.at[n_early], sems.at[0, n_early]).start()

                    start_b(sources[s][1 + g], slot, b_buf.at[n_early], sems.at[1, n_early])

                @pl.when(is_late)
                def _():
                    late[1 + 3 * n_late] = sources[s][0]
                    late[2 + 3 * n_late] = a_slot - last_first
                    late[3 + 3 * n_late] = hit % JB
                    into = b_late.at[rows_of(n_late, blk)]
                    start_b(sources[s][1 + g], slot, into, late_sems.at[n_late])

                return n_early + early.astype(jnp.int32), n_late + is_late.astype(jnp.int32)

            counts = lax.fori_loop(0, sb, one, counts)
    late[0] = counts[1]
    add_products(counts[0], lambda m: plan[m], a_buf, b_buf, sems, c_ref)

    def wait(m, carry):
        into = b_late.at[rows_of(m, blk)]
        pltpu.make_async_copy(into, into, late_sems.at[m]).wait()
        return carry

    lax.fori_loop(0, counts[1], wait, 0)


def late_kernel(n_a, late, c_in, b_late, *refs):
    a_refs, (c_ref, a_buf, b_buf, sems) = refs[:n_a], refs[n_a:]
    blk = a_buf.shape[1]

    def fetch(m, carry):
        start_from(a_refs, late[1 + 3 * m], rows_of(late[2 + 3 * m], blk), a_buf.at[m], sems.at[0, m])
        pltpu.make_async_copy(b_late.at[rows_of(m, blk)], b_buf.at[m], sems.at[1, m]).start()
        return carry

    lax.fori_loop(0, late[0], fetch, 0)
    c_ref[...] = c_in[...]
    add_products(late[0], lambda m: late[3 + 3 * m], a_buf, b_buf, sems, c_ref)


def add_early(chunks, a_sources, b_sources, slots, a_at, b_at):
    group, sb = slots
    b_flat = [array for held in b_sources for _, array in held]
    blk = b_flat[0].shape[1]
    most = STEPS * group * sb
    tails = STEPS * (1 + group)
    n_a = len(a_sources)
    first = chunks[:-1] or chunks
    buffers = [pltpu.VMEM((most, blk, blk), jnp.float32)] * 2 + [pltpu.SemaphoreType.DMA((2, most))]
    band = jax.ShapeDtypeStruct((blk, JB * blk), jnp.float32)
    late, c_early, b_late = pl.pallas_call(
        functools.partial(
            early_kernel, chunks, n_a, [[first for first, _ in held] for held in b_sources], slots, a_at, b_at
        ),
        out_shape=[
            jax.ShapeDtypeStruct((1 + 3 * most,), jnp.int32),
            band,
            jax.ShapeDtypeStruct((most * blk, blk), jnp.float32),
        ],
        in_specs=[ANY] * (n_a * len(first) + len(b_flat)),
        out_specs=[SMEM, VMEM, ANY],
        scratch_shapes=[
            pltpu.VMEM((tails, TAIL, blk), jnp.float32),
            pltpu.VMEM((max(8, STEPS * group), blk), jnp.int32),
            pltpu.SMEM((max(8, STEPS * group), blk), jnp.int32),
            pltpu.SMEM((most,), jnp.int32),
            *buffers,
            pltpu.SemaphoreType.DMA((most,)),
            pltpu.SemaphoreType.DMA((tails + 1,)),
        ],
        compiler_params=pltpu.CompilerParams(vmem_limit_bytes=24 * MIB),
        cost_estimate=pl.CostEstimate(flops=6 * 8 * blk**3, bytes_accessed=8 * MIB, transcendentals=0),
        name="early",
    )(*[x for arrays in a_sources for x in arrays[: len(first)]], *b_flat)
    return late, c_early, b_late


def add_late(late, c_early, b_late, a_last):
    blk = a_last[0].shape[1]
    most = (late.shape[0] - 1) // 3
    buffers = [pltpu.VMEM((most, blk, blk), jnp.float32)] * 2 + [pltpu.SemaphoreType.DMA((2, most))]
    return pl.pallas_call(
        functools.partial(late_kernel, len(a_last)),
        out_shape=jax.ShapeDtypeStruct(c_early.shape, c_early.dtype),
        in_specs=[SMEM, VMEM, ANY] + [ANY] * len(a_last),
        out_specs=VMEM,
        scratch_shapes=buffers,
        compiler_params=pltpu.CompilerParams(vmem_limit_bytes=24 * MIB),
        cost_estimate=pl.CostEstimate(flops=6 * 2 * blk**3, bytes_accessed=2 * MIB, transcendentals=0),
        name="late",
    )(late, c_early, b_late, *a_last)


def collect_kernel(n, at, half, *refs):
    sources, outs, sems = refs[:n], refs[n : n + 2 * STEPS], refs[n + 2 * STEPS]
    rows = sources[0].shape[0]
    for i, out in enumerate(outs):
        part = pl.ds(half, rows - half) if i % 2 else pl.ds(0, half)
        start_from(sources, at(i // 2), part, out, sems.at[i])
    for i, out in enumerate(outs):
        pltpu.make_async_copy(out, out, sems.at[i]).wait()


def collect(sources, at, half):
    rows, blk = sources[0].shape
    sizes = [half, rows - half] * STEPS
    return pl.pallas_call(
        functools.partial(collect_kernel, len(sources), at, half),
        out_shape=[jax.ShapeDtypeStruct((size, blk), sources[0].dtype) for size in sizes],
        in_specs=[ANY] * len(sources),
        out_specs=[ANY] * len(sizes),
        scratch_shapes=[pltpu.SemaphoreType.DMA((len(sizes),))],
        cost_estimate=pl.CostEstimate(flops=0, bytes_accessed=4 * MIB, transcendentals=0),
        name="collect",
    )(*sources)


def as_rows(x):
    return x.reshape(-1, x.shape[-1])


def gathered(a_vals, a_code, b_vals, b_code, panels, group):
    chunks = [(0, a_vals.shape[0])]
    _, a_own, b_own = prepare(chunks, a_code, b_code, panels, as_rows(a_vals), as_rows(b_vals))
    a_all = lax.all_gather(a_own, "col")
    b_all = lax.all_gather(b_own, "row")
    a_sources, b_sources = [], []
    for step in range(STEPS):
        a_sources.append([lax.dynamic_index_in_dim(a_all, panels[step], 0, keepdims=False)])
        for g in range(group):
            b_sources.append([(0, lax.dynamic_index_in_dim(b_all, panels[step] * group + g, 0, keepdims=False))])
    slots = (group, b_vals.shape[0])
    early = add_early(chunks, a_sources, b_sources, slots, lambda s: s, lambda s, g: s * group + g)
    return add_late(*early, [arrays[-1] for arrays in a_sources])


CHUNKS = [(0, 8), (8, 16)]
ROUTES = {
    (0, 1): [(None, ((0, 1), (1, 2))), (0, ((1, 2), (2, 3))), (1, ((2, 3), (3, 0)))],
    (0, 2): [(None, ((0, 1), (2, 3))), (0, ((1, 2), (3, 1))), (1, ((1, 0), (2, 3)))],
    (0, 3): [(None, ((0, 1), (3, 2))), (0, ((1, 2), (2, 1))), (1, ((2, 3), (1, 0)))],
    (1, 2): [(None, ((1, 0), (2, 3))), (None, ((1, 2), (2, 1))), (1, ((1, 0), (2, 3)))],
}
WRITTEN = ("0a", "0b", "x", "y", "g", "1a", "1b", "2a", "2b", "s", "t", "u", "v")
WAITS = {
    (0, 1): {"g": ("x", "y"), "v": ("2a",)},
    (0, 2): {"g": ("x", "y")},
    (0, 3): {"g": ("x", "y")},
    (1, 2): {"g": ("x", "y"), "2b": ("0b",), "2a": ("0a",)},
}


def route_of(roots, n):
    mirror = roots not in ROUTES
    key = tuple(sorted(n - 1 - p for p in roots)) if mirror else roots
    steps, brings = [], []
    for source, pairs in ROUTES[key]:
        if mirror:
            pairs = tuple((n - 1 - x, n - 1 - y) for x, y in pairs)
        steps.append((source, pairs))
        brings.append({y: x if source is None else brings[source][x] for x, y in pairs})
    return steps, brings, WAITS[key]


def pick(values, index):
    out = jnp.int32(values[0])
    for i, value in enumerate(values[1:], 1):
        out = jnp.where(index == i, jnp.int32(value), out)
    return out


def after(x, *earlier):
    return lax.optimization_barrier((x, *earlier))[0]


def pair_branch(roots, n, slots, pieces, b_own):
    group, sb = slots
    half = sb // 2
    blk = b_own.shape[1]
    parts = "abcdefgh"[: len(pieces)]

    def exchange(bit):
        return "row", [(r, r ^ bit) for r in range(n * group)]

    def from_chip(s):
        return (lax.axis_index("row") >> 1) ^ roots[s]

    moves = {name: ("o", *exchange(q * group)) for q, name in enumerate("xyg", 1)}
    moves.update({name: ("own " + name, *exchange(1)) for name in "stuv"})
    held = dict(zip(parts, pieces), o=b_own)
    a_names = [list(parts)]
    a_table = [[0] * n for _ in roots]
    steps, brings, waits = route_of(roots, n)
    for number, (source, pairs) in enumerate(steps):
        for at, p in brings[number].items():
            a_table[roots.index(p)][at] = len(a_names)
        for part in parts:
            moves[f"{number}{part}"] = (part if source is None else f"{source}{part}", "col", pairs)
        a_names.append([f"{number}{part}" for part in parts])

    while moves:
        for name in [name for name in WRITTEN if name in moves]:
            source, axis, pairs = moves[name]
            if name == "s" and source not in held and all(e in held for e in ("x", "y", "g", *waits.get("p", ()))):
                last = held["g"]
                if "p" in waits:
                    last = lax.optimization_barrier((last, *[held[e] for e in waits["p"]]))[0]
                halves = collect([held["o"], held["x"], held["y"], last], from_chip, half * blk)
                held.update({"own " + name: x for name, x in zip("stuv", halves)})
            if all(e in held for e in (source, *waits.get(name, ()))):
                x = held[source]
                if name in waits:
                    x = lax.optimization_barrier((x, *[held[e] for e in waits[name]]))[0]
                held[name] = lax.ppermute(x, axis, pairs)
                del moves[name]

    a_sources = [[held[name] for name in names] for names in a_names]
    b_sources = [[(0, held[name])] for name in "oxyg"]
    b_sources += [[(0, held[name]), (half, held[other])] for name, other in ("st", "uv")]

    def a_at(s):
        return pick(a_table[s], lax.axis_index("col"))

    def b_at(s, g):
        return jnp.where((lax.axis_index("row") & 1) == g, from_chip(s), n + s)

    early = add_early(CHUNKS, a_sources, b_sources, slots, a_at, b_at)
    return early, [arrays[-1] for arrays in a_sources[1:]]


def shards(a_vals, a_code, b_vals, b_code, panels):
    n = lax.axis_size("col")
    group = lax.axis_size("row") // n
    if group != 2 or n != 4:
        return gathered(a_vals, a_code, b_vals, b_code, panels, group)
    which, *pieces, b_own = prepare(CHUNKS, a_code, b_code, panels, as_rows(a_vals), as_rows(b_vals))
    slots = (group, b_vals.shape[0])
    branches = [functools.partial(pair_branch, pair, n, slots) for pair in itertools.combinations(range(n), 2)]
    early, a_last = lax.switch(which[0], branches, pieces, b_own)
    return add_late(*early, [pieces[-1], *a_last])


def solution(mesh):
    return jax.shard_map(
        shards,
        mesh=mesh,
        in_specs=(
            P("row", "col", None),
            P("row", "col"),
            P("row", "col", None),
            P("row", "col"),
            P(),
        ),
        out_specs=P("row", "col"),
        check_vma=False,
    )
```

```python
import functools
import itertools

import jax
import jax.numpy as jnp
from jax import lax
from jax.experimental import pallas as pl
from jax.experimental.pallas import tpu as pltpu
from jax.sharding import PartitionSpec as P

KPB = 64
STEPS = 2
JB = 8
TAIL = 8
MIB = 2**20

SMEM = pl.BlockSpec(memory_space=pltpu.SMEM)
VMEM = pl.BlockSpec(memory_space=pltpu.VMEM)
ANY = pl.BlockSpec(memory_space=pl.ANY)


def rows_of(slot, blk):
    return pl.ds(pl.multiple_of(slot * blk, blk), blk)


def prepare_kernel(chunks, a_code, b_code, panels, a_rows, b_rows, which, *refs):
    outs, (a_buf, b_buf, tails, sems) = refs[: len(chunks) + 1], refs[len(chunks) + 1 :]
    blk = a_rows.shape[1]
    loads = [(a_rows, a_buf, pl.ds(f * blk, (e - f) * blk)) for f, e in chunks] + [(b_rows, b_buf, pl.ds(0, b_rows.shape[0]))]
    loads = [pltpu.make_async_copy(rows.at[part], buf.at[part], sems.at[i]) for i, (rows, buf, part) in enumerate(loads)]
    for copy in loads:
        copy.start()
    stores = []
    tails[...] = jnp.zeros_like(tails)
    for i, (code, into) in enumerate(((a_code, outs[0]), (b_code, outs[-1]))):
        tails[i, 0:1, 0 : code.shape[1]] = code[...].astype(jnp.float32)
        last = into.shape[0] - TAIL
        stores.append(pltpu.make_async_copy(tails.at[i], into.at[pl.ds(last, TAIL)], sems.at[2 * len(loads) + i]))
        stores[-1].start()
    lo = jnp.minimum(panels[0], panels[1])
    hi = jnp.maximum(panels[0], panels[1])
    which[0] = jnp.where(lo == 0, 0, lo + 1) + hi - 1
    parts = [a_buf.at[pl.ds(f * blk, (e - f) * blk)] for f, e in chunks] + [b_buf]
    for i, (load, part, out) in enumerate(zip(loads, parts, outs)):
        load.wait()
        stores.append(pltpu.make_async_copy(part, out.at[pl.ds(0, part.shape[0])], sems.at[len(loads) + i]))
        stores[-1].start()
    for copy in stores:
        copy.wait()


def prepare(chunks, a_code, b_code, panels, a_rows, b_rows):
    blk = a_rows.shape[1]
    sizes = [(e - f) * blk for f, e in chunks]
    sizes[0] += TAIL
    sizes.append(b_rows.shape[0] + TAIL)
    return pl.pallas_call(
        functools.partial(prepare_kernel, chunks),
        out_shape=[jax.ShapeDtypeStruct((1,), jnp.int32)] + [jax.ShapeDtypeStruct((x, blk), jnp.float32) for x in sizes],
        in_specs=[VMEM, VMEM, SMEM, ANY, ANY],
        out_specs=[SMEM] + [ANY] * len(sizes),
        scratch_shapes=[
            pltpu.VMEM(a_rows.shape, jnp.float32),
            pltpu.VMEM(b_rows.shape, jnp.float32),
            pltpu.VMEM((2, TAIL, blk), jnp.float32),
            pltpu.SemaphoreType.DMA((2 * len(sizes) + 2,)),
        ],
        compiler_params=pltpu.CompilerParams(vmem_limit_bytes=8 * MIB),
        name="prepare",
    )(a_code.T, b_code.T, panels, a_rows, b_rows)


def split(x):
    high = x.astype(jnp.bfloat16)
    low = (x - high.astype(jnp.float32)).astype(jnp.bfloat16)
    return high, low


def product(a, b):
    a_high, a_low = split(a)
    b_high, b_low = split(b)
    left = jnp.concatenate([a_high, a_high, a_low], axis=1)
    right = jnp.concatenate([b_high, b_low, b_high], axis=0)
    return jnp.dot(left, right, preferred_element_type=jnp.float32)


def add_products(count, column, a_buf, b_buf, sems, c_ref):
    blk = a_buf.shape[1]

    def one(m, carry):
        for which, buf in enumerate((a_buf, b_buf)):
            pltpu.make_async_copy(buf.at[m], buf.at[m], sems.at[which, m]).wait()
        c_ref[:, rows_of(column(m), blk)] += product(a_buf[m], b_buf[m])
        return carry

    lax.fori_loop(0, count, one, 0)


def start_from(refs, source, rows, into, sem):
    for i, ref in enumerate(refs):

        @pl.when(source == i)
        def _():
            pltpu.make_async_copy(ref.at[rows], into, sem).start()


def early_kernel(chunks, n_a, b_parts, slots, a_at, b_at, *refs):
    group, sb = slots
    parts = max(1, len(chunks) - 1)
    n_b = sum(len(firsts) for firsts in b_parts)
    a_refs = [refs[i * parts : (i + 1) * parts] for i in range(n_a)]
    flat = iter(refs[n_a * parts : n_a * parts + n_b])
    b_refs = [[(first, next(flat)) for first in firsts] for firsts in b_parts]
    late, c_ref, b_late, tails, found, found_s, plan, a_buf, b_buf, sems, late_sems, tail_sems = refs[n_a * parts + n_b :]
    sa = chunks[-1][1]
    last_first = chunks[-1][0]
    blk = a_buf.shape[1]
    k_rows = KPB // group
    sources = [[a_at(s)] + [b_at(s, g) for g in range(group)] for s in range(STEPS)]

    def tail(s, i):
        return s * (1 + group) + i

    for s in range(STEPS):
        for i, source in enumerate(sources[s]):
            for j, holder in enumerate([held[-1][1] for held in b_refs] if i else [arrays[0] for arrays in a_refs]):

                @pl.when(source == j)
                def _():
                    rows = pl.ds(holder.shape[0] - TAIL, TAIL)
                    pltpu.make_async_copy(holder.at[rows], tails.at[tail(s, i)], tail_sems.at[tail(s, i)]).start()

    c_ref[...] = jnp.zeros_like(c_ref)
    found[...] = jnp.full_like(found, -1)
    for i in range(STEPS * (1 + group)):
        pltpu.make_async_copy(tails.at[i], tails.at[i], tail_sems.at[i]).wait()

    for s in range(STEPS):
        a_codes = tails[tail(s, 0), 0:1, :].astype(jnp.int32)
        for g in range(group):
            b_codes = tails[tail(s, 1 + g), 0:1, :].astype(jnp.int32)
            used = (b_codes >= 0) & (lax.broadcasted_iota(jnp.int32, b_codes.shape, 1) < sb)
            k = jnp.where(used, g * k_rows + b_codes // JB, -2)
            hit = jnp.full_like(k, -1)
            for slot in range(sa):
                hit = jnp.where(a_codes[:, slot : slot + 1] == k, slot, hit)
            found[s * group + g : s * group + g + 1, :] = jnp.where(hit >= 0, hit * JB + b_codes % JB, -1)
    copy = pltpu.make_async_copy(found, found_s, tail_sems.at[STEPS * (1 + group)])
    copy.start()
    copy.wait()

    def start_b(source, slot, into, sem):
        for i, held in enumerate(b_refs):

            @pl.when(source == i)
            def _():
                for j, (first, ref) in enumerate(held):
                    end = held[j + 1][0] if j + 1 < len(held) else sb

                    @pl.when((slot >= first) & (slot < end))
                    def _():
                        pltpu.make_async_copy(ref.at[rows_of(slot - first, blk)], into, sem).start()

    counts = (jnp.int32(0), jnp.int32(0))
    for s in range(STEPS):
        for g in range(group):

            def one(slot, counts):
                n_early, n_late = counts
                hit = found_s[s * group + g, slot]
                a_slot = hit // JB
                early = (hit >= 0) & (a_slot < last_first)
                is_late = a_slot >= last_first

                @pl.when(early)
                def _():
                    plan[n_early] = hit % JB
                    for i, arrays in enumerate(a_refs):

                        @pl.when(sources[s][0] == i)
                        def _():
                            for (f, e), ref in zip(chunks[:-1], arrays):

                                @pl.when((a_slot >= f) & (a_slot < e))
                                def _():
                                    rows = rows_of(a_slot - f, blk)
                                    pltpu.make_async_copy(ref.at[rows], a_buf.at[n_early], sems.at[0, n_early]).start()

                    start_b(sources[s][1 + g], slot, b_buf.at[n_early], sems.at[1, n_early])

                @pl.when(is_late)
                def _():
                    late[1 + 3 * n_late] = sources[s][0]
                    late[2 + 3 * n_late] = a_slot - last_first
                    late[3 + 3 * n_late] = hit % JB
                    into = b_late.at[rows_of(n_late, blk)]
                    start_b(sources[s][1 + g], slot, into, late_sems.at[n_late])

                return n_early + early.astype(jnp.int32), n_late + is_late.astype(jnp.int32)

            counts = lax.fori_loop(0, sb, one, counts)
    late[0] = counts[1]
    add_products(counts[0], lambda m: plan[m], a_buf, b_buf, sems, c_ref)

    def wait(m, carry):
        into = b_late.at[rows_of(m, blk)]
        pltpu.make_async_copy(into, into, late_sems.at[m]).wait()
        return carry

    lax.fori_loop(0, counts[1], wait, 0)


def late_kernel(n_a, late, c_in, b_late, *refs):
    a_refs, (c_ref, a_buf, b_buf, sems) = refs[:n_a], refs[n_a:]
    blk = a_buf.shape[1]

    def fetch(m, carry):
        start_from(a_refs, late[1 + 3 * m], rows_of(late[2 + 3 * m], blk), a_buf.at[m], sems.at[0, m])
        pltpu.make_async_copy(b_late.at[rows_of(m, blk)], b_buf.at[m], sems.at[1, m]).start()
        return carry

    lax.fori_loop(0, late[0], fetch, 0)
    c_ref[...] = c_in[...]
    add_products(late[0], lambda m: late[3 + 3 * m], a_buf, b_buf, sems, c_ref)


def add_early(chunks, a_sources, b_sources, slots, a_at, b_at):
    group, sb = slots
    b_flat = [array for held in b_sources for _, array in held]
    blk = b_flat[0].shape[1]
    most = STEPS * group * sb
    tails = STEPS * (1 + group)
    n_a = len(a_sources)
    first = chunks[:-1] or chunks
    buffers = [pltpu.VMEM((most, blk, blk), jnp.float32)] * 2 + [pltpu.SemaphoreType.DMA((2, most))]
    band = jax.ShapeDtypeStruct((blk, JB * blk), jnp.float32)
    late, c_early, b_late = pl.pallas_call(
        functools.partial(
            early_kernel, chunks, n_a, [[first for first, _ in held] for held in b_sources], slots, a_at, b_at
        ),
        out_shape=[
            jax.ShapeDtypeStruct((1 + 3 * most,), jnp.int32),
            band,
            jax.ShapeDtypeStruct((most * blk, blk), jnp.float32),
        ],
        in_specs=[ANY] * (n_a * len(first) + len(b_flat)),
        out_specs=[SMEM, VMEM, ANY],
        scratch_shapes=[
            pltpu.VMEM((tails, TAIL, blk), jnp.float32),
            pltpu.VMEM((max(8, STEPS * group), blk), jnp.int32),
            pltpu.SMEM((max(8, STEPS * group), blk), jnp.int32),
            pltpu.SMEM((most,), jnp.int32),
            *buffers,
            pltpu.SemaphoreType.DMA((most,)),
            pltpu.SemaphoreType.DMA((tails + 1,)),
        ],
        compiler_params=pltpu.CompilerParams(vmem_limit_bytes=12 * MIB),
        cost_estimate=pl.CostEstimate(flops=6 * 8 * blk**3, bytes_accessed=8 * MIB, transcendentals=0),
        name="early",
    )(*[x for arrays in a_sources for x in arrays[: len(first)]], *b_flat)
    return late, c_early, b_late


def add_late(late, c_early, b_late, a_last):
    blk = a_last[0].shape[1]
    most = (late.shape[0] - 1) // 3
    buffers = [pltpu.VMEM((most, blk, blk), jnp.float32)] * 2 + [pltpu.SemaphoreType.DMA((2, most))]
    return pl.pallas_call(
        functools.partial(late_kernel, len(a_last)),
        out_shape=jax.ShapeDtypeStruct(c_early.shape, c_early.dtype),
        in_specs=[SMEM, VMEM, ANY] + [ANY] * len(a_last),
        out_specs=VMEM,
        scratch_shapes=buffers,
        compiler_params=pltpu.CompilerParams(vmem_limit_bytes=12 * MIB),
        cost_estimate=pl.CostEstimate(flops=6 * 2 * blk**3, bytes_accessed=2 * MIB, transcendentals=0),
        name="late",
    )(late, c_early, b_late, *a_last)


def collect_kernel(n, at, half, *refs):
    sources, outs, (buf, sems) = refs[:n], refs[n : n + 2 * STEPS], refs[n + 2 * STEPS :]
    rows = sources[0].shape[0]
    parts = [pl.ds(half, rows - half) if i % 2 else pl.ds(0, half) for i in range(len(outs))]
    for i, part in enumerate(parts):
        start_from(sources, at(i // 2), part, buf.at[i // 2, part], sems.at[0, i])
    stores = []
    for i, (part, out) in enumerate(zip(parts, outs)):
        held = buf.at[i // 2, part]
        pltpu.make_async_copy(held, held, sems.at[0, i]).wait()
        stores.append(pltpu.make_async_copy(held, out, sems.at[1, i]))
        stores[-1].start()
    for copy in stores:
        copy.wait()


def collect(sources, at, half):
    rows, blk = sources[0].shape
    sizes = [half, rows - half] * STEPS
    return pl.pallas_call(
        functools.partial(collect_kernel, len(sources), at, half),
        out_shape=[jax.ShapeDtypeStruct((size, blk), sources[0].dtype) for size in sizes],
        in_specs=[ANY] * len(sources),
        out_specs=[ANY] * len(sizes),
        scratch_shapes=[pltpu.VMEM((STEPS, rows, blk), sources[0].dtype), pltpu.SemaphoreType.DMA((2, len(sizes)))],
        compiler_params=pltpu.CompilerParams(vmem_limit_bytes=8 * MIB),
        cost_estimate=pl.CostEstimate(flops=0, bytes_accessed=4 * MIB, transcendentals=0),
        name="collect",
    )(*sources)


def as_rows(x):
    return x.reshape(-1, x.shape[-1])


def gathered(a_vals, a_code, b_vals, b_code, panels, group):
    chunks = [(0, a_vals.shape[0])]
    _, a_own, b_own = prepare(chunks, a_code, b_code, panels, as_rows(a_vals), as_rows(b_vals))
    a_all = lax.all_gather(a_own, "col")
    b_all = lax.all_gather(b_own, "row")
    a_sources, b_sources = [], []
    for step in range(STEPS):
        a_sources.append([lax.dynamic_index_in_dim(a_all, panels[step], 0, keepdims=False)])
        for g in range(group):
            b_sources.append([(0, lax.dynamic_index_in_dim(b_all, panels[step] * group + g, 0, keepdims=False))])
    slots = (group, b_vals.shape[0])
    early = add_early(chunks, a_sources, b_sources, slots, lambda s: s, lambda s, g: s * group + g)
    return add_late(*early, [arrays[-1] for arrays in a_sources])


CHUNKS = [(0, 8), (8, 16)]
ROUTES = {
    (0, 1): [(None, ((0, 1), (1, 2))), (0, ((1, 2), (2, 3))), (1, ((2, 3), (3, 0)))],
    (0, 2): [(None, ((0, 1), (2, 3))), (0, ((1, 2), (3, 1))), (1, ((1, 0), (2, 3)))],
    (0, 3): [(None, ((0, 1), (3, 2))), (0, ((1, 2), (2, 1))), (1, ((2, 3), (1, 0)))],
    (1, 2): [(None, ((1, 0), (2, 3))), (None, ((1, 2), (2, 1))), (1, ((1, 0), (2, 3)))],
}
WRITTEN = ("0a", "0b", "x", "y", "g", "1a", "1b", "2a", "2b", "s", "t", "u", "v")
WAITS = {
    (0, 1): {"g": ("x", "y"), "v": ("2a",)},
    (0, 2): {"g": ("x", "y")},
    (0, 3): {"g": ("x", "y")},
    (1, 2): {"g": ("x", "y"), "2b": ("0b",), "2a": ("0a",)},
}


def route_of(roots, n):
    mirror = roots not in ROUTES
    key = tuple(sorted(n - 1 - p for p in roots)) if mirror else roots
    steps, brings = [], []
    for source, pairs in ROUTES[key]:
        if mirror:
            pairs = tuple((n - 1 - x, n - 1 - y) for x, y in pairs)
        steps.append((source, pairs))
        brings.append({y: x if source is None else brings[source][x] for x, y in pairs})
    return steps, brings, WAITS[key]


def pick(values, index):
    out = jnp.int32(values[0])
    for i, value in enumerate(values[1:], 1):
        out = jnp.where(index == i, jnp.int32(value), out)
    return out


def after(x, *earlier):
    return lax.optimization_barrier((x, *earlier))[0]


def pair_branch(roots, n, slots, pieces, b_own):
    group, sb = slots
    half = sb // 2
    blk = b_own.shape[1]
    parts = "abcdefgh"[: len(pieces)]

    def exchange(bit):
        return "row", [(r, r ^ bit) for r in range(n * group)]

    def from_chip(s):
        return (lax.axis_index("row") >> 1) ^ roots[s]

    moves = {name: ("o", *exchange(q * group)) for q, name in enumerate("xyg", 1)}
    moves.update({name: ("own " + name, *exchange(1)) for name in "stuv"})
    held = dict(zip(parts, pieces), o=b_own)
    a_names = [list(parts)]
    a_table = [[0] * n for _ in roots]
    steps, brings, waits = route_of(roots, n)
    for number, (source, pairs) in enumerate(steps):
        for at, p in brings[number].items():
            a_table[roots.index(p)][at] = len(a_names)
        for part in parts:
            moves[f"{number}{part}"] = (part if source is None else f"{source}{part}", "col", pairs)
        a_names.append([f"{number}{part}" for part in parts])

    while moves:
        for name in [name for name in WRITTEN if name in moves]:
            source, axis, pairs = moves[name]
            if name == "s" and source not in held and all(e in held for e in ("x", "y", "g", *waits.get("p", ()))):
                last = held["g"]
                if "p" in waits:
                    last = lax.optimization_barrier((last, *[held[e] for e in waits["p"]]))[0]
                halves = collect([held["o"], held["x"], held["y"], last], from_chip, half * blk)
                held.update({"own " + name: x for name, x in zip("stuv", halves)})
            if all(e in held for e in (source, *waits.get(name, ()))):
                x = held[source]
                if name in waits:
                    x = lax.optimization_barrier((x, *[held[e] for e in waits[name]]))[0]
                held[name] = lax.ppermute(x, axis, pairs)
                del moves[name]

    a_sources = [[held[name] for name in names] for names in a_names]
    b_sources = [[(0, held[name])] for name in "oxyg"]
    b_sources += [[(0, held[name]), (half, held[other])] for name, other in ("st", "uv")]

    def a_at(s):
        return pick(a_table[s], lax.axis_index("col"))

    def b_at(s, g):
        return jnp.where((lax.axis_index("row") & 1) == g, from_chip(s), n + s)

    early = add_early(CHUNKS, a_sources, b_sources, slots, a_at, b_at)
    return early, [arrays[-1] for arrays in a_sources[1:]]


def shards(a_vals, a_code, b_vals, b_code, panels):
    n = lax.axis_size("col")
    group = lax.axis_size("row") // n
    if group != 2 or n != 4:
        return gathered(a_vals, a_code, b_vals, b_code, panels, group)
    which, *pieces, b_own = prepare(CHUNKS, a_code, b_code, panels, as_rows(a_vals), as_rows(b_vals))
    slots = (group, b_vals.shape[0])
    branches = [functools.partial(pair_branch, pair, n, slots) for pair in itertools.combinations(range(n), 2)]
    early, a_last = lax.switch(which[0], branches, pieces, b_own)
    return add_late(*early, [pieces[-1], *a_last])


def solution(mesh):
    return jax.shard_map(
        shards,
        mesh=mesh,
        in_specs=(
            P("row", "col", None),
            P("row", "col"),
            P("row", "col", None),
            P("row", "col"),
            P(),
        ),
        out_specs=P("row", "col"),
        check_vma=False,
    )
```

```python
import functools
import itertools

import jax
import jax.numpy as jnp
from jax import lax
from jax.experimental import pallas as pl
from jax.experimental.pallas import tpu as pltpu
from jax.sharding import PartitionSpec as P

KPB = 64
STEPS = 2
JB = 8
TAIL = 8
MIB = 2**20

SMEM = pl.BlockSpec(memory_space=pltpu.SMEM)
VMEM = pl.BlockSpec(memory_space=pltpu.VMEM)
ANY = pl.BlockSpec(memory_space=pl.ANY)


def rows_of(slot, blk):
    return pl.ds(pl.multiple_of(slot * blk, blk), blk)


def prepare_kernel(chunks, a_code, b_code, panels, a_rows, b_rows, which, *refs):
    outs, (a_buf, b_buf, tails, sems) = refs[: len(chunks) + 1], refs[len(chunks) + 1 :]
    blk = a_rows.shape[1]
    loads = [(a_rows, a_buf, pl.ds(f * blk, (e - f) * blk)) for f, e in chunks] + [(b_rows, b_buf, pl.ds(0, b_rows.shape[0]))]
    loads = [pltpu.make_async_copy(rows.at[part], buf.at[part], sems.at[i]) for i, (rows, buf, part) in enumerate(loads)]
    for copy in loads:
        copy.start()
    stores = []
    tails[...] = jnp.zeros_like(tails)
    for i, (code, into) in enumerate(((a_code, outs[0]), (b_code, outs[-1]))):
        tails[i, 0:1, 0 : code.shape[1]] = code[...].astype(jnp.float32)
        last = into.shape[0] - TAIL
        stores.append(pltpu.make_async_copy(tails.at[i], into.at[pl.ds(last, TAIL)], sems.at[2 * len(loads) + i]))
        stores[-1].start()
    lo = jnp.minimum(panels[0], panels[1])
    hi = jnp.maximum(panels[0], panels[1])
    which[0] = jnp.where(lo == 0, 0, lo + 1) + hi - 1
    parts = [a_buf.at[pl.ds(f * blk, (e - f) * blk)] for f, e in chunks] + [b_buf]
    for i, (load, part, out) in enumerate(zip(loads, parts, outs)):
        load.wait()
        stores.append(pltpu.make_async_copy(part, out.at[pl.ds(0, part.shape[0])], sems.at[len(loads) + i]))
        stores[-1].start()
    for copy in stores:
        copy.wait()


def prepare(chunks, a_code, b_code, panels, a_rows, b_rows):
    blk = a_rows.shape[1]
    sizes = [(e - f) * blk for f, e in chunks]
    sizes[0] += TAIL
    sizes.append(b_rows.shape[0] + TAIL)
    return pl.pallas_call(
        functools.partial(prepare_kernel, chunks),
        out_shape=[jax.ShapeDtypeStruct((1,), jnp.int32)] + [jax.ShapeDtypeStruct((x, blk), jnp.float32) for x in sizes],
        in_specs=[VMEM, VMEM, SMEM, ANY, ANY],
        out_specs=[SMEM] + [ANY] * len(sizes),
        scratch_shapes=[
            pltpu.VMEM(a_rows.shape, jnp.float32),
            pltpu.VMEM(b_rows.shape, jnp.float32),
            pltpu.VMEM((2, TAIL, blk), jnp.float32),
            pltpu.SemaphoreType.DMA((2 * len(sizes) + 2,)),
        ],
        name="prepare",
    )(a_code.T, b_code.T, panels, a_rows, b_rows)


def split(x):
    high = x.astype(jnp.bfloat16)
    low = (x - high.astype(jnp.float32)).astype(jnp.bfloat16)
    return high, low


def product(a, b):
    a_high, a_low = split(a)
    b_high, b_low = split(b)
    left = jnp.concatenate([a_high, a_high, a_low], axis=1)
    right = jnp.concatenate([b_high, b_low, b_high], axis=0)
    return jnp.dot(left, right, preferred_element_type=jnp.float32)


def add_products(count, column, a_buf, b_buf, sems, c_ref):
    blk = a_buf.shape[1]

    def wait(m):
        for which, buf in enumerate((a_buf, b_buf)):
            pltpu.make_async_copy(buf.at[m], buf.at[m], sems.at[which, m]).wait()

    def add(m, value):
        c_ref[:, rows_of(column(m), blk)] += value

    def two(i, carry):
        m = 2 * i
        wait(m)
        wait(m + 1)
        first, second = product(a_buf[m], b_buf[m]), product(a_buf[m + 1], b_buf[m + 1])
        add(m, first)
        add(m + 1, second)
        return carry

    lax.fori_loop(0, count // 2, two, 0)

    @pl.when(count % 2 == 1)
    def _():
        wait(count - 1)
        add(count - 1, product(a_buf[count - 1], b_buf[count - 1]))


def start_from(refs, source, rows, into, sem):
    for i, ref in enumerate(refs):

        @pl.when(source == i)
        def _():
            pltpu.make_async_copy(ref.at[rows], into, sem).start()


def early_kernel(chunks, n_a, b_parts, slots, a_at, b_at, *refs):
    group, sb = slots
    parts = max(1, len(chunks) - 1)
    n_b = sum(len(firsts) for firsts in b_parts)
    a_refs = [refs[i * parts : (i + 1) * parts] for i in range(n_a)]
    flat = iter(refs[n_a * parts : n_a * parts + n_b])
    b_refs = [[(first, next(flat)) for first in firsts] for firsts in b_parts]
    late, c_ref, b_late, tails, found, found_s, plan, a_buf, b_buf, sems, late_sems, tail_sems = refs[n_a * parts + n_b :]
    sa = chunks[-1][1]
    last_first = chunks[-1][0]
    blk = a_buf.shape[1]
    k_rows = KPB // group
    sources = [[a_at(s)] + [b_at(s, g) for g in range(group)] for s in range(STEPS)]

    def tail(s, i):
        return s * (1 + group) + i

    for s in range(STEPS):
        for i, source in enumerate(sources[s]):
            for j, holder in enumerate([held[-1][1] for held in b_refs] if i else [arrays[0] for arrays in a_refs]):

                @pl.when(source == j)
                def _():
                    rows = pl.ds(holder.shape[0] - TAIL, TAIL)
                    pltpu.make_async_copy(holder.at[rows], tails.at[tail(s, i)], tail_sems.at[tail(s, i)]).start()

    c_ref[...] = jnp.zeros_like(c_ref)
    found[...] = jnp.full_like(found, -1)
    for i in range(STEPS * (1 + group)):
        pltpu.make_async_copy(tails.at[i], tails.at[i], tail_sems.at[i]).wait()

    for s in range(STEPS):
        a_codes = tails[tail(s, 0), 0:1, :].astype(jnp.int32)
        for g in range(group):
            b_codes = tails[tail(s, 1 + g), 0:1, :].astype(jnp.int32)
            used = (b_codes >= 0) & (lax.broadcasted_iota(jnp.int32, b_codes.shape, 1) < sb)
            k = jnp.where(used, g * k_rows + b_codes // JB, -2)
            hit = jnp.full_like(k, -1)
            for slot in range(sa):
                hit = jnp.where(a_codes[:, slot : slot + 1] == k, slot, hit)
            found[s * group + g : s * group + g + 1, :] = jnp.where(hit >= 0, hit * JB + b_codes % JB, -1)
    copy = pltpu.make_async_copy(found, found_s, tail_sems.at[STEPS * (1 + group)])
    copy.start()
    copy.wait()

    n_early = n_late = jnp.int32(0)
    for row in range(STEPS * group):
        for slot in range(sb):
            hit = found_s[row, slot]
            entry = hit + (row * sb + slot) * sa * JB
            is_late = hit >= last_first * JB
            plan[0, n_early] = entry
            plan[1, n_late] = entry
            n_early += ((hit >= 0) & jnp.logical_not(is_late)).astype(jnp.int32)
            n_late += is_late.astype(jnp.int32)

    def start_b(row, slot, into, sem):
        source = pick([sources[s][1 + g] for s in range(STEPS) for g in range(group)], row)
        for i, held in enumerate(b_refs):

            @pl.when(source == i)
            def _():
                for j, (first, ref) in enumerate(held):
                    end = held[j + 1][0] if j + 1 < len(held) else sb

                    @pl.when((slot >= first) & (slot < end))
                    def _():
                        pltpu.make_async_copy(ref.at[rows_of(slot - first, blk)], into, sem).start()

    def fetch(which, m):
        number, hit = plan[which, m] // (sa * JB), plan[which, m] % (sa * JB)
        row, slot = number // sb, number % sb
        return row, slot, pick([sources[s][0] for s in range(STEPS)], row // group), hit // JB, hit % JB

    def fetch_early(m, carry):
        row, slot, source, a_slot, j = fetch(0, m)
        plan[0, m] = j
        for i, arrays in enumerate(a_refs):
            for (f, e), ref in zip(chunks[:-1], arrays):

                @pl.when((source == i) & (a_slot >= f) & (a_slot < e))
                def _():
                    pltpu.make_async_copy(ref.at[rows_of(a_slot - f, blk)], a_buf.at[m], sems.at[0, m]).start()

        start_b(row, slot, b_buf.at[m], sems.at[1, m])
        return carry

    def fetch_late(m, carry):
        row, slot, source, a_slot, j = fetch(1, m)
        late[1 + 3 * m] = source
        late[2 + 3 * m] = a_slot - last_first
        late[3 + 3 * m] = j
        start_b(row, slot, b_late.at[rows_of(m, blk)], late_sems.at[m])
        return carry

    lax.fori_loop(0, n_early, fetch_early, 0)
    lax.fori_loop(0, n_late, fetch_late, 0)
    counts = (n_early, n_late)
    late[0] = counts[1]
    add_products(counts[0], lambda m: plan[0, m], a_buf, b_buf, sems, c_ref)

    def wait(m, carry):
        into = b_late.at[rows_of(m, blk)]
        pltpu.make_async_copy(into, into, late_sems.at[m]).wait()
        return carry

    lax.fori_loop(0, counts[1], wait, 0)


def late_kernel(n_a, late, c_in, b_late, *refs):
    a_refs, (c_ref, a_buf, b_buf, sems) = refs[:n_a], refs[n_a:]
    blk = a_buf.shape[1]

    def fetch(m, carry):
        start_from(a_refs, late[1 + 3 * m], rows_of(late[2 + 3 * m], blk), a_buf.at[m], sems.at[0, m])
        pltpu.make_async_copy(b_late.at[rows_of(m, blk)], b_buf.at[m], sems.at[1, m]).start()
        return carry

    lax.fori_loop(0, late[0], fetch, 0)
    c_ref[...] = c_in[...]
    add_products(late[0], lambda m: late[3 + 3 * m], a_buf, b_buf, sems, c_ref)


def add_early(chunks, a_sources, b_sources, slots, a_at, b_at):
    group, sb = slots
    b_flat = [array for held in b_sources for _, array in held]
    blk = b_flat[0].shape[1]
    most = STEPS * group * sb
    tails = STEPS * (1 + group)
    n_a = len(a_sources)
    first = chunks[:-1] or chunks
    buffers = [pltpu.VMEM((most, blk, blk), jnp.float32)] * 2 + [pltpu.SemaphoreType.DMA((2, most))]
    band = jax.ShapeDtypeStruct((blk, JB * blk), jnp.float32)
    late, c_early, b_late = pl.pallas_call(
        functools.partial(
            early_kernel, chunks, n_a, [[first for first, _ in held] for held in b_sources], slots, a_at, b_at
        ),
        out_shape=[
            jax.ShapeDtypeStruct((1 + 3 * most,), jnp.int32),
            band,
            jax.ShapeDtypeStruct((most * blk, blk), jnp.float32),
        ],
        in_specs=[ANY] * (n_a * len(first) + len(b_flat)),
        out_specs=[SMEM, VMEM, ANY],
        scratch_shapes=[
            pltpu.VMEM((tails, TAIL, blk), jnp.float32),
            pltpu.VMEM((max(8, STEPS * group), blk), jnp.int32),
            pltpu.SMEM((max(8, STEPS * group), blk), jnp.int32),
            pltpu.SMEM((2, most + 1), jnp.int32),
            *buffers,
            pltpu.SemaphoreType.DMA((most,)),
            pltpu.SemaphoreType.DMA((tails + 1,)),
        ],
        compiler_params=pltpu.CompilerParams(vmem_limit_bytes=12 * MIB),
        cost_estimate=pl.CostEstimate(flops=6 * 8 * blk**3, bytes_accessed=8 * MIB, transcendentals=0),
        name="early",
    )(*[x for arrays in a_sources for x in arrays[: len(first)]], *b_flat)
    return late, c_early, b_late


def add_late(late, c_early, b_late, a_last):
    blk = a_last[0].shape[1]
    most = (late.shape[0] - 1) // 3
    buffers = [pltpu.VMEM((most, blk, blk), jnp.float32)] * 2 + [pltpu.SemaphoreType.DMA((2, most))]
    return pl.pallas_call(
        functools.partial(late_kernel, len(a_last)),
        out_shape=jax.ShapeDtypeStruct(c_early.shape, c_early.dtype),
        in_specs=[SMEM, VMEM, ANY] + [ANY] * len(a_last),
        out_specs=VMEM,
        scratch_shapes=buffers,
        compiler_params=pltpu.CompilerParams(vmem_limit_bytes=12 * MIB),
        cost_estimate=pl.CostEstimate(flops=6 * 2 * blk**3, bytes_accessed=2 * MIB, transcendentals=0),
        name="late",
    )(late, c_early, b_late, *a_last)


def collect_kernel(n, at, half, *refs):
    sources, outs, (buf, sems) = refs[:n], refs[n : n + 2 * STEPS], refs[n + 2 * STEPS :]
    rows = sources[0].shape[0]
    parts = [pl.ds(half, rows - half) if i % 2 else pl.ds(0, half) for i in range(len(outs))]
    for i, part in enumerate(parts):
        start_from(sources, at(i // 2), part, buf.at[i // 2, part], sems.at[0, i])
    stores = []
    for i, (part, out) in enumerate(zip(parts, outs)):
        held = buf.at[i // 2, part]
        pltpu.make_async_copy(held, held, sems.at[0, i]).wait()
        stores.append(pltpu.make_async_copy(held, out, sems.at[1, i]))
        stores[-1].start()
    for copy in stores:
        copy.wait()


def collect(sources, at, half):
    rows, blk = sources[0].shape
    sizes = [half, rows - half] * STEPS
    return pl.pallas_call(
        functools.partial(collect_kernel, len(sources), at, half),
        out_shape=[jax.ShapeDtypeStruct((size, blk), sources[0].dtype) for size in sizes],
        in_specs=[ANY] * len(sources),
        out_specs=[ANY] * len(sizes),
        scratch_shapes=[pltpu.VMEM((STEPS, rows, blk), sources[0].dtype), pltpu.SemaphoreType.DMA((2, len(sizes)))],
        compiler_params=pltpu.CompilerParams(vmem_limit_bytes=8 * MIB),
        cost_estimate=pl.CostEstimate(flops=0, bytes_accessed=4 * MIB, transcendentals=0),
        name="collect",
    )(*sources)


def as_rows(x):
    return x.reshape(-1, x.shape[-1])


def gathered(a_vals, a_code, b_vals, b_code, panels, group):
    chunks = [(0, a_vals.shape[0])]
    _, a_own, b_own = prepare(chunks, a_code, b_code, panels, as_rows(a_vals), as_rows(b_vals))
    a_all = lax.all_gather(a_own, "col")
    b_all = lax.all_gather(b_own, "row")
    a_sources, b_sources = [], []
    for step in range(STEPS):
        a_sources.append([lax.dynamic_index_in_dim(a_all, panels[step], 0, keepdims=False)])
        for g in range(group):
            b_sources.append([(0, lax.dynamic_index_in_dim(b_all, panels[step] * group + g, 0, keepdims=False))])
    slots = (group, b_vals.shape[0])
    early = add_early(chunks, a_sources, b_sources, slots, lambda s: s, lambda s, g: s * group + g)
    return add_late(*early, [arrays[-1] for arrays in a_sources])


CHUNKS = [(0, 8), (8, 16)]
ROUTES = {
    (0, 1): [(None, ((0, 1), (1, 2))), (0, ((1, 2), (2, 3))), (1, ((2, 3), (3, 0)))],
    (0, 2): [(None, ((0, 1), (2, 3))), (0, ((1, 2), (3, 1))), (1, ((1, 0), (2, 3)))],
    (0, 3): [(None, ((0, 1), (3, 2))), (0, ((1, 2), (2, 1))), (1, ((2, 3), (1, 0)))],
    (1, 2): [(None, ((1, 0), (2, 3))), (None, ((1, 2), (2, 1))), (1, ((1, 0), (2, 3)))],
}
WRITTEN = ("0a", "0b", "x", "y", "g", "1a", "1b", "2a", "2b", "s", "t", "u", "v")
WAITS = {
    (0, 1): {"g": ("x", "y"), "v": ("2a",)},
    (0, 2): {"g": ("x", "y")},
    (0, 3): {"g": ("x", "y")},
    (1, 2): {"g": ("x", "y"), "0b": ("1b",), "2b": ("0b",), "2a": ("0a",)},
}


def route_of(roots, n):
    mirror = roots not in ROUTES
    key = tuple(sorted(n - 1 - p for p in roots)) if mirror else roots
    steps, brings = [], []
    for source, pairs in ROUTES[key]:
        if mirror:
            pairs = tuple((n - 1 - x, n - 1 - y) for x, y in pairs)
        steps.append((source, pairs))
        brings.append({y: x if source is None else brings[source][x] for x, y in pairs})
    return steps, brings, WAITS[key]


def pick(values, index):
    out = jnp.asarray(values[0], jnp.int32)
    for i, value in enumerate(values[1:], 1):
        out = jnp.where(index == i, jnp.asarray(value, jnp.int32), out)
    return out


def pair_branch(roots, n, slots, pieces, b_own):
    group, sb = slots
    half = sb // 2
    blk = b_own.shape[1]
    parts = "abcdefgh"[: len(pieces)]

    def exchange(bit):
        return "row", [(r, r ^ bit) for r in range(n * group)]

    def from_chip(s):
        return (lax.axis_index("row") >> 1) ^ roots[s]

    moves = {name: ("o", *exchange(q * group)) for q, name in enumerate("xyg", 1)}
    moves.update({name: ("own " + name, *exchange(1)) for name in "stuv"})
    held = dict(zip(parts, pieces), o=b_own)
    a_names = [list(parts)]
    a_table = [[0] * n for _ in roots]
    steps, brings, waits = route_of(roots, n)
    for number, (source, pairs) in enumerate(steps):
        for at, p in brings[number].items():
            a_table[roots.index(p)][at] = len(a_names)
        for part in parts:
            moves[f"{number}{part}"] = (part if source is None else f"{source}{part}", "col", pairs)
        a_names.append([f"{number}{part}" for part in parts])

    while moves:
        for name in [name for name in WRITTEN if name in moves]:
            source, axis, pairs = moves[name]
            if name == "s" and source not in held and all(e in held for e in ("x", "y", "g", *waits.get("p", ()))):
                last = held["g"]
                if "p" in waits:
                    last = lax.optimization_barrier((last, *[held[e] for e in waits["p"]]))[0]
                halves = collect([held["o"], held["x"], held["y"], last], from_chip, half * blk)
                held.update({"own " + name: x for name, x in zip("stuv", halves)})
            if all(e in held for e in (source, *waits.get(name, ()))):
                x = held[source]
                if name in waits:
                    x = lax.optimization_barrier((x, *[held[e] for e in waits[name]]))[0]
                held[name] = lax.ppermute(x, axis, pairs)
                del moves[name]

    a_sources = [[held[name] for name in names] for names in a_names]
    b_sources = [[(0, held[name])] for name in "oxyg"]
    b_sources += [[(0, held[name]), (half, held[other])] for name, other in ("st", "uv")]

    def a_at(s):
        return pick(a_table[s], lax.axis_index("col"))

    def b_at(s, g):
        return jnp.where((lax.axis_index("row") & 1) == g, from_chip(s), n + s)

    early = add_early(CHUNKS, a_sources, b_sources, slots, a_at, b_at)
    return early, [arrays[-1] for arrays in a_sources[1:]]


def shards(a_vals, a_code, b_vals, b_code, panels):
    n = lax.axis_size("col")
    group = lax.axis_size("row") // n
    if group != 2 or n != 4:
        return gathered(a_vals, a_code, b_vals, b_code, panels, group)
    which, *pieces, b_own = prepare(CHUNKS, a_code, b_code, panels, as_rows(a_vals), as_rows(b_vals))
    slots = (group, b_vals.shape[0])
    branches = [functools.partial(pair_branch, pair, n, slots) for pair in itertools.combinations(range(n), 2)]
    early, a_last = lax.switch(which[0], branches, pieces, b_own)
    return add_late(*early, [pieces[-1], *a_last])


def solution(mesh):
    return jax.shard_map(
        shards,
        mesh=mesh,
        in_specs=(
            P("row", "col", None),
            P("row", "col"),
            P("row", "col", None),
            P("row", "col"),
            P(),
        ),
        out_specs=P("row", "col"),
        check_vma=False,
    )
```

```python
import functools
import itertools

import jax
import jax.numpy as jnp
from jax import lax
from jax.experimental import pallas as pl
from jax.experimental.pallas import tpu as pltpu
from jax.sharding import PartitionSpec as P

KPB = 64
STEPS = 2
JB = 8
TAIL = 8
MIB = 2**20

SMEM = pl.BlockSpec(memory_space=pltpu.SMEM)
VMEM = pl.BlockSpec(memory_space=pltpu.VMEM)
ANY = pl.BlockSpec(memory_space=pl.ANY)


def rows_of(slot, blk):
    return pl.ds(pl.multiple_of(slot * blk, blk), blk)


def prepare_kernel(chunks, a_code, b_code, panels, a_rows, b_rows, which, *refs):
    outs, (a_buf, b_buf, tails, sems) = refs[: len(chunks) + 1], refs[len(chunks) + 1 :]
    blk = a_rows.shape[1]
    loads = [(a_rows, a_buf, pl.ds(f * blk, (e - f) * blk)) for f, e in chunks] + [(b_rows, b_buf, pl.ds(0, b_rows.shape[0]))]
    loads = [pltpu.make_async_copy(rows.at[part], buf.at[part], sems.at[i]) for i, (rows, buf, part) in enumerate(loads)]
    for copy in loads:
        copy.start()
    stores = []
    tails[...] = jnp.zeros_like(tails)
    for i, (code, into) in enumerate(((a_code, outs[0]), (b_code, outs[-1]))):
        tails[i, 0:1, 0 : code.shape[1]] = code[...].astype(jnp.float32)
        last = into.shape[0] - TAIL
        stores.append(pltpu.make_async_copy(tails.at[i], into.at[pl.ds(last, TAIL)], sems.at[2 * len(loads) + i]))
        stores[-1].start()
    lo = jnp.minimum(panels[0], panels[1])
    hi = jnp.maximum(panels[0], panels[1])
    which[0] = jnp.where(lo == 0, 0, lo + 1) + hi - 1
    parts = [a_buf.at[pl.ds(f * blk, (e - f) * blk)] for f, e in chunks] + [b_buf]
    for i, (load, part, out) in enumerate(zip(loads, parts, outs)):
        load.wait()
        stores.append(pltpu.make_async_copy(part, out.at[pl.ds(0, part.shape[0])], sems.at[len(loads) + i]))
        stores[-1].start()
    for copy in stores:
        copy.wait()


def prepare(chunks, a_code, b_code, panels, a_rows, b_rows):
    blk = a_rows.shape[1]
    sizes = [(e - f) * blk for f, e in chunks]
    sizes[0] += TAIL
    sizes.append(b_rows.shape[0] + TAIL)
    return pl.pallas_call(
        functools.partial(prepare_kernel, chunks),
        out_shape=[jax.ShapeDtypeStruct((1,), jnp.int32)] + [jax.ShapeDtypeStruct((x, blk), jnp.float32) for x in sizes],
        in_specs=[VMEM, VMEM, SMEM, ANY, ANY],
        out_specs=[SMEM] + [ANY] * len(sizes),
        scratch_shapes=[
            pltpu.VMEM(a_rows.shape, jnp.float32),
            pltpu.VMEM(b_rows.shape, jnp.float32),
            pltpu.VMEM((2, TAIL, blk), jnp.float32),
            pltpu.SemaphoreType.DMA((2 * len(sizes) + 2,)),
        ],
        name="prepare",
    )(a_code.T, b_code.T, panels, a_rows, b_rows)


def split(x):
    high = x.astype(jnp.bfloat16)
    low = (x - high.astype(jnp.float32)).astype(jnp.bfloat16)
    return high, low


def product(a, b):
    a_high, a_low = split(a)
    b_high, b_low = split(b)
    left = jnp.concatenate([a_high, a_high, a_low], axis=1)
    right = jnp.concatenate([b_high, b_low, b_high], axis=0)
    return jnp.dot(left, right, preferred_element_type=jnp.float32)


def add_products(count, column, a_buf, b_buf, sems, c_ref):
    blk = a_buf.shape[1]

    def wait(m):
        for which, buf in enumerate((a_buf, b_buf)):
            pltpu.make_async_copy(buf.at[m], buf.at[m], sems.at[which, m]).wait()

    def add(m, value):
        c_ref[:, rows_of(column(m), blk)] += value

    def two(i, carry):
        m = 2 * i
        wait(m)
        wait(m + 1)
        first, second = product(a_buf[m], b_buf[m]), product(a_buf[m + 1], b_buf[m + 1])
        add(m, first)
        add(m + 1, second)
        return carry

    lax.fori_loop(0, count // 2, two, 0)

    @pl.when(count % 2 == 1)
    def _():
        wait(count - 1)
        add(count - 1, product(a_buf[count - 1], b_buf[count - 1]))


def start_from(refs, source, rows, into, sem):
    for i, ref in enumerate(refs):

        @pl.when(source == i)
        def _():
            pltpu.make_async_copy(ref.at[rows], into, sem).start()


def early_kernel(chunks, n_a, b_parts, slots, a_at, b_at, *refs):
    group, sb = slots
    parts = max(1, len(chunks) - 1)
    n_b = sum(len(firsts) for firsts in b_parts)
    a_refs = [refs[i * parts : (i + 1) * parts] for i in range(n_a)]
    flat = iter(refs[n_a * parts : n_a * parts + n_b])
    b_refs = [[(first, next(flat)) for first in firsts] for firsts in b_parts]
    late, c_ref, b_late, tails, found, found_s, plan, a_buf, b_buf, sems, late_sems, tail_sems = refs[n_a * parts + n_b :]
    sa = chunks[-1][1]
    last_first = chunks[-1][0]
    blk = a_buf.shape[1]
    k_rows = KPB // group
    sources = [[a_at(s)] + [b_at(s, g) for g in range(group)] for s in range(STEPS)]

    def tail(s, i):
        return s * (1 + group) + i

    for s in range(STEPS):
        for i, source in enumerate(sources[s]):
            for j, holder in enumerate([held[-1][1] for held in b_refs] if i else [arrays[0] for arrays in a_refs]):

                @pl.when(source == j)
                def _():
                    rows = pl.ds(holder.shape[0] - TAIL, TAIL)
                    pltpu.make_async_copy(holder.at[rows], tails.at[tail(s, i)], tail_sems.at[tail(s, i)]).start()

    c_ref[...] = jnp.zeros_like(c_ref)
    found[...] = jnp.full_like(found, -1)
    for i in range(STEPS * (1 + group)):
        pltpu.make_async_copy(tails.at[i], tails.at[i], tail_sems.at[i]).wait()

    for s in range(STEPS):
        a_codes = tails[tail(s, 0), 0:1, :].astype(jnp.int32)
        for g in range(group):
            b_codes = tails[tail(s, 1 + g), 0:1, :].astype(jnp.int32)
            used = (b_codes >= 0) & (lax.broadcasted_iota(jnp.int32, b_codes.shape, 1) < sb)
            k = jnp.where(used, g * k_rows + b_codes // JB, -2)
            hit = jnp.full_like(k, -1)
            for slot in range(sa):
                hit = jnp.where(a_codes[:, slot : slot + 1] == k, slot, hit)
            found[s * group + g : s * group + g + 1, :] = jnp.where(hit >= 0, hit * JB + b_codes % JB, -1)
    copy = pltpu.make_async_copy(found, found_s, tail_sems.at[STEPS * (1 + group)])
    copy.start()
    copy.wait()

    n_early = n_late = jnp.int32(0)
    for row in range(STEPS * group):
        for slot in range(sb):
            hit = found_s[row, slot]
            entry = hit + (row * sb + slot) * sa * JB
            is_late = hit >= last_first * JB
            plan[0, n_early] = entry
            plan[1, n_late] = entry
            n_early += ((hit >= 0) & jnp.logical_not(is_late)).astype(jnp.int32)
            n_late += is_late.astype(jnp.int32)

    def start_b(row, slot, into, sem):
        source = pick([sources[s][1 + g] for s in range(STEPS) for g in range(group)], row)
        for i, held in enumerate(b_refs):

            @pl.when(source == i)
            def _():
                for j, (first, ref) in enumerate(held):
                    end = held[j + 1][0] if j + 1 < len(held) else sb

                    @pl.when((slot >= first) & (slot < end))
                    def _():
                        pltpu.make_async_copy(ref.at[rows_of(slot - first, blk)], into, sem).start()

    def fetch(which, m):
        number, hit = plan[which, m] // (sa * JB), plan[which, m] % (sa * JB)
        row, slot = number // sb, number % sb
        return row, slot, pick([sources[s][0] for s in range(STEPS)], row // group), hit // JB, hit % JB

    def fetch_early(m, carry):
        row, slot, source, a_slot, j = fetch(0, m)
        plan[0, m] = j
        for i, arrays in enumerate(a_refs):
            for (f, e), ref in zip(chunks[:-1], arrays):

                @pl.when((source == i) & (a_slot >= f) & (a_slot < e))
                def _():
                    pltpu.make_async_copy(ref.at[rows_of(a_slot - f, blk)], a_buf.at[m], sems.at[0, m]).start()

        start_b(row, slot, b_buf.at[m], sems.at[1, m])
        return carry

    def fetch_late(m, carry):
        row, slot, source, a_slot, j = fetch(1, m)
        late[1 + 3 * m] = source
        late[2 + 3 * m] = a_slot - last_first
        late[3 + 3 * m] = j
        start_b(row, slot, b_late.at[rows_of(m, blk)], late_sems.at[m])
        return carry

    lax.fori_loop(0, n_early, fetch_early, 0)
    lax.fori_loop(0, n_late, fetch_late, 0)
    counts = (n_early, n_late)
    late[0] = counts[1]
    add_products(counts[0], lambda m: plan[0, m], a_buf, b_buf, sems, c_ref)

    def wait(m, carry):
        into = b_late.at[rows_of(m, blk)]
        pltpu.make_async_copy(into, into, late_sems.at[m]).wait()
        return carry

    lax.fori_loop(0, counts[1], wait, 0)


def late_kernel(n_a, late, c_in, b_late, *refs):
    a_refs, (c_ref, a_buf, b_buf, sems) = refs[:n_a], refs[n_a:]
    blk = a_buf.shape[1]

    def fetch(m, carry):
        start_from(a_refs, late[1 + 3 * m], rows_of(late[2 + 3 * m], blk), a_buf.at[m], sems.at[0, m])
        pltpu.make_async_copy(b_late.at[rows_of(m, blk)], b_buf.at[m], sems.at[1, m]).start()
        return carry

    lax.fori_loop(0, late[0], fetch, 0)
    c_ref[...] = c_in[...]
    add_products(late[0], lambda m: late[3 + 3 * m], a_buf, b_buf, sems, c_ref)


def add_early(chunks, a_sources, b_sources, slots, a_at, b_at):
    group, sb = slots
    b_flat = [array for held in b_sources for _, array in held]
    blk = b_flat[0].shape[1]
    most = STEPS * group * sb
    tails = STEPS * (1 + group)
    n_a = len(a_sources)
    first = chunks[:-1] or chunks
    buffers = [pltpu.VMEM((most, blk, blk), jnp.float32)] * 2 + [pltpu.SemaphoreType.DMA((2, most))]
    band = jax.ShapeDtypeStruct((blk, JB * blk), jnp.float32)
    late, c_early, b_late = pl.pallas_call(
        functools.partial(
            early_kernel, chunks, n_a, [[first for first, _ in held] for held in b_sources], slots, a_at, b_at
        ),
        out_shape=[
            jax.ShapeDtypeStruct((1 + 3 * most,), jnp.int32),
            band,
            jax.ShapeDtypeStruct((most * blk, blk), jnp.float32),
        ],
        in_specs=[ANY] * (n_a * len(first) + len(b_flat)),
        out_specs=[SMEM, VMEM, ANY],
        scratch_shapes=[
            pltpu.VMEM((tails, TAIL, blk), jnp.float32),
            pltpu.VMEM((max(8, STEPS * group), blk), jnp.int32),
            pltpu.SMEM((max(8, STEPS * group), blk), jnp.int32),
            pltpu.SMEM((2, most + 1), jnp.int32),
            *buffers,
            pltpu.SemaphoreType.DMA((most,)),
            pltpu.SemaphoreType.DMA((tails + 1,)),
        ],
        compiler_params=pltpu.CompilerParams(vmem_limit_bytes=12 * MIB),
        cost_estimate=pl.CostEstimate(flops=6 * 8 * blk**3, bytes_accessed=8 * MIB, transcendentals=0),
        name="early",
    )(*[x for arrays in a_sources for x in arrays[: len(first)]], *b_flat)
    return late, c_early, b_late


def add_late(late, c_early, b_late, a_last):
    blk = a_last[0].shape[1]
    most = (late.shape[0] - 1) // 3
    buffers = [pltpu.VMEM((most, blk, blk), jnp.float32)] * 2 + [pltpu.SemaphoreType.DMA((2, most))]
    return pl.pallas_call(
        functools.partial(late_kernel, len(a_last)),
        out_shape=jax.ShapeDtypeStruct(c_early.shape, c_early.dtype),
        in_specs=[SMEM, VMEM, ANY] + [ANY] * len(a_last),
        out_specs=VMEM,
        scratch_shapes=buffers,
        compiler_params=pltpu.CompilerParams(vmem_limit_bytes=12 * MIB),
        cost_estimate=pl.CostEstimate(flops=6 * 2 * blk**3, bytes_accessed=2 * MIB, transcendentals=0),
        name="late",
    )(late, c_early, b_late, *a_last)


def collect_kernel(n, at, *refs):
    sources, outs, (buf, sems) = refs[:n], refs[n : n + 2 * STEPS], refs[n + 2 * STEPS :]
    half = outs[0].shape[0]
    rows = half + outs[1].shape[0]
    parts = [pl.ds(half, rows - half) if i % 2 else pl.ds(0, half) for i in range(len(outs))]
    for i, part in enumerate(parts):
        views = [ref.at[part] for ref in sources[:-2]] + [sources[len(sources) - 2 + i % 2]]
        for j, view in enumerate(views):

            @pl.when(at(i // 2) == j)
            def _():
                pltpu.make_async_copy(view, buf.at[i // 2, part], sems.at[0, i]).start()

    stores = []
    for i, (part, out) in enumerate(zip(parts, outs)):
        held = buf.at[i // 2, part]
        pltpu.make_async_copy(held, held, sems.at[0, i]).wait()
        stores.append(pltpu.make_async_copy(held, out, sems.at[1, i]))
        stores[-1].start()
    for copy in stores:
        copy.wait()


def collect(whole, halves, at):
    rows, blk = whole[0].shape
    sources = [*whole, *halves]
    sizes = [x.shape[0] for x in halves] * STEPS
    return pl.pallas_call(
        functools.partial(collect_kernel, len(sources), at),
        out_shape=[jax.ShapeDtypeStruct((size, blk), whole[0].dtype) for size in sizes],
        in_specs=[ANY] * len(sources),
        out_specs=[ANY] * len(sizes),
        scratch_shapes=[pltpu.VMEM((STEPS, rows, blk), whole[0].dtype), pltpu.SemaphoreType.DMA((2, len(sizes)))],
        compiler_params=pltpu.CompilerParams(vmem_limit_bytes=8 * MIB),
        cost_estimate=pl.CostEstimate(flops=0, bytes_accessed=4 * MIB, transcendentals=0),
        name="collect",
    )(*sources)


def as_rows(x):
    return x.reshape(-1, x.shape[-1])


def gathered(a_vals, a_code, b_vals, b_code, panels, group):
    chunks = [(0, a_vals.shape[0])]
    _, a_own, b_own = prepare(chunks, a_code, b_code, panels, as_rows(a_vals), as_rows(b_vals))
    a_all = lax.all_gather(a_own, "col")
    b_all = lax.all_gather(b_own, "row")
    a_sources, b_sources = [], []
    for step in range(STEPS):
        a_sources.append([lax.dynamic_index_in_dim(a_all, panels[step], 0, keepdims=False)])
        for g in range(group):
            b_sources.append([(0, lax.dynamic_index_in_dim(b_all, panels[step] * group + g, 0, keepdims=False))])
    slots = (group, b_vals.shape[0])
    early = add_early(chunks, a_sources, b_sources, slots, lambda s: s, lambda s, g: s * group + g)
    return add_late(*early, [arrays[-1] for arrays in a_sources])


CHUNKS = [(0, 8), (8, 16)]
ROUTES = {
    (0, 1): [(None, ((0, 1), (1, 2))), (0, ((1, 2), (2, 3))), (1, ((2, 3), (3, 0)))],
    (0, 2): [(None, ((0, 1), (2, 3))), (0, ((1, 2), (3, 1))), (1, ((1, 0), (2, 3)))],
    (0, 3): [(None, ((0, 1), (3, 2))), (0, ((1, 2), (2, 1))), (1, ((2, 3), (1, 0)))],
    (1, 2): [(None, ((1, 0), (2, 3))), (None, ((1, 2), (2, 1))), (1, ((1, 0), (2, 3)))],
}
WRITTEN = ("0a", "0b", "x", "y", "g", "h", "1a", "1b", "2a", "2b", "s", "t", "u", "v")
WAITS = {
    (0, 1): {"1b": ("x", "y"), "v": ("2a",), "u": ("s", "g")},
    (0, 2): {"1b": ("x", "y"), "v": ("2a", "t")},
    (0, 3): {"1b": ("x", "y"), "v": ("2a", "t")},
    (1, 2): {"2b": ("0b", "g", "h"), "2a": ("0a",)},
}


def route_of(roots, n):
    mirror = roots not in ROUTES
    key = tuple(sorted(n - 1 - p for p in roots)) if mirror else roots
    steps, brings = [], []
    for source, pairs in ROUTES[key]:
        if mirror:
            pairs = tuple((n - 1 - x, n - 1 - y) for x, y in pairs)
        steps.append((source, pairs))
        brings.append({y: x if source is None else brings[source][x] for x, y in pairs})
    return steps, brings, WAITS[key]


def pick(values, index):
    out = jnp.asarray(values[0], jnp.int32)
    for i, value in enumerate(values[1:], 1):
        out = jnp.where(index == i, jnp.asarray(value, jnp.int32), out)
    return out


def pair_branch(roots, n, slots, pieces, b_own):
    group, sb = slots
    half = sb // 2
    blk = b_own.shape[1]
    parts = "abcdefgh"[: len(pieces)]

    def exchange(bit):
        return "row", [(r, r ^ bit) for r in range(n * group)]

    def from_chip(s):
        return (lax.axis_index("row") >> 1) ^ roots[s]

    moves = {"x": ("o", *exchange(group)), "y": ("o", *exchange(2 * group))}
    moves.update(g=("first of y", *exchange(group)), h=("last of x", *exchange(2 * group)))
    moves.update({name: ("own " + name, *exchange(1)) for name in "stuv"})
    held = dict(zip(parts, pieces), o=b_own)
    a_names = [list(parts)]
    a_table = [[0] * n for _ in roots]
    steps, brings, waits = route_of(roots, n)
    for number, (source, pairs) in enumerate(steps):
        for at, p in brings[number].items():
            a_table[roots.index(p)][at] = len(a_names)
        for part in parts:
            moves[f"{number}{part}"] = (part if source is None else f"{source}{part}", "col", pairs)
        a_names.append([f"{number}{part}" for part in parts])

    while moves:
        for name in [name for name in WRITTEN if name in moves]:
            source, axis, pairs = moves[name]
            if name == "g" and "y" in held:
                held[source] = held["y"][: half * blk]
            if name == "h" and "x" in held:
                held[source] = held["x"][half * blk :]
            if name == "s" and source not in held and all(e in held for e in ("x", "y", "g", "h", *waits.get("p", ()))):
                last = held["h"]
                if "p" in waits:
                    last = lax.optimization_barrier((last, *[held[e] for e in waits["p"]]))[0]
                halves = collect([held[e] for e in "oxy"], [held["g"], last], from_chip)
                held.update({"own " + name: x for name, x in zip("stuv", halves)})
            if all(e in held for e in (source, *waits.get(name, ()))):
                x = held[source]
                if name in waits:
                    x = lax.optimization_barrier((x, *[held[e] for e in waits[name]]))[0]
                held[name] = lax.ppermute(x, axis, pairs)
                del moves[name]

    a_sources = [[held[name] for name in names] for names in a_names]
    b_sources = [[(0, held[name])] for name in "oxy"]
    b_sources += [[(0, held[name]), (half, held[other])] for name, other in ("gh", "st", "uv")]

    def a_at(s):
        return pick(a_table[s], lax.axis_index("col"))

    def b_at(s, g):
        return jnp.where((lax.axis_index("row") & 1) == g, from_chip(s), n + s)

    early = add_early(CHUNKS, a_sources, b_sources, slots, a_at, b_at)
    return early, [arrays[-1] for arrays in a_sources[1:]]


def shards(a_vals, a_code, b_vals, b_code, panels):
    n = lax.axis_size("col")
    group = lax.axis_size("row") // n
    if group != 2 or n != 4:
        return gathered(a_vals, a_code, b_vals, b_code, panels, group)
    which, *pieces, b_own = prepare(CHUNKS, a_code, b_code, panels, as_rows(a_vals), as_rows(b_vals))
    slots = (group, b_vals.shape[0])
    branches = [functools.partial(pair_branch, pair, n, slots) for pair in itertools.combinations(range(n), 2)]
    early, a_last = lax.switch(which[0], branches, pieces, b_own)
    return add_late(*early, [pieces[-1], *a_last])


def solution(mesh):
    return jax.shard_map(
        shards,
        mesh=mesh,
        in_specs=(
            P("row", "col", None),
            P("row", "col"),
            P("row", "col", None),
            P("row", "col"),
            P(),
        ),
        out_specs=P("row", "col"),
        check_vma=False,
    )
```

```python
import functools
import itertools

import jax
import jax.numpy as jnp
from jax import lax
from jax.experimental import pallas as pl
from jax.experimental.pallas import tpu as pltpu
from jax.sharding import PartitionSpec as P

KPB = 64
STEPS = 2
JB = 8
TAIL = 8
MIB = 2**20

SMEM = pl.BlockSpec(memory_space=pltpu.SMEM)
VMEM = pl.BlockSpec(memory_space=pltpu.VMEM)
ANY = pl.BlockSpec(memory_space=pl.ANY)


def rows_of(slot, blk):
    return pl.ds(pl.multiple_of(slot * blk, blk), blk)


def prepare_kernel(chunks, a_code, b_code, panels, a_rows, b_rows, which, *refs):
    outs, (a_buf, b_buf, tails, sems) = refs[: len(chunks) + 1], refs[len(chunks) + 1 :]
    blk = a_rows.shape[1]
    loads = [(a_rows, a_buf, pl.ds(f * blk, (e - f) * blk)) for f, e in chunks] + [(b_rows, b_buf, pl.ds(0, b_rows.shape[0]))]
    loads = [pltpu.make_async_copy(rows.at[part], buf.at[part], sems.at[i]) for i, (rows, buf, part) in enumerate(loads)]
    for copy in loads:
        copy.start()
    stores = []
    tails[...] = jnp.zeros_like(tails)
    for i, (code, into) in enumerate(((a_code, outs[0]), (b_code, outs[-1]))):
        tails[i, 0:1, 0 : code.shape[1]] = code[...].astype(jnp.float32)
        last = into.shape[0] - TAIL
        stores.append(pltpu.make_async_copy(tails.at[i], into.at[pl.ds(last, TAIL)], sems.at[2 * len(loads) + i]))
        stores[-1].start()
    lo = jnp.minimum(panels[0], panels[1])
    hi = jnp.maximum(panels[0], panels[1])
    which[0] = jnp.where(lo == 0, 0, lo + 1) + hi - 1
    parts = [a_buf.at[pl.ds(f * blk, (e - f) * blk)] for f, e in chunks] + [b_buf]
    for i, (load, part, out) in enumerate(zip(loads, parts, outs)):
        load.wait()
        stores.append(pltpu.make_async_copy(part, out.at[pl.ds(0, part.shape[0])], sems.at[len(loads) + i]))
        stores[-1].start()
    for copy in stores:
        copy.wait()


def prepare(chunks, a_code, b_code, panels, a_rows, b_rows):
    blk = a_rows.shape[1]
    sizes = [(e - f) * blk for f, e in chunks]
    sizes[0] += TAIL
    sizes.append(b_rows.shape[0] + TAIL)
    return pl.pallas_call(
        functools.partial(prepare_kernel, chunks),
        out_shape=[jax.ShapeDtypeStruct((1,), jnp.int32)] + [jax.ShapeDtypeStruct((x, blk), jnp.float32) for x in sizes],
        in_specs=[VMEM, VMEM, SMEM, ANY, ANY],
        out_specs=[SMEM] + [ANY] * len(sizes),
        scratch_shapes=[
            pltpu.VMEM(a_rows.shape, jnp.float32),
            pltpu.VMEM(b_rows.shape, jnp.float32),
            pltpu.VMEM((2, TAIL, blk), jnp.float32),
            pltpu.SemaphoreType.DMA((2 * len(sizes) + 2,)),
        ],
        name="prepare",
    )(a_code.T, b_code.T, panels, a_rows, b_rows)


def split(x):
    high = x.astype(jnp.bfloat16)
    low = (x - high.astype(jnp.float32)).astype(jnp.bfloat16)
    return high, low


def product(a, b):
    a_high, a_low = split(a)
    b_high, b_low = split(b)
    left = jnp.concatenate([a_high, a_high, a_low], axis=1)
    right = jnp.concatenate([b_high, b_low, b_high], axis=0)
    return jnp.dot(left, right, preferred_element_type=jnp.float32)


def add_products(count, column, a_buf, b_buf, sems, c_ref):
    blk = a_buf.shape[1]

    def wait(m):
        for which, buf in enumerate((a_buf, b_buf)):
            pltpu.make_async_copy(buf.at[m], buf.at[m], sems.at[which, m]).wait()

    def add(m, value):
        c_ref[:, rows_of(column(m), blk)] += value

    def two(i, carry):
        m = 2 * i
        wait(m)
        wait(m + 1)
        first, second = product(a_buf[m], b_buf[m]), product(a_buf[m + 1], b_buf[m + 1])
        add(m, first)
        add(m + 1, second)
        return carry

    lax.fori_loop(0, count // 2, two, 0)

    @pl.when(count % 2 == 1)
    def _():
        wait(count - 1)
        add(count - 1, product(a_buf[count - 1], b_buf[count - 1]))


def start_from(refs, source, rows, into, sem):
    for i, ref in enumerate(refs):

        @pl.when(source == i)
        def _():
            pltpu.make_async_copy(ref.at[rows], into, sem).start()


def early_kernel(chunks, n_a, b_parts, slots, a_at, b_at, *refs):
    group, sb = slots
    parts = max(1, len(chunks) - 1)
    n_b = sum(len(firsts) for firsts in b_parts)
    a_refs = [refs[i * parts : (i + 1) * parts] for i in range(n_a)]
    flat = iter(refs[n_a * parts : n_a * parts + n_b])
    b_refs = [[(first, next(flat)) for first in firsts] for firsts in b_parts]
    late, c_ref, b_late, tails, found, found_s, plan, a_buf, b_buf, sems, late_sems, tail_sems = refs[n_a * parts + n_b :]
    sa = chunks[-1][1]
    last_first = chunks[-1][0]
    blk = a_buf.shape[1]
    k_rows = KPB // group
    sources = [[a_at(s)] + [b_at(s, g) for g in range(group)] for s in range(STEPS)]

    def tail(s, i):
        return s * (1 + group) + i

    for s in range(STEPS):
        for i, source in enumerate(sources[s]):
            for j, holder in enumerate([held[-1][1] for held in b_refs] if i else [arrays[0] for arrays in a_refs]):

                @pl.when(source == j)
                def _():
                    rows = pl.ds(holder.shape[0] - TAIL, TAIL)
                    pltpu.make_async_copy(holder.at[rows], tails.at[tail(s, i)], tail_sems.at[tail(s, i)]).start()

    c_ref[...] = jnp.zeros_like(c_ref)
    found[...] = jnp.full_like(found, -1)
    for i in range(STEPS * (1 + group)):
        pltpu.make_async_copy(tails.at[i], tails.at[i], tail_sems.at[i]).wait()

    for s in range(STEPS):
        a_codes = tails[tail(s, 0), 0:1, :].astype(jnp.int32)
        for g in range(group):
            b_codes = tails[tail(s, 1 + g), 0:1, :].astype(jnp.int32)
            used = (b_codes >= 0) & (lax.broadcasted_iota(jnp.int32, b_codes.shape, 1) < sb)
            k = jnp.where(used, g * k_rows + b_codes // JB, -2)
            hit = jnp.full_like(k, -1)
            for slot in range(sa):
                hit = jnp.where(a_codes[:, slot : slot + 1] == k, slot, hit)
            found[s * group + g : s * group + g + 1, :] = jnp.where(hit >= 0, hit * JB + b_codes % JB, -1)
    copy = pltpu.make_async_copy(found, found_s, tail_sems.at[STEPS * (1 + group)])
    copy.start()
    copy.wait()

    n_early = n_late = jnp.int32(0)
    for row in range(STEPS * group):
        for slot in range(sb):
            hit = found_s[row, slot]
            entry = hit + (row * sb + slot) * sa * JB
            is_late = hit >= last_first * JB
            plan[0, n_early] = entry
            plan[1, n_late] = entry
            n_early += ((hit >= 0) & jnp.logical_not(is_late)).astype(jnp.int32)
            n_late += is_late.astype(jnp.int32)

    def start_b(row, slot, into, sem):
        source = pick([sources[s][1 + g] for s in range(STEPS) for g in range(group)], row)
        for i, held in enumerate(b_refs):

            @pl.when(source == i)
            def _():
                for j, (first, ref) in enumerate(held):
                    end = held[j + 1][0] if j + 1 < len(held) else sb

                    @pl.when((slot >= first) & (slot < end))
                    def _():
                        pltpu.make_async_copy(ref.at[rows_of(slot - first, blk)], into, sem).start()

    def fetch(which, m):
        number, hit = plan[which, m] // (sa * JB), plan[which, m] % (sa * JB)
        row, slot = number // sb, number % sb
        return row, slot, pick([sources[s][0] for s in range(STEPS)], row // group), hit // JB, hit % JB

    def fetch_early(m, carry):
        row, slot, source, a_slot, j = fetch(0, m)
        plan[0, m] = j
        for i, arrays in enumerate(a_refs):
            for (f, e), ref in zip(chunks[:-1], arrays):

                @pl.when((source == i) & (a_slot >= f) & (a_slot < e))
                def _():
                    pltpu.make_async_copy(ref.at[rows_of(a_slot - f, blk)], a_buf.at[m], sems.at[0, m]).start()

        start_b(row, slot, b_buf.at[m], sems.at[1, m])
        return carry

    def fetch_late(m, carry):
        row, slot, source, a_slot, j = fetch(1, m)
        late[1 + 3 * m] = source
        late[2 + 3 * m] = a_slot - last_first
        late[3 + 3 * m] = j
        start_b(row, slot, b_late.at[rows_of(m, blk)], late_sems.at[m])
        return carry

    lax.fori_loop(0, n_early, fetch_early, 0)
    lax.fori_loop(0, n_late, fetch_late, 0)
    counts = (n_early, n_late)
    late[0] = counts[1]
    add_products(counts[0], lambda m: plan[0, m], a_buf, b_buf, sems, c_ref)

    def wait(m, carry):
        into = b_late.at[rows_of(m, blk)]
        pltpu.make_async_copy(into, into, late_sems.at[m]).wait()
        return carry

    lax.fori_loop(0, counts[1], wait, 0)


def late_kernel(n_a, late, c_in, b_late, *refs):
    a_refs, (c_ref, a_buf, b_buf, sems) = refs[:n_a], refs[n_a:]
    blk = a_buf.shape[1]

    def fetch(m, carry):
        start_from(a_refs, late[1 + 3 * m], rows_of(late[2 + 3 * m], blk), a_buf.at[m], sems.at[0, m])
        pltpu.make_async_copy(b_late.at[rows_of(m, blk)], b_buf.at[m], sems.at[1, m]).start()
        return carry

    lax.fori_loop(0, late[0], fetch, 0)
    c_ref[...] = c_in[...]
    add_products(late[0], lambda m: late[3 + 3 * m], a_buf, b_buf, sems, c_ref)


def add_early(chunks, a_sources, b_sources, slots, a_at, b_at):
    group, sb = slots
    b_flat = [array for held in b_sources for _, array in held]
    blk = b_flat[0].shape[1]
    most = STEPS * group * sb
    tails = STEPS * (1 + group)
    n_a = len(a_sources)
    first = chunks[:-1] or chunks
    buffers = [pltpu.VMEM((most, blk, blk), jnp.float32)] * 2 + [pltpu.SemaphoreType.DMA((2, most))]
    band = jax.ShapeDtypeStruct((blk, JB * blk), jnp.float32)
    late, c_early, b_late = pl.pallas_call(
        functools.partial(
            early_kernel, chunks, n_a, [[first for first, _ in held] for held in b_sources], slots, a_at, b_at
        ),
        out_shape=[
            jax.ShapeDtypeStruct((1 + 3 * most,), jnp.int32),
            band,
            jax.ShapeDtypeStruct((most * blk, blk), jnp.float32),
        ],
        in_specs=[ANY] * (n_a * len(first) + len(b_flat)),
        out_specs=[SMEM, VMEM, ANY],
        scratch_shapes=[
            pltpu.VMEM((tails, TAIL, blk), jnp.float32),
            pltpu.VMEM((max(8, STEPS * group), blk), jnp.int32),
            pltpu.SMEM((max(8, STEPS * group), blk), jnp.int32),
            pltpu.SMEM((2, most + 1), jnp.int32),
            *buffers,
            pltpu.SemaphoreType.DMA((most,)),
            pltpu.SemaphoreType.DMA((tails + 1,)),
        ],
        compiler_params=pltpu.CompilerParams(vmem_limit_bytes=12 * MIB),
        cost_estimate=pl.CostEstimate(flops=6 * 8 * blk**3, bytes_accessed=8 * MIB, transcendentals=0),
        name="early",
    )(*[x for arrays in a_sources for x in arrays[: len(first)]], *b_flat)
    return late, c_early, b_late


def add_late(late, c_early, b_late, a_last):
    blk = a_last[0].shape[1]
    most = (late.shape[0] - 1) // 3
    buffers = [pltpu.VMEM((most, blk, blk), jnp.float32)] * 2 + [pltpu.SemaphoreType.DMA((2, most))]
    return pl.pallas_call(
        functools.partial(late_kernel, len(a_last)),
        out_shape=jax.ShapeDtypeStruct(c_early.shape, c_early.dtype),
        in_specs=[SMEM, VMEM, ANY] + [ANY] * len(a_last),
        out_specs=VMEM,
        scratch_shapes=buffers,
        compiler_params=pltpu.CompilerParams(vmem_limit_bytes=12 * MIB),
        cost_estimate=pl.CostEstimate(flops=6 * 2 * blk**3, bytes_accessed=2 * MIB, transcendentals=0),
        name="late",
    )(late, c_early, b_late, *a_last)


def collect_kernel(n, at, *refs):
    sources, outs, (buf, sems) = refs[:n], refs[n : n + 2 * STEPS], refs[n + 2 * STEPS :]
    half = outs[0].shape[0]
    rows = half + outs[1].shape[0]
    parts = [pl.ds(half, rows - half) if i % 2 else pl.ds(0, half) for i in range(len(outs))]
    for i, part in enumerate(parts):
        views = [ref.at[part] for ref in sources[:-2]] + [sources[len(sources) - 2 + i % 2]]
        for j, view in enumerate(views):

            @pl.when(at(i // 2) == j)
            def _():
                pltpu.make_async_copy(view, buf.at[i // 2, part], sems.at[0, i]).start()

    stores = []
    for i, (part, out) in enumerate(zip(parts, outs)):
        held = buf.at[i // 2, part]
        pltpu.make_async_copy(held, held, sems.at[0, i]).wait()
        stores.append(pltpu.make_async_copy(held, out, sems.at[1, i]))
        stores[-1].start()
    for copy in stores:
        copy.wait()


def collect(whole, halves, at):
    rows, blk = whole[0].shape
    sources = [*whole, *halves]
    sizes = [x.shape[0] for x in halves] * STEPS
    return pl.pallas_call(
        functools.partial(collect_kernel, len(sources), at),
        out_shape=[jax.ShapeDtypeStruct((size, blk), whole[0].dtype) for size in sizes],
        in_specs=[ANY] * len(sources),
        out_specs=[ANY] * len(sizes),
        scratch_shapes=[pltpu.VMEM((STEPS, rows, blk), whole[0].dtype), pltpu.SemaphoreType.DMA((2, len(sizes)))],
        compiler_params=pltpu.CompilerParams(vmem_limit_bytes=8 * MIB),
        cost_estimate=pl.CostEstimate(flops=0, bytes_accessed=4 * MIB, transcendentals=0),
        name="collect",
    )(*sources)


def as_rows(x):
    return x.reshape(-1, x.shape[-1])


def gathered(a_vals, a_code, b_vals, b_code, panels, group):
    chunks = [(0, a_vals.shape[0])]
    _, a_own, b_own = prepare(chunks, a_code, b_code, panels, as_rows(a_vals), as_rows(b_vals))
    a_all = lax.all_gather(a_own, "col")
    b_all = lax.all_gather(b_own, "row")
    a_sources, b_sources = [], []
    for step in range(STEPS):
        a_sources.append([lax.dynamic_index_in_dim(a_all, panels[step], 0, keepdims=False)])
        for g in range(group):
            b_sources.append([(0, lax.dynamic_index_in_dim(b_all, panels[step] * group + g, 0, keepdims=False))])
    slots = (group, b_vals.shape[0])
    early = add_early(chunks, a_sources, b_sources, slots, lambda s: s, lambda s, g: s * group + g)
    return add_late(*early, [arrays[-1] for arrays in a_sources])


CHUNKS = [(0, 8), (8, 16)]
ROUTES = {
    (0, 1): [(None, ((0, 1), (1, 2))), (0, ((1, 2), (2, 3))), (1, ((2, 3), (3, 0)))],
    (0, 2): [(None, ((0, 1), (2, 3))), (0, ((1, 2), (3, 1))), (1, ((1, 0), (2, 3)))],
    (0, 3): [(None, ((0, 1), (3, 2))), (0, ((1, 2), (2, 1))), (1, ((2, 3), (1, 0)))],
    (1, 2): [(None, ((1, 0), (2, 3))), (None, ((1, 2), (2, 1))), (1, ((1, 0), (2, 3)))],
}
WRITTEN = ("0a", "0b", "x", "y", "g", "h", "1a", "1b", "2a", "2b", "s", "t", "u", "v")
WAITS = {
    (0, 1): {"1b": ("x", "y"), "v": ("2a",), "u": ("s", "g")},
    (0, 2): {"2b": ("2a", "1b")},
    (0, 3): {"2b": ("2a", "1b")},
    (1, 2): {"2b": ("2a", "1b", "0b")},
}


def route_of(roots, n):
    mirror = roots not in ROUTES
    key = tuple(sorted(n - 1 - p for p in roots)) if mirror else roots
    steps, brings = [], []
    for source, pairs in ROUTES[key]:
        if mirror:
            pairs = tuple((n - 1 - x, n - 1 - y) for x, y in pairs)
        steps.append((source, pairs))
        brings.append({y: x if source is None else brings[source][x] for x, y in pairs})
    return steps, brings, WAITS[key]


def pick(values, index):
    out = jnp.asarray(values[0], jnp.int32)
    for i, value in enumerate(values[1:], 1):
        out = jnp.where(index == i, jnp.asarray(value, jnp.int32), out)
    return out


def pair_branch(roots, n, slots, pieces, b_own):
    group, sb = slots
    half = sb // 2
    blk = b_own.shape[1]
    parts = "abcdefgh"[: len(pieces)]

    def exchange(bit):
        return "row", [(r, r ^ bit) for r in range(n * group)]

    def from_chip(s):
        return (lax.axis_index("row") >> 1) ^ roots[s]

    moves = {"x": ("o", *exchange(group)), "y": ("o", *exchange(2 * group))}
    moves.update(g=("first of y", *exchange(group)), h=("last of x", *exchange(2 * group)))
    moves.update({name: ("own " + name, *exchange(1)) for name in "stuv"})
    held = dict(zip(parts, pieces), o=b_own)
    a_names = [list(parts)]
    a_table = [[0] * n for _ in roots]
    steps, brings, waits = route_of(roots, n)
    for number, (source, pairs) in enumerate(steps):
        for at, p in brings[number].items():
            a_table[roots.index(p)][at] = len(a_names)
        for part in parts:
            moves[f"{number}{part}"] = (part if source is None else f"{source}{part}", "col", pairs)
        a_names.append([f"{number}{part}" for part in parts])

    while moves:
        for name in [name for name in WRITTEN if name in moves]:
            source, axis, pairs = moves[name]
            if name == "g" and "y" in held:
                held[source] = held["y"][: half * blk]
            if name == "h" and "x" in held:
                held[source] = held["x"][half * blk :]
            if name == "s" and source not in held and all(e in held for e in ("x", "y", "g", "h", *waits.get("p", ()))):
                last = held["h"]
                if "p" in waits:
                    last = lax.optimization_barrier((last, *[held[e] for e in waits["p"]]))[0]
                halves = collect([held[e] for e in "oxy"], [held["g"], last], from_chip)
                held.update({"own " + name: x for name, x in zip("stuv", halves)})
            if all(e in held for e in (source, *waits.get(name, ()))):
                x = held[source]
                if name in waits:
                    x = lax.optimization_barrier((x, *[held[e] for e in waits[name]]))[0]
                held[name] = lax.ppermute(x, axis, pairs)
                del moves[name]

    a_sources = [[held[name] for name in names] for names in a_names]
    b_sources = [[(0, held[name])] for name in "oxy"]
    b_sources += [[(0, held[name]), (half, held[other])] for name, other in ("gh", "st", "uv")]

    def a_at(s):
        return pick(a_table[s], lax.axis_index("col"))

    def b_at(s, g):
        return jnp.where((lax.axis_index("row") & 1) == g, from_chip(s), n + s)

    early = add_early(CHUNKS, a_sources, b_sources, slots, a_at, b_at)
    return early, [arrays[-1] for arrays in a_sources[1:]]


def shards(a_vals, a_code, b_vals, b_code, panels):
    n = lax.axis_size("col")
    group = lax.axis_size("row") // n
    if group != 2 or n != 4:
        return gathered(a_vals, a_code, b_vals, b_code, panels, group)
    which, *pieces, b_own = prepare(CHUNKS, a_code, b_code, panels, as_rows(a_vals), as_rows(b_vals))
    slots = (group, b_vals.shape[0])
    branches = [functools.partial(pair_branch, pair, n, slots) for pair in itertools.combinations(range(n), 2)]
    early, a_last = lax.switch(which[0], branches, pieces, b_own)
    return add_late(*early, [pieces[-1], *a_last])


def solution(mesh):
    return jax.shard_map(
        shards,
        mesh=mesh,
        in_specs=(
            P("row", "col", None),
            P("row", "col"),
            P("row", "col", None),
            P("row", "col"),
            P(),
        ),
        out_specs=P("row", "col"),
        check_vma=False,
    )
```

```python
import functools
import itertools

import jax
import jax.numpy as jnp
from jax import lax
from jax.experimental import pallas as pl
from jax.experimental.pallas import tpu as pltpu
from jax.sharding import PartitionSpec as P

KPB = 64
STEPS = 2
JB = 8
TAIL = 8
MIB = 2**20

SMEM = pl.BlockSpec(memory_space=pltpu.SMEM)
VMEM = pl.BlockSpec(memory_space=pltpu.VMEM)
ANY = pl.BlockSpec(memory_space=pl.ANY)


def rows_of(slot, blk):
    return pl.ds(pl.multiple_of(slot * blk, blk), blk)


def prepare_kernel(chunks, a_code, b_code, panels, a_rows, b_rows, which, *refs):
    outs, (a_buf, b_buf, tails, sems) = refs[: len(chunks) + 1], refs[len(chunks) + 1 :]
    blk = a_rows.shape[1]
    loads = [(a_rows, a_buf, pl.ds(f * blk, (e - f) * blk)) for f, e in chunks] + [(b_rows, b_buf, pl.ds(0, b_rows.shape[0]))]
    loads = [pltpu.make_async_copy(rows.at[part], buf.at[part], sems.at[i]) for i, (rows, buf, part) in enumerate(loads)]
    for copy in loads:
        copy.start()
    stores = []
    tails[...] = jnp.zeros_like(tails)
    for i, (code, into) in enumerate(((a_code, outs[0]), (b_code, outs[-1]))):
        tails[i, 0:1, 0 : code.shape[1]] = code[...].astype(jnp.float32)
        last = into.shape[0] - TAIL
        stores.append(pltpu.make_async_copy(tails.at[i], into.at[pl.ds(last, TAIL)], sems.at[2 * len(loads) + i]))
        stores[-1].start()
    lo = jnp.minimum(panels[0], panels[1])
    hi = jnp.maximum(panels[0], panels[1])
    which[0] = jnp.where(lo == 0, 0, lo + 1) + hi - 1
    parts = [a_buf.at[pl.ds(f * blk, (e - f) * blk)] for f, e in chunks] + [b_buf]
    for i, (load, part, out) in enumerate(zip(loads, parts, outs)):
        load.wait()
        stores.append(pltpu.make_async_copy(part, out.at[pl.ds(0, part.shape[0])], sems.at[len(loads) + i]))
        stores[-1].start()
    for copy in stores:
        copy.wait()


def prepare(chunks, a_code, b_code, panels, a_rows, b_rows):
    blk = a_rows.shape[1]
    sizes = [(e - f) * blk for f, e in chunks]
    sizes[0] += TAIL
    sizes.append(b_rows.shape[0] + TAIL)
    return pl.pallas_call(
        functools.partial(prepare_kernel, chunks),
        out_shape=[jax.ShapeDtypeStruct((1,), jnp.int32)] + [jax.ShapeDtypeStruct((x, blk), jnp.float32) for x in sizes],
        in_specs=[VMEM, VMEM, SMEM, ANY, ANY],
        out_specs=[SMEM] + [ANY] * len(sizes),
        scratch_shapes=[
            pltpu.VMEM(a_rows.shape, jnp.float32),
            pltpu.VMEM(b_rows.shape, jnp.float32),
            pltpu.VMEM((2, TAIL, blk), jnp.float32),
            pltpu.SemaphoreType.DMA((2 * len(sizes) + 2,)),
        ],
        name="prepare",
    )(a_code.T, b_code.T, panels, a_rows, b_rows)


def split(x):
    high = x.astype(jnp.bfloat16)
    low = (x - high.astype(jnp.float32)).astype(jnp.bfloat16)
    return high, low


def product(a, b):
    a_high, a_low = split(a)
    b_high, b_low = split(b)
    left = jnp.concatenate([a_high, a_high, a_low], axis=1)
    right = jnp.concatenate([b_high, b_low, b_high], axis=0)
    return jnp.dot(left, right, preferred_element_type=jnp.float32)


def add_products(count, column, pair, c_ref):
    blk = c_ref.shape[0]

    def add(m, value):
        c_ref[:, rows_of(column(m), blk)] += value

    def two(i, carry):
        m = 2 * i
        (a, b), (a_next, b_next) = pair(m), pair(m + 1)
        first, second = product(a, b), product(a_next, b_next)
        add(m, first)
        add(m + 1, second)
        return carry

    lax.fori_loop(0, count // 2, two, 0)

    @pl.when(count % 2 == 1)
    def _():
        add(count - 1, product(*pair(count - 1)))


def start_from(refs, source, rows, into, sem):
    for i, ref in enumerate(refs):

        @pl.when(source == i)
        def _():
            pltpu.make_async_copy(ref.at[rows], into, sem).start()


def early_kernel(chunks, n_a, b_parts, slots, a_at, b_at, *refs):
    group, sb = slots
    parts = max(1, len(chunks) - 1)
    n_b = sum(len(firsts) for firsts in b_parts)
    a_refs = [refs[i * parts : (i + 1) * parts] for i in range(n_a)]
    flat = iter(refs[n_a * parts : n_a * parts + n_b])
    b_refs = [[(first, next(flat)) for first in firsts] for firsts in b_parts]
    late, c_ref, b_late, tails, found, found_s, plan, a_buf, b_buf, sems, late_sems, tail_sems = refs[n_a * parts + n_b :]
    sa = chunks[-1][1]
    last_first = chunks[-1][0]
    blk = a_buf.shape[1]
    k_rows = KPB // group
    sources = [[a_at(s)] + [b_at(s, g) for g in range(group)] for s in range(STEPS)]

    def tail(s, i):
        return s * (1 + group) + i

    for s in range(STEPS):
        for i, source in enumerate(sources[s]):
            for j, holder in enumerate([held[-1][1] for held in b_refs] if i else [arrays[0] for arrays in a_refs]):

                @pl.when(source == j)
                def _():
                    rows = pl.ds(holder.shape[0] - TAIL, TAIL)
                    pltpu.make_async_copy(holder.at[rows], tails.at[tail(s, i)], tail_sems.at[tail(s, i)]).start()

    c_ref[...] = jnp.zeros_like(c_ref)
    found[...] = jnp.full_like(found, -1)
    for i in range(STEPS * (1 + group)):
        pltpu.make_async_copy(tails.at[i], tails.at[i], tail_sems.at[i]).wait()

    for s in range(STEPS):
        a_codes = tails[tail(s, 0), 0:1, :].astype(jnp.int32)
        for g in range(group):
            b_codes = tails[tail(s, 1 + g), 0:1, :].astype(jnp.int32)
            used = (b_codes >= 0) & (lax.broadcasted_iota(jnp.int32, b_codes.shape, 1) < sb)
            k = jnp.where(used, g * k_rows + b_codes // JB, -2)
            hit = jnp.full_like(k, -1)
            for slot in range(sa):
                hit = jnp.where(a_codes[:, slot : slot + 1] == k, slot, hit)
            found[s * group + g : s * group + g + 1, :] = jnp.where(hit >= 0, hit * JB + b_codes % JB, -1)
    copy = pltpu.make_async_copy(found, found_s, tail_sems.at[STEPS * (1 + group)])
    copy.start()
    copy.wait()

    n_early = n_late = jnp.int32(0)
    for row in range(STEPS * group):
        for slot in range(sb):
            hit = found_s[row, slot]
            entry = hit + (row * sb + slot) * sa * JB
            is_late = hit >= last_first * JB
            plan[0, n_early] = entry
            plan[1, n_late] = entry
            n_early += ((hit >= 0) & jnp.logical_not(is_late)).astype(jnp.int32)
            n_late += is_late.astype(jnp.int32)

    def start_b(row, slot, into, sem):
        source = pick([sources[s][1 + g] for s in range(STEPS) for g in range(group)], row)
        for i, held in enumerate(b_refs):

            @pl.when(source == i)
            def _():
                for j, (first, ref) in enumerate(held):
                    end = held[j + 1][0] if j + 1 < len(held) else sb

                    @pl.when((slot >= first) & (slot < end))
                    def _():
                        pltpu.make_async_copy(ref.at[rows_of(slot - first, blk)], into, sem).start()

    def fetch(which, m):
        number, hit = plan[which, m] // (sa * JB), plan[which, m] % (sa * JB)
        row, slot = number // sb, number % sb
        return row, slot, pick([sources[s][0] for s in range(STEPS)], row // group), hit // JB, hit % JB

    def fetch_early(m, carry):
        row, slot, source, a_slot, j = fetch(0, m)
        plan[0, m] = j
        for i, arrays in enumerate(a_refs):
            for (f, e), ref in zip(chunks[:-1], arrays):

                @pl.when((source == i) & (a_slot >= f) & (a_slot < e))
                def _():
                    pltpu.make_async_copy(ref.at[rows_of(a_slot - f, blk)], a_buf.at[m], sems.at[0, m]).start()

        start_b(row, slot, b_buf.at[m], sems.at[1, m])
        return carry

    def fetch_late(m, carry):
        row, slot, source, a_slot, j = fetch(1, m)
        late[1 + 3 * m] = source
        late[2 + 3 * m] = a_slot - last_first
        late[3 + 3 * m] = j
        start_b(row, slot, b_late.at[rows_of(m, blk)], late_sems.at[m])
        return carry

    lax.fori_loop(0, n_early, fetch_early, 0)
    lax.fori_loop(0, n_late, fetch_late, 0)
    counts = (n_early, n_late)
    late[0] = counts[1]

    def pair(m):
        for which, buf in enumerate((a_buf, b_buf)):
            pltpu.make_async_copy(buf.at[m], buf.at[m], sems.at[which, m]).wait()
        return a_buf[m], b_buf[m]

    add_products(counts[0], lambda m: plan[0, m], pair, c_ref)

    def wait(m, carry):
        into = b_late.at[rows_of(m, blk)]
        pltpu.make_async_copy(into, into, late_sems.at[m]).wait()
        return carry

    lax.fori_loop(0, counts[1], wait, 0)


def late_kernel(n_a, late, c_in, b_late, *refs):
    a_refs, (c_ref, a_buf, sems) = refs[:n_a], refs[n_a:]
    blk = a_buf.shape[1]

    def fetch(m, carry):
        start_from(a_refs, late[1 + 3 * m], rows_of(late[2 + 3 * m], blk), a_buf.at[m], sems.at[m])
        return carry

    def pair(m):
        pltpu.make_async_copy(a_buf.at[m], a_buf.at[m], sems.at[m]).wait()
        return a_buf[m], b_late[rows_of(m, blk), :]

    lax.fori_loop(0, late[0], fetch, 0)
    c_ref[...] = c_in[...]
    add_products(late[0], lambda m: late[3 + 3 * m], pair, c_ref)


def add_early(chunks, a_sources, b_sources, slots, a_at, b_at):
    group, sb = slots
    b_flat = [array for held in b_sources for _, array in held]
    blk = b_flat[0].shape[1]
    most = STEPS * group * sb
    tails = STEPS * (1 + group)
    n_a = len(a_sources)
    first = chunks[:-1] or chunks
    buffers = [pltpu.VMEM((most, blk, blk), jnp.float32)] * 2 + [pltpu.SemaphoreType.DMA((2, most))]
    band = jax.ShapeDtypeStruct((blk, JB * blk), jnp.float32)
    late, c_early, b_late = pl.pallas_call(
        functools.partial(
            early_kernel, chunks, n_a, [[first for first, _ in held] for held in b_sources], slots, a_at, b_at
        ),
        out_shape=[
            jax.ShapeDtypeStruct((1 + 3 * most,), jnp.int32),
            band,
            jax.ShapeDtypeStruct((most * blk, blk), jnp.float32),
        ],
        in_specs=[ANY] * (n_a * len(first) + len(b_flat)),
        out_specs=[SMEM, VMEM, ANY],
        scratch_shapes=[
            pltpu.VMEM((tails, TAIL, blk), jnp.float32),
            pltpu.VMEM((max(8, STEPS * group), blk), jnp.int32),
            pltpu.SMEM((max(8, STEPS * group), blk), jnp.int32),
            pltpu.SMEM((2, most + 1), jnp.int32),
            *buffers,
            pltpu.SemaphoreType.DMA((most,)),
            pltpu.SemaphoreType.DMA((tails + 1,)),
        ],
        compiler_params=pltpu.CompilerParams(vmem_limit_bytes=12 * MIB),
        cost_estimate=pl.CostEstimate(flops=6 * 8 * blk**3, bytes_accessed=8 * MIB, transcendentals=0),
        name="early",
    )(*[x for arrays in a_sources for x in arrays[: len(first)]], *b_flat)
    return late, c_early, b_late


def add_late(late, c_early, b_late, a_last):
    blk = a_last[0].shape[1]
    most = (late.shape[0] - 1) // 3
    return pl.pallas_call(
        functools.partial(late_kernel, len(a_last)),
        out_shape=jax.ShapeDtypeStruct(c_early.shape, c_early.dtype),
        in_specs=[SMEM, VMEM, VMEM] + [ANY] * len(a_last),
        out_specs=VMEM,
        scratch_shapes=[pltpu.VMEM((most, blk, blk), jnp.float32), pltpu.SemaphoreType.DMA((most,))],
        compiler_params=pltpu.CompilerParams(vmem_limit_bytes=12 * MIB),
        cost_estimate=pl.CostEstimate(flops=6 * 2 * blk**3, bytes_accessed=2 * MIB, transcendentals=0),
        name="late",
    )(late, c_early, b_late, *a_last)


def collect_kernel(n, at, *refs):
    sources, outs, (buf, sems) = refs[:n], refs[n : n + 2 * STEPS], refs[n + 2 * STEPS :]
    half = outs[0].shape[0]
    rows = half + outs[1].shape[0]
    parts = [pl.ds(half, rows - half) if i % 2 else pl.ds(0, half) for i in range(len(outs))]
    for i, part in enumerate(parts):
        views = [ref.at[part] for ref in sources[:-2]] + [sources[len(sources) - 2 + i % 2]]
        for j, view in enumerate(views):

            @pl.when(at(i // 2) == j)
            def _():
                pltpu.make_async_copy(view, buf.at[i // 2, part], sems.at[0, i]).start()

    stores = []
    for i, (part, out) in enumerate(zip(parts, outs)):
        held = buf.at[i // 2, part]
        pltpu.make_async_copy(held, held, sems.at[0, i]).wait()
        stores.append(pltpu.make_async_copy(held, out, sems.at[1, i]))
        stores[-1].start()
    for copy in stores:
        copy.wait()


def collect(whole, halves, at):
    rows, blk = whole[0].shape
    sources = [*whole, *halves]
    sizes = [x.shape[0] for x in halves] * STEPS
    return pl.pallas_call(
        functools.partial(collect_kernel, len(sources), at),
        out_shape=[jax.ShapeDtypeStruct((size, blk), whole[0].dtype) for size in sizes],
        in_specs=[ANY] * len(sources),
        out_specs=[ANY] * len(sizes),
        scratch_shapes=[pltpu.VMEM((STEPS, rows, blk), whole[0].dtype), pltpu.SemaphoreType.DMA((2, len(sizes)))],
        compiler_params=pltpu.CompilerParams(vmem_limit_bytes=8 * MIB),
        cost_estimate=pl.CostEstimate(flops=0, bytes_accessed=4 * MIB, transcendentals=0),
        name="collect",
    )(*sources)


def as_rows(x):
    return x.reshape(-1, x.shape[-1])


def gathered(a_vals, a_code, b_vals, b_code, panels, group):
    chunks = [(0, a_vals.shape[0])]
    _, a_own, b_own = prepare(chunks, a_code, b_code, panels, as_rows(a_vals), as_rows(b_vals))
    a_all = lax.all_gather(a_own, "col")
    b_all = lax.all_gather(b_own, "row")
    a_sources, b_sources = [], []
    for step in range(STEPS):
        a_sources.append([lax.dynamic_index_in_dim(a_all, panels[step], 0, keepdims=False)])
        for g in range(group):
            b_sources.append([(0, lax.dynamic_index_in_dim(b_all, panels[step] * group + g, 0, keepdims=False))])
    slots = (group, b_vals.shape[0])
    early = add_early(chunks, a_sources, b_sources, slots, lambda s: s, lambda s, g: s * group + g)
    return add_late(*early, [arrays[-1] for arrays in a_sources])


CHUNKS = [(0, 8), (8, 16)]
ROUTES = {
    (0, 1): [(None, ((0, 1), (1, 2))), (0, ((1, 2), (2, 3))), (1, ((2, 3), (3, 0)))],
    (0, 2): [(None, ((0, 1), (2, 3))), (0, ((1, 2), (3, 1))), (1, ((1, 0), (2, 3)))],
    (0, 3): [(None, ((0, 1), (3, 2))), (0, ((1, 2), (2, 1))), (1, ((2, 3), (1, 0)))],
    (1, 2): [(None, ((1, 0), (2, 3))), (None, ((1, 2), (2, 1))), (1, ((1, 0), (2, 3)))],
}
WRITTEN = ("0a", "0b", "x", "y", "g", "h", "1a", "1b", "2a", "2b", "s", "t", "u", "v")
WAITS = {
    (0, 1): {"1b": ("x", "y"), "v": ("2a",), "u": ("s", "g")},
    (0, 2): {"u": ("s",), "v": ("s", "2a")},
    (0, 3): {"u": ("s",), "v": ("s", "2a")},
    (1, 2): {"2b": ("0b", "g", "h"), "2a": ("0a",)},
}


def route_of(roots, n):
    mirror = roots not in ROUTES
    key = tuple(sorted(n - 1 - p for p in roots)) if mirror else roots
    steps, brings = [], []
    for source, pairs in ROUTES[key]:
        if mirror:
            pairs = tuple((n - 1 - x, n - 1 - y) for x, y in pairs)
        steps.append((source, pairs))
        brings.append({y: x if source is None else brings[source][x] for x, y in pairs})
    return steps, brings, WAITS[key]


def pick(values, index):
    out = jnp.asarray(values[0], jnp.int32)
    for i, value in enumerate(values[1:], 1):
        out = jnp.where(index == i, jnp.asarray(value, jnp.int32), out)
    return out


def pair_branch(roots, n, slots, pieces, b_own):
    group, sb = slots
    half = sb // 2
    blk = b_own.shape[1]
    parts = "abcdefgh"[: len(pieces)]

    def exchange(bit):
        return "row", [(r, r ^ bit) for r in range(n * group)]

    def from_chip(s):
        return (lax.axis_index("row") >> 1) ^ roots[s]

    moves = {"x": ("o", *exchange(group)), "y": ("o", *exchange(2 * group))}
    moves.update(g=("first of y", *exchange(group)), h=("last of x", *exchange(2 * group)))
    moves.update({name: ("own " + name, *exchange(1)) for name in "stuv"})
    held = dict(zip(parts, pieces), o=b_own)
    a_names = [list(parts)]
    a_table = [[0] * n for _ in roots]
    steps, brings, waits = route_of(roots, n)
    for number, (source, pairs) in enumerate(steps):
        for at, p in brings[number].items():
            a_table[roots.index(p)][at] = len(a_names)
        for part in parts:
            moves[f"{number}{part}"] = (part if source is None else f"{source}{part}", "col", pairs)
        a_names.append([f"{number}{part}" for part in parts])

    while moves:
        for name in [name for name in WRITTEN if name in moves]:
            source, axis, pairs = moves[name]
            if name == "g" and "y" in held:
                held[source] = held["y"][: half * blk]
            if name == "h" and "x" in held:
                held[source] = held["x"][half * blk :]
            if name == "s" and source not in held and all(e in held for e in ("x", "y", "g", "h", *waits.get("p", ()))):
                last = held["h"]
                if "p" in waits:
                    last = lax.optimization_barrier((last, *[held[e] for e in waits["p"]]))[0]
                halves = collect([held[e] for e in "oxy"], [held["g"], last], from_chip)
                held.update({"own " + name: x for name, x in zip("stuv", halves)})
            if all(e in held for e in (source, *waits.get(name, ()))):
                x = held[source]
                if name in waits:
                    x = lax.optimization_barrier((x, *[held[e] for e in waits[name]]))[0]
                held[name] = lax.ppermute(x, axis, pairs)
                del moves[name]

    a_sources = [[held[name] for name in names] for names in a_names]
    b_sources = [[(0, held[name])] for name in "oxy"]
    b_sources += [[(0, held[name]), (half, held[other])] for name, other in ("gh", "st", "uv")]

    def a_at(s):
        return pick(a_table[s], lax.axis_index("col"))

    def b_at(s, g):
        return jnp.where((lax.axis_index("row") & 1) == g, from_chip(s), n + s)

    early = add_early(CHUNKS, a_sources, b_sources, slots, a_at, b_at)
    return early, [arrays[-1] for arrays in a_sources[1:]]


def shards(a_vals, a_code, b_vals, b_code, panels):
    n = lax.axis_size("col")
    group = lax.axis_size("row") // n
    if group != 2 or n != 4:
        return gathered(a_vals, a_code, b_vals, b_code, panels, group)
    which, *pieces, b_own = prepare(CHUNKS, a_code, b_code, panels, as_rows(a_vals), as_rows(b_vals))
    slots = (group, b_vals.shape[0])
    branches = [functools.partial(pair_branch, pair, n, slots) for pair in itertools.combinations(range(n), 2)]
    early, a_last = lax.switch(which[0], branches, pieces, b_own)
    return add_late(*early, [pieces[-1], *a_last])


def solution(mesh):
    return jax.shard_map(
        shards,
        mesh=mesh,
        in_specs=(
            P("row", "col", None),
            P("row", "col"),
            P("row", "col", None),
            P("row", "col"),
            P(),
        ),
        out_specs=P("row", "col"),
        check_vma=False,
    )
```

```python
import functools
import itertools

import jax
import jax.numpy as jnp
from jax import lax
from jax.experimental import pallas as pl
from jax.experimental.pallas import tpu as pltpu
from jax.sharding import PartitionSpec as P

KPB = 64
STEPS = 2
JB = 8
TAIL = 8
MIB = 2**20

SMEM = pl.BlockSpec(memory_space=pltpu.SMEM)
VMEM = pl.BlockSpec(memory_space=pltpu.VMEM)
ANY = pl.BlockSpec(memory_space=pl.ANY)


def rows_of(slot, blk):
    return pl.ds(pl.multiple_of(slot * blk, blk), blk)


def prepare_kernel(chunks, a_code, b_code, panels, a_rows, b_rows, which, *refs):
    outs, sems = refs[:-1], refs[-1]
    blk = a_rows.shape[1]
    parts = [a_rows.at[pl.ds(f * blk, (e - f) * blk)] for f, e in chunks] + [b_rows]
    copies = [
        pltpu.make_async_copy(part, out.at[pl.ds(0, part.shape[0])], sems.at[i])
        for i, (part, out) in enumerate(zip(parts, outs))
    ]
    for copy in copies:
        copy.start()
    for code, out in ((a_code, outs[0]), (b_code, outs[-1])):
        last = out.shape[0] - TAIL
        out[last:, :] = jnp.zeros((TAIL, blk), jnp.float32)
        out[last : last + 1, 0 : code.shape[1]] = code[...].astype(jnp.float32)
    lo = jnp.minimum(panels[0], panels[1])
    hi = jnp.maximum(panels[0], panels[1])
    which[0] = jnp.where(lo == 0, 0, lo + 1) + hi - 1
    for copy in copies:
        copy.wait()


def prepare(chunks, a_code, b_code, panels, a_rows, b_rows):
    blk = a_rows.shape[1]
    sizes = [(e - f) * blk for f, e in chunks]
    sizes[0] += TAIL
    sizes.append(b_rows.shape[0] + TAIL)
    return pl.pallas_call(
        functools.partial(prepare_kernel, chunks),
        out_shape=[jax.ShapeDtypeStruct((1,), jnp.int32)] + [jax.ShapeDtypeStruct((x, blk), jnp.float32) for x in sizes],
        in_specs=[VMEM, VMEM, SMEM, ANY, ANY],
        out_specs=[SMEM] + [VMEM] * len(sizes),
        scratch_shapes=[pltpu.SemaphoreType.DMA((len(sizes),))],
        name="prepare",
    )(a_code.T, b_code.T, panels, a_rows, b_rows)


def split(x):
    high = x.astype(jnp.bfloat16)
    low = (x - high.astype(jnp.float32)).astype(jnp.bfloat16)
    return high, low


def product(a, b):
    a_high, a_low = split(a)
    b_high, b_low = split(b)
    left = jnp.concatenate([a_high, a_high, a_low], axis=1)
    right = jnp.concatenate([b_high, b_low, b_high], axis=0)
    return jnp.dot(left, right, preferred_element_type=jnp.float32)


def add_products(count, column, pair, c_ref):
    blk = c_ref.shape[0]

    def add(m, value):
        c_ref[:, rows_of(column(m), blk)] += value

    def two(i, carry):
        m = 2 * i
        (a, b), (a_next, b_next) = pair(m), pair(m + 1)
        first, second = product(a, b), product(a_next, b_next)
        add(m, first)
        add(m + 1, second)
        return carry

    lax.fori_loop(0, count // 2, two, 0)

    @pl.when(count % 2 == 1)
    def _():
        add(count - 1, product(*pair(count - 1)))


def start_from(refs, source, rows, into, sem):
    for i, ref in enumerate(refs):

        @pl.when(source == i)
        def _():
            pltpu.make_async_copy(ref.at[rows], into, sem).start()


def early_kernel(chunks, n_a, b_parts, slots, a_at, b_at, *refs):
    group, sb = slots
    parts = max(1, len(chunks) - 1)
    n_b = sum(len(firsts) for firsts in b_parts)
    a_refs = [refs[i * parts : (i + 1) * parts] for i in range(n_a)]
    flat = iter(refs[n_a * parts : n_a * parts + n_b])
    b_refs = [[(first, next(flat)) for first in firsts] for firsts in b_parts]
    late, c_ref, b_late, tails, found, found_s, plan, a_buf, b_buf, sems, late_sems, tail_sems = refs[n_a * parts + n_b :]
    sa = chunks[-1][1]
    last_first = chunks[-1][0]
    blk = a_buf.shape[1]
    k_rows = KPB // group
    sources = [[a_at(s)] + [b_at(s, g) for g in range(group)] for s in range(STEPS)]

    def tail(s, i):
        return s * (1 + group) + i

    for s in range(STEPS):
        for i, source in enumerate(sources[s]):
            for j, holder in enumerate([held[-1][1] for held in b_refs] if i else [arrays[0] for arrays in a_refs]):

                @pl.when(source == j)
                def _():
                    rows = pl.ds(holder.shape[0] - TAIL, TAIL)
                    pltpu.make_async_copy(holder.at[rows], tails.at[tail(s, i)], tail_sems.at[tail(s, i)]).start()

    c_ref[...] = jnp.zeros_like(c_ref)
    found[...] = jnp.full_like(found, -1)
    for i in range(STEPS * (1 + group)):
        pltpu.make_async_copy(tails.at[i], tails.at[i], tail_sems.at[i]).wait()

    for s in range(STEPS):
        a_codes = tails[tail(s, 0), 0:1, :].astype(jnp.int32)
        for g in range(group):
            b_codes = tails[tail(s, 1 + g), 0:1, :].astype(jnp.int32)
            used = (b_codes >= 0) & (lax.broadcasted_iota(jnp.int32, b_codes.shape, 1) < sb)
            k = jnp.where(used, g * k_rows + b_codes // JB, -2)
            hit = jnp.full_like(k, -1)
            for slot in range(sa):
                hit = jnp.where(a_codes[:, slot : slot + 1] == k, slot, hit)
            found[s * group + g : s * group + g + 1, :] = jnp.where(hit >= 0, hit * JB + b_codes % JB, -1)
    copy = pltpu.make_async_copy(found, found_s, tail_sems.at[STEPS * (1 + group)])
    copy.start()
    copy.wait()

    n_early = n_late = jnp.int32(0)
    for row in range(STEPS * group):
        for slot in range(sb):
            hit = found_s[row, slot]
            entry = hit + (row * sb + slot) * sa * JB
            is_late = hit >= last_first * JB
            plan[0, n_early] = entry
            plan[1, n_late] = entry
            n_early += ((hit >= 0) & jnp.logical_not(is_late)).astype(jnp.int32)
            n_late += is_late.astype(jnp.int32)

    def start_b(row, slot, into, sem):
        source = pick([sources[s][1 + g] for s in range(STEPS) for g in range(group)], row)
        for i, held in enumerate(b_refs):

            @pl.when(source == i)
            def _():
                for j, (first, ref) in enumerate(held):
                    end = held[j + 1][0] if j + 1 < len(held) else sb

                    @pl.when((slot >= first) & (slot < end))
                    def _():
                        pltpu.make_async_copy(ref.at[rows_of(slot - first, blk)], into, sem).start()

    def fetch(which, m):
        number, hit = plan[which, m] // (sa * JB), plan[which, m] % (sa * JB)
        row, slot = number // sb, number % sb
        return row, slot, pick([sources[s][0] for s in range(STEPS)], row // group), hit // JB, hit % JB

    def fetch_early(m, carry):
        row, slot, source, a_slot, j = fetch(0, m)
        plan[0, m] = j
        for i, arrays in enumerate(a_refs):
            for (f, e), ref in zip(chunks[:-1], arrays):

                @pl.when((source == i) & (a_slot >= f) & (a_slot < e))
                def _():
                    pltpu.make_async_copy(ref.at[rows_of(a_slot - f, blk)], a_buf.at[m], sems.at[0, m]).start()

        start_b(row, slot, b_buf.at[m], sems.at[1, m])
        return carry

    def fetch_late(m, carry):
        row, slot, source, a_slot, j = fetch(1, m)
        late[1 + 3 * m] = source
        late[2 + 3 * m] = a_slot - last_first
        late[3 + 3 * m] = j
        start_b(row, slot, b_late.at[rows_of(m, blk)], late_sems.at[m])
        return carry

    lax.fori_loop(0, n_early, fetch_early, 0)
    lax.fori_loop(0, n_late, fetch_late, 0)
    counts = (n_early, n_late)
    late[0] = counts[1]

    def pair(m):
        for which, buf in enumerate((a_buf, b_buf)):
            pltpu.make_async_copy(buf.at[m], buf.at[m], sems.at[which, m]).wait()
        return a_buf[m], b_buf[m]

    add_products(counts[0], lambda m: plan[0, m], pair, c_ref)

    def wait(m, carry):
        into = b_late.at[rows_of(m, blk)]
        pltpu.make_async_copy(into, into, late_sems.at[m]).wait()
        return carry

    lax.fori_loop(0, counts[1], wait, 0)


def late_kernel(n_a, late, c_in, b_late, *refs):
    a_refs, (c_ref, a_buf, sems) = refs[:n_a], refs[n_a:]
    blk = a_buf.shape[1]

    def fetch(m, carry):
        start_from(a_refs, late[1 + 3 * m], rows_of(late[2 + 3 * m], blk), a_buf.at[m], sems.at[m])
        return carry

    def pair(m):
        pltpu.make_async_copy(a_buf.at[m], a_buf.at[m], sems.at[m]).wait()
        return a_buf[m], b_late[rows_of(m, blk), :]

    lax.fori_loop(0, late[0], fetch, 0)
    c_ref[...] = c_in[...]
    add_products(late[0], lambda m: late[3 + 3 * m], pair, c_ref)


def add_early(chunks, a_sources, b_sources, slots, a_at, b_at):
    group, sb = slots
    b_flat = [array for held in b_sources for _, array in held]
    blk = b_flat[0].shape[1]
    most = STEPS * group * sb
    tails = STEPS * (1 + group)
    n_a = len(a_sources)
    first = chunks[:-1] or chunks
    buffers = [pltpu.VMEM((most, blk, blk), jnp.float32)] * 2 + [pltpu.SemaphoreType.DMA((2, most))]
    band = jax.ShapeDtypeStruct((blk, JB * blk), jnp.float32)
    late, c_early, b_late = pl.pallas_call(
        functools.partial(
            early_kernel, chunks, n_a, [[first for first, _ in held] for held in b_sources], slots, a_at, b_at
        ),
        out_shape=[
            jax.ShapeDtypeStruct((1 + 3 * most,), jnp.int32),
            band,
            jax.ShapeDtypeStruct((most * blk, blk), jnp.float32),
        ],
        in_specs=[ANY] * (n_a * len(first) + len(b_flat)),
        out_specs=[SMEM, VMEM, ANY],
        scratch_shapes=[
            pltpu.VMEM((tails, TAIL, blk), jnp.float32),
            pltpu.VMEM((max(8, STEPS * group), blk), jnp.int32),
            pltpu.SMEM((max(8, STEPS * group), blk), jnp.int32),
            pltpu.SMEM((2, most + 1), jnp.int32),
            *buffers,
            pltpu.SemaphoreType.DMA((most,)),
            pltpu.SemaphoreType.DMA((tails + 1,)),
        ],
        compiler_params=pltpu.CompilerParams(vmem_limit_bytes=12 * MIB),
        cost_estimate=pl.CostEstimate(flops=6 * 8 * blk**3, bytes_accessed=8 * MIB, transcendentals=0),
        name="early",
    )(*[x for arrays in a_sources for x in arrays[: len(first)]], *b_flat)
    return late, c_early, b_late


def add_late(late, c_early, b_late, a_last):
    blk = a_last[0].shape[1]
    most = (late.shape[0] - 1) // 3
    return pl.pallas_call(
        functools.partial(late_kernel, len(a_last)),
        out_shape=jax.ShapeDtypeStruct(c_early.shape, c_early.dtype),
        in_specs=[SMEM, VMEM, VMEM] + [ANY] * len(a_last),
        out_specs=VMEM,
        scratch_shapes=[pltpu.VMEM((most, blk, blk), jnp.float32), pltpu.SemaphoreType.DMA((most,))],
        compiler_params=pltpu.CompilerParams(vmem_limit_bytes=12 * MIB),
        cost_estimate=pl.CostEstimate(flops=6 * 2 * blk**3, bytes_accessed=2 * MIB, transcendentals=0),
        name="late",
    )(late, c_early, b_late, *a_last)


def collect_kernel(n, at, *refs):
    sources, outs, sems = refs[:n], refs[n : n + 2 * STEPS], refs[n + 2 * STEPS]
    half = outs[0].shape[0]
    for i, out in enumerate(outs):
        part = pl.ds(half if i % 2 else 0, out.shape[0])
        views = [ref.at[part] for ref in sources[:-2]] + [sources[len(sources) - 2 + i % 2]]
        for j, view in enumerate(views):

            @pl.when(at(i // 2) == j)
            def _():
                pltpu.make_async_copy(view, out, sems.at[i]).start()

    for i, out in enumerate(outs):
        pltpu.make_async_copy(out, out, sems.at[i]).wait()


def collect(whole, halves, at):
    rows, blk = whole[0].shape
    sources = [*whole, *halves]
    sizes = [x.shape[0] for x in halves] * STEPS
    return pl.pallas_call(
        functools.partial(collect_kernel, len(sources), at),
        out_shape=[jax.ShapeDtypeStruct((size, blk), whole[0].dtype) for size in sizes],
        in_specs=[ANY] * len(sources),
        out_specs=[VMEM] * len(sizes),
        scratch_shapes=[pltpu.SemaphoreType.DMA((len(sizes),))],
        compiler_params=pltpu.CompilerParams(vmem_limit_bytes=8 * MIB),
        cost_estimate=pl.CostEstimate(flops=0, bytes_accessed=4 * MIB, transcendentals=0),
        name="collect",
    )(*sources)


def as_rows(x):
    return x.reshape(-1, x.shape[-1])


def gathered(a_vals, a_code, b_vals, b_code, panels, group):
    chunks = [(0, a_vals.shape[0])]
    _, a_own, b_own = prepare(chunks, a_code, b_code, panels, as_rows(a_vals), as_rows(b_vals))
    a_all = lax.all_gather(a_own, "col")
    b_all = lax.all_gather(b_own, "row")
    a_sources, b_sources = [], []
    for step in range(STEPS):
        a_sources.append([lax.dynamic_index_in_dim(a_all, panels[step], 0, keepdims=False)])
        for g in range(group):
            b_sources.append([(0, lax.dynamic_index_in_dim(b_all, panels[step] * group + g, 0, keepdims=False))])
    slots = (group, b_vals.shape[0])
    early = add_early(chunks, a_sources, b_sources, slots, lambda s: s, lambda s, g: s * group + g)
    return add_late(*early, [arrays[-1] for arrays in a_sources])


CHUNKS = [(0, 8), (8, 16)]
ROUTES = {
    (0, 1): [(None, ((0, 1), (1, 2))), (0, ((1, 2), (2, 3))), (1, ((2, 3), (3, 0)))],
    (0, 2): [(None, ((0, 1), (2, 3))), (0, ((1, 2), (3, 1))), (1, ((1, 0), (2, 3)))],
    (0, 3): [(None, ((0, 1), (3, 2))), (0, ((1, 2), (2, 1))), (1, ((2, 3), (1, 0)))],
    (1, 2): [(None, ((1, 0), (2, 3))), (None, ((1, 2), (2, 1))), (1, ((1, 0), (2, 3)))],
}
WRITTEN = ("0a", "0b", "x", "y", "g", "h", "1a", "1b", "2a", "2b", "s", "t", "u", "v")
WAITS = {
    (0, 1): {"1b": ("x", "y"), "v": ("2a",), "u": ("s", "g")},
    (0, 2): {"u": ("s",), "v": ("s", "2a")},
    (0, 3): {"u": ("s",), "v": ("s", "2a")},
    (1, 2): {"2b": ("0b", "g", "h"), "2a": ("0a",)},
}


def route_of(roots, n):
    mirror = roots not in ROUTES
    key = tuple(sorted(n - 1 - p for p in roots)) if mirror else roots
    steps, brings = [], []
    for source, pairs in ROUTES[key]:
        if mirror:
            pairs = tuple((n - 1 - x, n - 1 - y) for x, y in pairs)
        steps.append((source, pairs))
        brings.append({y: x if source is None else brings[source][x] for x, y in pairs})
    return steps, brings, WAITS[key]


def pick(values, index):
    out = jnp.asarray(values[0], jnp.int32)
    for i, value in enumerate(values[1:], 1):
        out = jnp.where(index == i, jnp.asarray(value, jnp.int32), out)
    return out


def pair_branch(roots, n, slots, pieces, b_own):
    group, sb = slots
    half = sb // 2
    blk = b_own.shape[1]
    parts = "abcdefgh"[: len(pieces)]

    def exchange(bit):
        return "row", [(r, r ^ bit) for r in range(n * group)]

    def from_chip(s):
        return (lax.axis_index("row") >> 1) ^ roots[s]

    moves = {"x": ("o", *exchange(group)), "y": ("o", *exchange(2 * group))}
    moves.update(g=("first of y", *exchange(group)), h=("last of x", *exchange(2 * group)))
    moves.update({name: ("own " + name, *exchange(1)) for name in "stuv"})
    held = dict(zip(parts, pieces), o=b_own)
    a_names = [list(parts)]
    a_table = [[0] * n for _ in roots]
    steps, brings, waits = route_of(roots, n)
    for number, (source, pairs) in enumerate(steps):
        for at, p in brings[number].items():
            a_table[roots.index(p)][at] = len(a_names)
        for part in parts:
            moves[f"{number}{part}"] = (part if source is None else f"{source}{part}", "col", pairs)
        a_names.append([f"{number}{part}" for part in parts])

    while moves:
        for name in [name for name in WRITTEN if name in moves]:
            source, axis, pairs = moves[name]
            if name == "g" and "y" in held:
                held[source] = held["y"][: half * blk]
            if name == "h" and "x" in held:
                held[source] = held["x"][half * blk :]
            if name == "s" and source not in held and all(e in held for e in ("x", "y", "g", "h", *waits.get("p", ()))):
                last = held["h"]
                if "p" in waits:
                    last = lax.optimization_barrier((last, *[held[e] for e in waits["p"]]))[0]
                halves = collect([held[e] for e in "oxy"], [held["g"], last], from_chip)
                held.update({"own " + name: x for name, x in zip("stuv", halves)})
            if all(e in held for e in (source, *waits.get(name, ()))):
                x = held[source]
                if name in waits:
                    x = lax.optimization_barrier((x, *[held[e] for e in waits[name]]))[0]
                held[name] = lax.ppermute(x, axis, pairs)
                del moves[name]

    a_sources = [[held[name] for name in names] for names in a_names]
    b_sources = [[(0, held[name])] for name in "oxy"]
    b_sources += [[(0, held[name]), (half, held[other])] for name, other in ("gh", "st", "uv")]

    def a_at(s):
        return pick(a_table[s], lax.axis_index("col"))

    def b_at(s, g):
        return jnp.where((lax.axis_index("row") & 1) == g, from_chip(s), n + s)

    early = add_early(CHUNKS, a_sources, b_sources, slots, a_at, b_at)
    return early, [arrays[-1] for arrays in a_sources[1:]]


def shards(a_vals, a_code, b_vals, b_code, panels):
    n = lax.axis_size("col")
    group = lax.axis_size("row") // n
    if group != 2 or n != 4:
        return gathered(a_vals, a_code, b_vals, b_code, panels, group)
    which, *pieces, b_own = prepare(CHUNKS, a_code, b_code, panels, as_rows(a_vals), as_rows(b_vals))
    slots = (group, b_vals.shape[0])
    branches = [functools.partial(pair_branch, pair, n, slots) for pair in itertools.combinations(range(n), 2)]
    early, a_last = lax.switch(which[0], branches, pieces, b_own)
    return add_late(*early, [pieces[-1], *a_last])


def solution(mesh):
    return jax.shard_map(
        shards,
        mesh=mesh,
        in_specs=(
            P("row", "col", None),
            P("row", "col"),
            P("row", "col", None),
            P("row", "col"),
            P(),
        ),
        out_specs=P("row", "col"),
        check_vma=False,
    )
```

```python
import functools
import itertools

import jax
import jax.numpy as jnp
from jax import lax
from jax.experimental import pallas as pl
from jax.experimental.pallas import tpu as pltpu
from jax.sharding import PartitionSpec as P

KPB = 64
STEPS = 2
JB = 8
TAIL = 8
MIB = 2**20

SMEM = pl.BlockSpec(memory_space=pltpu.SMEM)
VMEM = pl.BlockSpec(memory_space=pltpu.VMEM)
ANY = pl.BlockSpec(memory_space=pl.ANY)


def rows_of(slot, blk):
    return pl.ds(pl.multiple_of(slot * blk, blk), blk)


def prepare_kernel(chunks, a_code, b_code, panels, a_rows, b_rows, which, *refs):
    outs, (a_small, b_small, panels_s, sems) = refs[:-4], refs[-4:]
    blk = a_rows.shape[1]
    small = [(panels, panels_s), (a_code, a_small), (b_code, b_small)]
    small = [pltpu.make_async_copy(x, y, sems.at[len(outs) + i]) for i, (x, y) in enumerate(small)]
    for copy in small:
        copy.start()
    parts = [a_rows.at[pl.ds(f * blk, (e - f) * blk)] for f, e in chunks] + [b_rows]
    copies = [
        pltpu.make_async_copy(part, out.at[pl.ds(0, part.shape[0])], sems.at[i])
        for i, (part, out) in enumerate(zip(parts, outs))
    ]
    for copy in copies:
        copy.start()
    for copy in small:
        copy.wait()
    for code, out in ((a_small, outs[0]), (b_small, outs[-1])):
        last = out.shape[0] - TAIL
        out[last:, :] = jnp.zeros((TAIL, blk), jnp.float32)
        out[last : last + 1, 0 : code.shape[1]] = code[...].astype(jnp.float32)
    lo = jnp.minimum(panels_s[0], panels_s[1])
    hi = jnp.maximum(panels_s[0], panels_s[1])
    which[0] = jnp.where(lo == 0, 0, lo + 1) + hi - 1
    for copy in copies:
        copy.wait()


def prepare(chunks, a_code, b_code, panels, a_rows, b_rows):
    blk = a_rows.shape[1]
    sizes = [(e - f) * blk for f, e in chunks]
    sizes[0] += TAIL
    sizes.append(b_rows.shape[0] + TAIL)
    return pl.pallas_call(
        functools.partial(prepare_kernel, chunks),
        out_shape=[jax.ShapeDtypeStruct((1,), jnp.int32)] + [jax.ShapeDtypeStruct((x, blk), jnp.float32) for x in sizes],
        in_specs=[ANY] * 5,
        out_specs=[SMEM] + [VMEM] * len(sizes),
        scratch_shapes=[
            pltpu.VMEM(a_code.T.shape, jnp.int32),
            pltpu.VMEM(b_code.T.shape, jnp.int32),
            pltpu.SMEM(panels.shape, jnp.int32),
            pltpu.SemaphoreType.DMA((len(sizes) + 3,)),
        ],
        name="prepare",
    )(a_code.T, b_code.T, panels, a_rows, b_rows)


def split(x):
    high = x.astype(jnp.bfloat16)
    low = (x - high.astype(jnp.float32)).astype(jnp.bfloat16)
    return high, low


def product(a, b):
    a_high, a_low = split(a)
    b_high, b_low = split(b)
    left = jnp.concatenate([a_high, a_high, a_low], axis=1)
    right = jnp.concatenate([b_high, b_low, b_high], axis=0)
    return jnp.dot(left, right, preferred_element_type=jnp.float32)


def add_products(count, column, pair, c_ref):
    blk = c_ref.shape[0]

    def add(m, value):
        c_ref[:, rows_of(column(m), blk)] += value

    def two(i, carry):
        m = 2 * i
        (a, b), (a_next, b_next) = pair(m), pair(m + 1)
        first, second = product(a, b), product(a_next, b_next)
        add(m, first)
        add(m + 1, second)
        return carry

    lax.fori_loop(0, count // 2, two, 0)

    @pl.when(count % 2 == 1)
    def _():
        add(count - 1, product(*pair(count - 1)))


def start_from(refs, source, rows, into, sem):
    for i, ref in enumerate(refs):

        @pl.when(source == i)
        def _():
            pltpu.make_async_copy(ref.at[rows], into, sem).start()


def early_kernel(chunks, n_a, b_parts, slots, a_at, b_at, *refs):
    group, sb = slots
    parts = max(1, len(chunks) - 1)
    n_b = sum(len(firsts) for firsts in b_parts)
    a_refs = [refs[i * parts : (i + 1) * parts] for i in range(n_a)]
    flat = iter(refs[n_a * parts : n_a * parts + n_b])
    b_refs = [[(first, next(flat)) for first in firsts] for firsts in b_parts]
    late, c_ref, b_late, tails, found, found_s, plan, a_buf, b_buf, sems, late_sems, tail_sems = refs[n_a * parts + n_b :]
    sa = chunks[-1][1]
    last_first = chunks[-1][0]
    blk = a_buf.shape[1]
    k_rows = KPB // group
    sources = [[a_at(s)] + [b_at(s, g) for g in range(group)] for s in range(STEPS)]

    def tail(s, i):
        return s * (1 + group) + i

    for s in range(STEPS):
        for i, source in enumerate(sources[s]):
            for j, holder in enumerate([held[-1][1] for held in b_refs] if i else [arrays[0] for arrays in a_refs]):

                @pl.when(source == j)
                def _():
                    rows = pl.ds(holder.shape[0] - TAIL, TAIL)
                    pltpu.make_async_copy(holder.at[rows], tails.at[tail(s, i)], tail_sems.at[tail(s, i)]).start()

    c_ref[...] = jnp.zeros_like(c_ref)
    found[...] = jnp.full_like(found, -1)
    for i in range(STEPS * (1 + group)):
        pltpu.make_async_copy(tails.at[i], tails.at[i], tail_sems.at[i]).wait()

    for s in range(STEPS):
        a_codes = tails[tail(s, 0), 0:1, :].astype(jnp.int32)
        for g in range(group):
            b_codes = tails[tail(s, 1 + g), 0:1, :].astype(jnp.int32)
            used = (b_codes >= 0) & (lax.broadcasted_iota(jnp.int32, b_codes.shape, 1) < sb)
            k = jnp.where(used, g * k_rows + b_codes // JB, -2)
            hit = jnp.full_like(k, -1)
            for slot in range(sa):
                hit = jnp.where(a_codes[:, slot : slot + 1] == k, slot, hit)
            found[s * group + g : s * group + g + 1, :] = jnp.where(hit >= 0, hit * JB + b_codes % JB, -1)
    copy = pltpu.make_async_copy(found, found_s, tail_sems.at[STEPS * (1 + group)])
    copy.start()
    copy.wait()

    n_early = n_late = jnp.int32(0)
    for row in range(STEPS * group):
        for slot in range(sb):
            hit = found_s[row, slot]
            entry = hit + (row * sb + slot) * sa * JB
            is_late = hit >= last_first * JB
            plan[0, n_early] = entry
            plan[1, n_late] = entry
            n_early += ((hit >= 0) & jnp.logical_not(is_late)).astype(jnp.int32)
            n_late += is_late.astype(jnp.int32)

    def start_b(row, slot, into, sem):
        source = pick([sources[s][1 + g] for s in range(STEPS) for g in range(group)], row)
        for i, held in enumerate(b_refs):

            @pl.when(source == i)
            def _():
                for j, (first, ref) in enumerate(held):
                    end = held[j + 1][0] if j + 1 < len(held) else sb

                    @pl.when((slot >= first) & (slot < end))
                    def _():
                        pltpu.make_async_copy(ref.at[rows_of(slot - first, blk)], into, sem).start()

    def fetch(which, m):
        number, hit = plan[which, m] // (sa * JB), plan[which, m] % (sa * JB)
        row, slot = number // sb, number % sb
        return row, slot, pick([sources[s][0] for s in range(STEPS)], row // group), hit // JB, hit % JB

    def fetch_early(m, carry):
        row, slot, source, a_slot, j = fetch(0, m)
        plan[0, m] = j
        for i, arrays in enumerate(a_refs):
            for (f, e), ref in zip(chunks[:-1], arrays):

                @pl.when((source == i) & (a_slot >= f) & (a_slot < e))
                def _():
                    pltpu.make_async_copy(ref.at[rows_of(a_slot - f, blk)], a_buf.at[m], sems.at[0, m]).start()

        start_b(row, slot, b_buf.at[m], sems.at[1, m])
        return carry

    def fetch_late(m, carry):
        row, slot, source, a_slot, j = fetch(1, m)
        late[1 + 3 * m] = source
        late[2 + 3 * m] = a_slot - last_first
        late[3 + 3 * m] = j
        start_b(row, slot, b_late.at[rows_of(m, blk)], late_sems.at[m])
        return carry

    lax.fori_loop(0, n_early, fetch_early, 0)
    lax.fori_loop(0, n_late, fetch_late, 0)
    counts = (n_early, n_late)
    late[0] = counts[1]

    def pair(m):
        for which, buf in enumerate((a_buf, b_buf)):
            pltpu.make_async_copy(buf.at[m], buf.at[m], sems.at[which, m]).wait()
        return a_buf[m], b_buf[m]

    add_products(counts[0], lambda m: plan[0, m], pair, c_ref)

    def wait(m, carry):
        into = b_late.at[rows_of(m, blk)]
        pltpu.make_async_copy(into, into, late_sems.at[m]).wait()
        return carry

    lax.fori_loop(0, counts[1], wait, 0)


def late_kernel(n_a, late, c_in, b_late, *refs):
    a_refs, (c_ref, total, a_buf, touched, sems, c_sems) = refs[:n_a], refs[n_a:]
    blk = a_buf.shape[1]
    columns = [pl.ds(j * blk, blk) for j in range(JB)]

    def fetch(m, carry):
        start_from(a_refs, late[1 + 3 * m], rows_of(late[2 + 3 * m], blk), a_buf.at[m], sems.at[m])
        touched[late[3 + 3 * m]] = jnp.int32(1)
        return carry

    def pair(m):
        pltpu.make_async_copy(a_buf.at[m], a_buf.at[m], sems.at[m]).wait()
        return a_buf[m], b_late[rows_of(m, blk), :]

    for j in range(JB):
        touched[j] = jnp.int32(0)
    lax.fori_loop(0, late[0], fetch, 0)
    for j, part in enumerate(columns):

        @pl.when(touched[j] == 0)
        def _():
            pltpu.make_async_copy(c_in.at[:, part], c_ref.at[:, part], c_sems.at[j]).start()

        @pl.when(touched[j] != 0)
        def _():
            total[:, part] = c_in[:, part]

    add_products(late[0], lambda m: late[3 + 3 * m], pair, total)
    for j, part in enumerate(columns):

        @pl.when(touched[j] != 0)
        def _():
            pltpu.make_async_copy(total.at[:, part], c_ref.at[:, part], c_sems.at[j]).start()

    for j, part in enumerate(columns):
        pltpu.make_async_copy(total.at[:, part], c_ref.at[:, part], c_sems.at[j]).wait()


def add_early(chunks, a_sources, b_sources, slots, a_at, b_at):
    group, sb = slots
    b_flat = [array for held in b_sources for _, array in held]
    blk = b_flat[0].shape[1]
    most = STEPS * group * sb
    tails = STEPS * (1 + group)
    n_a = len(a_sources)
    first = chunks[:-1] or chunks
    buffers = [pltpu.VMEM((most, blk, blk), jnp.float32)] * 2 + [pltpu.SemaphoreType.DMA((2, most))]
    band = jax.ShapeDtypeStruct((blk, JB * blk), jnp.float32)
    late, c_early, b_late = pl.pallas_call(
        functools.partial(
            early_kernel, chunks, n_a, [[first for first, _ in held] for held in b_sources], slots, a_at, b_at
        ),
        out_shape=[
            jax.ShapeDtypeStruct((1 + 3 * most,), jnp.int32),
            band,
            jax.ShapeDtypeStruct((most * blk, blk), jnp.float32),
        ],
        in_specs=[ANY] * (n_a * len(first) + len(b_flat)),
        out_specs=[SMEM, VMEM, ANY],
        scratch_shapes=[
            pltpu.VMEM((tails, TAIL, blk), jnp.float32),
            pltpu.VMEM((max(8, STEPS * group), blk), jnp.int32),
            pltpu.SMEM((max(8, STEPS * group), blk), jnp.int32),
            pltpu.SMEM((2, most + 1), jnp.int32),
            *buffers,
            pltpu.SemaphoreType.DMA((most,)),
            pltpu.SemaphoreType.DMA((tails + 1,)),
        ],
        compiler_params=pltpu.CompilerParams(vmem_limit_bytes=12 * MIB),
        cost_estimate=pl.CostEstimate(flops=6 * 8 * blk**3, bytes_accessed=8 * MIB, transcendentals=0),
        name="early",
    )(*[x for arrays in a_sources for x in arrays[: len(first)]], *b_flat)
    return late, c_early, b_late


def add_late(late, c_early, b_late, a_last):
    blk = a_last[0].shape[1]
    most = (late.shape[0] - 1) // 3
    return pl.pallas_call(
        functools.partial(late_kernel, len(a_last)),
        out_shape=jax.ShapeDtypeStruct(c_early.shape, c_early.dtype),
        in_specs=[SMEM, VMEM, VMEM] + [ANY] * len(a_last),
        out_specs=ANY,
        scratch_shapes=[
            pltpu.VMEM(c_early.shape, jnp.float32),
            pltpu.VMEM((most, blk, blk), jnp.float32),
            pltpu.SMEM((JB,), jnp.int32),
            pltpu.SemaphoreType.DMA((most,)),
            pltpu.SemaphoreType.DMA((JB,)),
        ],
        compiler_params=pltpu.CompilerParams(vmem_limit_bytes=12 * MIB),
        cost_estimate=pl.CostEstimate(flops=6 * 2 * blk**3, bytes_accessed=2 * MIB, transcendentals=0),
        name="late",
    )(late, c_early, b_late, *a_last)


def collect_kernel(n, at, *refs):
    sources, outs, sems = refs[:n], refs[n : n + 2 * STEPS], refs[n + 2 * STEPS]
    half = outs[0].shape[0]
    for i, out in enumerate(outs):
        part = pl.ds(half if i % 2 else 0, out.shape[0])
        views = [ref.at[part] for ref in sources[:-2]] + [sources[len(sources) - 2 + i % 2]]
        for j, view in enumerate(views):

            @pl.when(at(i // 2) == j)
            def _():
                pltpu.make_async_copy(view, out, sems.at[i]).start()

    for i, out in enumerate(outs):
        pltpu.make_async_copy(out, out, sems.at[i]).wait()


def collect(whole, halves, at):
    rows, blk = whole[0].shape
    sources = [*whole, *halves]
    sizes = [x.shape[0] for x in halves] * STEPS
    return pl.pallas_call(
        functools.partial(collect_kernel, len(sources), at),
        out_shape=[jax.ShapeDtypeStruct((size, blk), whole[0].dtype) for size in sizes],
        in_specs=[ANY] * len(sources),
        out_specs=[VMEM] * len(sizes),
        scratch_shapes=[pltpu.SemaphoreType.DMA((len(sizes),))],
        compiler_params=pltpu.CompilerParams(vmem_limit_bytes=8 * MIB),
        cost_estimate=pl.CostEstimate(flops=0, bytes_accessed=4 * MIB, transcendentals=0),
        name="collect",
    )(*sources)


def as_rows(x):
    return x.reshape(-1, x.shape[-1])


def gathered(a_vals, a_code, b_vals, b_code, panels, group):
    chunks = [(0, a_vals.shape[0])]
    _, a_own, b_own = prepare(chunks, a_code, b_code, panels, as_rows(a_vals), as_rows(b_vals))
    a_all = lax.all_gather(a_own, "col")
    b_all = lax.all_gather(b_own, "row")
    a_sources, b_sources = [], []
    for step in range(STEPS):
        a_sources.append([lax.dynamic_index_in_dim(a_all, panels[step], 0, keepdims=False)])
        for g in range(group):
            b_sources.append([(0, lax.dynamic_index_in_dim(b_all, panels[step] * group + g, 0, keepdims=False))])
    slots = (group, b_vals.shape[0])
    early = add_early(chunks, a_sources, b_sources, slots, lambda s: s, lambda s, g: s * group + g)
    return add_late(*early, [arrays[-1] for arrays in a_sources])


CHUNKS = [(0, 8), (8, 16)]
ROUTES = {
    (0, 1): [(None, ((0, 1), (1, 2))), (0, ((1, 2), (2, 3))), (1, ((2, 3), (3, 0)))],
    (0, 2): [(None, ((0, 1), (2, 3))), (0, ((1, 2), (3, 1))), (1, ((1, 0), (2, 3)))],
    (0, 3): [(None, ((0, 1), (3, 2))), (0, ((1, 2), (2, 1))), (1, ((2, 3), (1, 0)))],
    (1, 2): [(None, ((1, 0), (2, 3))), (None, ((1, 2), (2, 1))), (1, ((1, 0), (2, 3)))],
}
WRITTEN = ("0a", "0b", "x", "y", "g", "h", "1a", "1b", "2a", "2b", "s", "t", "u", "v")
WAITS = {
    (0, 1): {"1b": ("x", "y"), "v": ("2a",), "u": ("s", "g")},
    (0, 2): {"u": ("s",), "v": ("s", "2a")},
    (0, 3): {"u": ("s",), "v": ("s", "2a")},
    (1, 2): {"2b": ("0b", "g", "h"), "2a": ("0a",)},
}


def route_of(roots, n):
    mirror = roots not in ROUTES
    key = tuple(sorted(n - 1 - p for p in roots)) if mirror else roots
    steps, brings = [], []
    for source, pairs in ROUTES[key]:
        if mirror:
            pairs = tuple((n - 1 - x, n - 1 - y) for x, y in pairs)
        steps.append((source, pairs))
        brings.append({y: x if source is None else brings[source][x] for x, y in pairs})
    return steps, brings, WAITS[key]


def pick(values, index):
    out = jnp.asarray(values[0], jnp.int32)
    for i, value in enumerate(values[1:], 1):
        out = jnp.where(index == i, jnp.asarray(value, jnp.int32), out)
    return out


def pair_branch(roots, n, slots, pieces, b_own):
    group, sb = slots
    half = sb // 2
    blk = b_own.shape[1]
    parts = "abcdefgh"[: len(pieces)]

    def exchange(bit):
        return "row", [(r, r ^ bit) for r in range(n * group)]

    def from_chip(s):
        return (lax.axis_index("row") >> 1) ^ roots[s]

    moves = {"x": ("o", *exchange(group)), "y": ("o", *exchange(2 * group))}
    moves.update(g=("first of y", *exchange(group)), h=("last of x", *exchange(2 * group)))
    moves.update({name: ("own " + name, *exchange(1)) for name in "stuv"})
    held = dict(zip(parts, pieces), o=b_own)
    a_names = [list(parts)]
    a_table = [[0] * n for _ in roots]
    steps, brings, waits = route_of(roots, n)
    for number, (source, pairs) in enumerate(steps):
        for at, p in brings[number].items():
            a_table[roots.index(p)][at] = len(a_names)
        for part in parts:
            moves[f"{number}{part}"] = (part if source is None else f"{source}{part}", "col", pairs)
        a_names.append([f"{number}{part}" for part in parts])

    while moves:
        for name in [name for name in WRITTEN if name in moves]:
            source, axis, pairs = moves[name]
            if name == "g" and "y" in held:
                held[source] = held["y"][: half * blk]
            if name == "h" and "x" in held:
                held[source] = held["x"][half * blk :]
            if name == "s" and source not in held and all(e in held for e in ("x", "y", "g", "h", *waits.get("p", ()))):
                last = held["h"]
                if "p" in waits:
                    last = lax.optimization_barrier((last, *[held[e] for e in waits["p"]]))[0]
                halves = collect([held[e] for e in "oxy"], [held["g"], last], from_chip)
                held.update({"own " + name: x for name, x in zip("stuv", halves)})
            if all(e in held for e in (source, *waits.get(name, ()))):
                x = held[source]
                if name in waits:
                    x = lax.optimization_barrier((x, *[held[e] for e in waits[name]]))[0]
                held[name] = lax.ppermute(x, axis, pairs)
                del moves[name]

    a_sources = [[held[name] for name in names] for names in a_names]
    b_sources = [[(0, held[name])] for name in "oxy"]
    b_sources += [[(0, held[name]), (half, held[other])] for name, other in ("gh", "st", "uv")]

    def a_at(s):
        return pick(a_table[s], lax.axis_index("col"))

    def b_at(s, g):
        return jnp.where((lax.axis_index("row") & 1) == g, from_chip(s), n + s)

    early = add_early(CHUNKS, a_sources, b_sources, slots, a_at, b_at)
    return early, [arrays[-1] for arrays in a_sources[1:]]


def shards(a_vals, a_code, b_vals, b_code, panels):
    n = lax.axis_size("col")
    group = lax.axis_size("row") // n
    if group != 2 or n != 4:
        return gathered(a_vals, a_code, b_vals, b_code, panels, group)
    which, *pieces, b_own = prepare(CHUNKS, a_code, b_code, panels, as_rows(a_vals), as_rows(b_vals))
    slots = (group, b_vals.shape[0])
    branches = [functools.partial(pair_branch, pair, n, slots) for pair in itertools.combinations(range(n), 2)]
    early, a_last = lax.switch(which[0], branches, pieces, b_own)
    return add_late(*early, [pieces[-1], *a_last])


def solution(mesh):
    return jax.shard_map(
        shards,
        mesh=mesh,
        in_specs=(
            P("row", "col", None),
            P("row", "col"),
            P("row", "col", None),
            P("row", "col"),
            P(),
        ),
        out_specs=P("row", "col"),
        check_vma=False,
    )
```

```python
import functools
import itertools

import jax
import jax.numpy as jnp
from jax import lax
from jax.experimental import pallas as pl
from jax.experimental.pallas import tpu as pltpu
from jax.sharding import PartitionSpec as P

KPB = 64
STEPS = 2
JB = 8
TAIL = 8
MIB = 2**20

SMEM = pl.BlockSpec(memory_space=pltpu.SMEM)
VMEM = pl.BlockSpec(memory_space=pltpu.VMEM)
ANY = pl.BlockSpec(memory_space=pl.ANY)


def rows_of(slot, blk):
    return pl.ds(pl.multiple_of(slot * blk, blk), blk)


def prepare_kernel(chunks, a_code, b_code, panels, a_rows, b_rows, which, *refs):
    outs, (a_small, b_small, panels_s, sems) = refs[:-4], refs[-4:]
    blk = a_rows.shape[1]
    small = [(panels, panels_s), (a_code, a_small), (b_code, b_small)]
    small = [pltpu.make_async_copy(x, y, sems.at[len(outs) + i]) for i, (x, y) in enumerate(small)]
    for copy in small:
        copy.start()
    parts = [a_rows.at[pl.ds(f * blk, (e - f) * blk)] for f, e in chunks] + [b_rows]
    copies = [
        pltpu.make_async_copy(part, out.at[pl.ds(0, part.shape[0])], sems.at[i])
        for i, (part, out) in enumerate(zip(parts, outs))
    ]
    for copy in copies:
        copy.start()
    for copy in small:
        copy.wait()
    for code, out in ((a_small, outs[0]), (b_small, outs[-1])):
        last = out.shape[0] - TAIL
        out[last:, :] = jnp.zeros((TAIL, blk), jnp.float32)
        out[last : last + 1, 0 : code.shape[1]] = code[...].astype(jnp.float32)
    lo = jnp.minimum(panels_s[0], panels_s[1])
    hi = jnp.maximum(panels_s[0], panels_s[1])
    which[0] = jnp.where(lo == 0, 0, lo + 1) + hi - 1
    for copy in copies:
        copy.wait()


def prepare(chunks, a_code, b_code, panels, a_rows, b_rows):
    blk = a_rows.shape[1]
    sizes = [(e - f) * blk for f, e in chunks]
    sizes[0] += TAIL
    sizes.append(b_rows.shape[0] + TAIL)
    return pl.pallas_call(
        functools.partial(prepare_kernel, chunks),
        out_shape=[jax.ShapeDtypeStruct((1,), jnp.int32)] + [jax.ShapeDtypeStruct((x, blk), jnp.float32) for x in sizes],
        in_specs=[ANY] * 5,
        out_specs=[SMEM] + [VMEM] * len(sizes),
        scratch_shapes=[
            pltpu.VMEM(a_code.T.shape, jnp.int32),
            pltpu.VMEM(b_code.T.shape, jnp.int32),
            pltpu.SMEM(panels.shape, jnp.int32),
            pltpu.SemaphoreType.DMA((len(sizes) + 3,)),
        ],
        name="prepare",
    )(a_code.T, b_code.T, panels, a_rows, b_rows)


def split(x):
    high = x.astype(jnp.bfloat16)
    low = (x - high.astype(jnp.float32)).astype(jnp.bfloat16)
    return high, low


def product(a, b):
    a_high, a_low = split(a)
    b_high, b_low = split(b)
    left = jnp.concatenate([a_high, a_high, a_low], axis=1)
    right = jnp.concatenate([b_high, b_low, b_high], axis=0)
    return jnp.dot(left, right, preferred_element_type=jnp.float32)


def add_products(count, column, pair, c_ref):
    blk = c_ref.shape[0]

    def add(m, value):
        c_ref[:, rows_of(column(m), blk)] += value

    def two(i, carry):
        m = 2 * i
        (a, b), (a_next, b_next) = pair(m), pair(m + 1)
        first, second = product(a, b), product(a_next, b_next)
        add(m, first)
        add(m + 1, second)
        return carry

    lax.fori_loop(0, count // 2, two, 0)

    @pl.when(count % 2 == 1)
    def _():
        add(count - 1, product(*pair(count - 1)))


def start_from(refs, source, rows, into, sem):
    for i, ref in enumerate(refs):

        @pl.when(source == i)
        def _():
            pltpu.make_async_copy(ref.at[rows], into, sem).start()


def early_kernel(chunks, n_a, b_parts, slots, a_at, b_at, *refs):
    group, sb = slots
    parts = max(1, len(chunks) - 1)
    n_b = sum(len(firsts) for firsts in b_parts)
    a_refs = [refs[i * parts : (i + 1) * parts] for i in range(n_a)]
    flat = iter(refs[n_a * parts : n_a * parts + n_b])
    b_refs = [[(first, next(flat)) for first in firsts] for firsts in b_parts]
    late, c_ref, b_late, tails, found, found_s, plan, a_buf, b_buf, sems, late_sems, tail_sems = refs[n_a * parts + n_b :]
    sa = chunks[-1][1]
    last_first = chunks[-1][0]
    blk = a_buf.shape[1]
    k_rows = KPB // group
    sources = [[a_at(s)] + [b_at(s, g) for g in range(group)] for s in range(STEPS)]

    def tail(s, i):
        return s * (1 + group) + i

    for s in range(STEPS):
        for i, source in enumerate(sources[s]):
            for j, holder in enumerate([held[-1][1] for held in b_refs] if i else [arrays[0] for arrays in a_refs]):

                @pl.when(source == j)
                def _():
                    rows = pl.ds(holder.shape[0] - TAIL, TAIL)
                    pltpu.make_async_copy(holder.at[rows], tails.at[tail(s, i)], tail_sems.at[tail(s, i)]).start()

    c_ref[...] = jnp.zeros_like(c_ref)
    found[...] = jnp.full_like(found, -1)
    for i in range(STEPS * (1 + group)):
        pltpu.make_async_copy(tails.at[i], tails.at[i], tail_sems.at[i]).wait()

    for s in range(STEPS):
        a_codes = tails[tail(s, 0), 0:1, :].astype(jnp.int32)
        for g in range(group):
            b_codes = tails[tail(s, 1 + g), 0:1, :].astype(jnp.int32)
            used = (b_codes >= 0) & (lax.broadcasted_iota(jnp.int32, b_codes.shape, 1) < sb)
            k = jnp.where(used, g * k_rows + b_codes // JB, -2)
            hit = jnp.full_like(k, -1)
            for slot in range(sa):
                hit = jnp.where(a_codes[:, slot : slot + 1] == k, slot, hit)
            found[s * group + g : s * group + g + 1, :] = jnp.where(hit >= 0, hit * JB + b_codes % JB, -1)
    copy = pltpu.make_async_copy(found, found_s, tail_sems.at[STEPS * (1 + group)])
    copy.start()
    copy.wait()

    n_early = n_late = jnp.int32(0)
    for row in range(STEPS * group):
        for slot in range(sb):
            hit = found_s[row, slot]
            entry = hit + (row * sb + slot) * sa * JB
            is_late = hit >= last_first * JB
            plan[0, n_early] = entry
            plan[1, n_late] = entry
            n_early += ((hit >= 0) & jnp.logical_not(is_late)).astype(jnp.int32)
            n_late += is_late.astype(jnp.int32)

    def start_b(row, slot, into, sem):
        source = pick([sources[s][1 + g] for s in range(STEPS) for g in range(group)], row)
        for i, held in enumerate(b_refs):

            @pl.when(source == i)
            def _():
                for j, (first, ref) in enumerate(held):
                    end = held[j + 1][0] if j + 1 < len(held) else sb

                    @pl.when((slot >= first) & (slot < end))
                    def _():
                        pltpu.make_async_copy(ref.at[rows_of(slot - first, blk)], into, sem).start()

    def fetch(which, m):
        number, hit = plan[which, m] // (sa * JB), plan[which, m] % (sa * JB)
        row, slot = number // sb, number % sb
        return row, slot, pick([sources[s][0] for s in range(STEPS)], row // group), hit // JB, hit % JB

    def fetch_early(m, carry):
        row, slot, source, a_slot, j = fetch(0, m)
        plan[0, m] = j
        for i, arrays in enumerate(a_refs):
            for (f, e), ref in zip(chunks[:-1], arrays):

                @pl.when((source == i) & (a_slot >= f) & (a_slot < e))
                def _():
                    pltpu.make_async_copy(ref.at[rows_of(a_slot - f, blk)], a_buf.at[m], sems.at[0, m]).start()

        start_b(row, slot, b_buf.at[m], sems.at[1, m])
        return carry

    def fetch_late(m, carry):
        row, slot, source, a_slot, j = fetch(1, m)
        late[1 + 3 * m] = source
        late[2 + 3 * m] = a_slot - last_first
        late[3 + 3 * m] = j
        start_b(row, slot, b_late.at[rows_of(m, blk)], late_sems.at[m])
        return carry

    lax.fori_loop(0, n_early, fetch_early, 0)
    lax.fori_loop(0, n_late, fetch_late, 0)
    counts = (n_early, n_late)
    late[0] = counts[1]

    def pair(m):
        for which, buf in enumerate((a_buf, b_buf)):
            pltpu.make_async_copy(buf.at[m], buf.at[m], sems.at[which, m]).wait()
        return a_buf[m], b_buf[m]

    add_products(counts[0], lambda m: plan[0, m], pair, c_ref)

    def wait(m, carry):
        into = b_late.at[rows_of(m, blk)]
        pltpu.make_async_copy(into, into, late_sems.at[m]).wait()
        return carry

    lax.fori_loop(0, counts[1], wait, 0)


def late_kernel(n_a, late, c_in, b_late, *refs):
    a_refs, (c_ref, a_buf, sems) = refs[:n_a], refs[n_a:]
    blk = a_buf.shape[1]

    def fetch(m, carry):
        start_from(a_refs, late[1 + 3 * m], rows_of(late[2 + 3 * m], blk), a_buf.at[m], sems.at[m])
        return carry

    def pair(m):
        pltpu.make_async_copy(a_buf.at[m], a_buf.at[m], sems.at[m]).wait()
        return a_buf[m], b_late[rows_of(m, blk), :]

    lax.fori_loop(0, late[0], fetch, 0)
    c_ref[...] = c_in[...]
    add_products(late[0], lambda m: late[3 + 3 * m], pair, c_ref)


def add_early(chunks, a_sources, b_sources, slots, a_at, b_at):
    group, sb = slots
    b_flat = [array for held in b_sources for _, array in held]
    blk = b_flat[0].shape[1]
    most = STEPS * group * sb
    tails = STEPS * (1 + group)
    n_a = len(a_sources)
    first = chunks[:-1] or chunks
    buffers = [pltpu.VMEM((most, blk, blk), jnp.float32)] * 2 + [pltpu.SemaphoreType.DMA((2, most))]
    band = jax.ShapeDtypeStruct((blk, JB * blk), jnp.float32)
    late, c_early, b_late = pl.pallas_call(
        functools.partial(
            early_kernel, chunks, n_a, [[first for first, _ in held] for held in b_sources], slots, a_at, b_at
        ),
        out_shape=[
            jax.ShapeDtypeStruct((1 + 3 * most,), jnp.int32),
            band,
            jax.ShapeDtypeStruct((most * blk, blk), jnp.float32),
        ],
        in_specs=[ANY] * (n_a * len(first) + len(b_flat)),
        out_specs=[SMEM, VMEM, ANY],
        scratch_shapes=[
            pltpu.VMEM((tails, TAIL, blk), jnp.float32),
            pltpu.VMEM((max(8, STEPS * group), blk), jnp.int32),
            pltpu.SMEM((max(8, STEPS * group), blk), jnp.int32),
            pltpu.SMEM((2, most + 1), jnp.int32),
            *buffers,
            pltpu.SemaphoreType.DMA((most,)),
            pltpu.SemaphoreType.DMA((tails + 1,)),
        ],
        compiler_params=pltpu.CompilerParams(vmem_limit_bytes=12 * MIB),
        cost_estimate=pl.CostEstimate(flops=6 * 8 * blk**3, bytes_accessed=8 * MIB, transcendentals=0),
        name="early",
    )(*[x for arrays in a_sources for x in arrays[: len(first)]], *b_flat)
    return late, c_early, b_late


def add_late(late, c_early, b_late, a_last):
    blk = a_last[0].shape[1]
    most = (late.shape[0] - 1) // 3
    return pl.pallas_call(
        functools.partial(late_kernel, len(a_last)),
        out_shape=jax.ShapeDtypeStruct(c_early.shape, c_early.dtype),
        in_specs=[SMEM, VMEM, VMEM] + [ANY] * len(a_last),
        out_specs=VMEM,
        scratch_shapes=[pltpu.VMEM((most, blk, blk), jnp.float32), pltpu.SemaphoreType.DMA((most,))],
        compiler_params=pltpu.CompilerParams(vmem_limit_bytes=12 * MIB),
        cost_estimate=pl.CostEstimate(flops=6 * 2 * blk**3, bytes_accessed=2 * MIB, transcendentals=0),
        name="late",
    )(late, c_early, b_late, *a_last)


def collect_kernel(n, at, *refs):
    sources, outs, sems = refs[:n], refs[n : n + 2 * STEPS], refs[n + 2 * STEPS]
    half = outs[0].shape[0]
    for i, out in enumerate(outs):
        part = pl.ds(half if i % 2 else 0, out.shape[0])
        views = [ref.at[part] for ref in sources[:-2]] + [sources[len(sources) - 2 + i % 2]]
        for j, view in enumerate(views):

            @pl.when(at(i // 2) == j)
            def _():
                pltpu.make_async_copy(view, out, sems.at[i]).start()

    for i, out in enumerate(outs):
        pltpu.make_async_copy(out, out, sems.at[i]).wait()


def collect(whole, halves, at):
    rows, blk = whole[0].shape
    sources = [*whole, *halves]
    sizes = [x.shape[0] for x in halves] * STEPS
    return pl.pallas_call(
        functools.partial(collect_kernel, len(sources), at),
        out_shape=[jax.ShapeDtypeStruct((size, blk), whole[0].dtype) for size in sizes],
        in_specs=[ANY] * len(sources),
        out_specs=[VMEM] * len(sizes),
        scratch_shapes=[pltpu.SemaphoreType.DMA((len(sizes),))],
        compiler_params=pltpu.CompilerParams(vmem_limit_bytes=8 * MIB),
        cost_estimate=pl.CostEstimate(flops=0, bytes_accessed=4 * MIB, transcendentals=0),
        name="collect",
    )(*sources)


def as_rows(x):
    return x.reshape(-1, x.shape[-1])


def gathered(a_vals, a_code, b_vals, b_code, panels, group):
    chunks = [(0, a_vals.shape[0])]
    _, a_own, b_own = prepare(chunks, a_code, b_code, panels, as_rows(a_vals), as_rows(b_vals))
    a_all = lax.all_gather(a_own, "col")
    b_all = lax.all_gather(b_own, "row")
    a_sources, b_sources = [], []
    for step in range(STEPS):
        a_sources.append([lax.dynamic_index_in_dim(a_all, panels[step], 0, keepdims=False)])
        for g in range(group):
            b_sources.append([(0, lax.dynamic_index_in_dim(b_all, panels[step] * group + g, 0, keepdims=False))])
    slots = (group, b_vals.shape[0])
    early = add_early(chunks, a_sources, b_sources, slots, lambda s: s, lambda s, g: s * group + g)
    return add_late(*early, [arrays[-1] for arrays in a_sources])


CHUNKS = [(0, 8), (8, 16)]
ROUTES = {
    (0, 1): [(None, ((0, 1), (1, 2))), (0, ((1, 2), (2, 3))), (1, ((2, 3), (3, 0)))],
    (0, 2): [(None, ((0, 1), (2, 3))), (0, ((1, 2), (3, 1))), (1, ((1, 0), (2, 3)))],
    (0, 3): [(None, ((0, 1), (3, 2))), (0, ((1, 2), (2, 1))), (1, ((2, 3), (1, 0)))],
    (1, 2): [(None, ((1, 0), (2, 3))), (None, ((1, 2), (2, 1))), (1, ((1, 0), (2, 3)))],
}
WRITTEN = ("0a", "0b", "x", "y", "g", "h", "1a", "1b", "2a", "2b", "s", "t", "u", "v")
WAITS = {
    (0, 1): {"1b": ("x", "y"), "v": ("2a",), "u": ("s", "g")},
    (0, 2): {"u": ("s",), "v": ("s", "2a")},
    (0, 3): {"u": ("s",), "v": ("s", "2a")},
    (1, 2): {"2b": ("0b", "g", "h"), "2a": ("0a",)},
}


def route_of(roots, n):
    mirror = roots not in ROUTES
    key = tuple(sorted(n - 1 - p for p in roots)) if mirror else roots
    steps, brings = [], []
    for source, pairs in ROUTES[key]:
        if mirror:
            pairs = tuple((n - 1 - x, n - 1 - y) for x, y in pairs)
        steps.append((source, pairs))
        brings.append({y: x if source is None else brings[source][x] for x, y in pairs})
    return steps, brings, WAITS[key]


def pick(values, index):
    out = jnp.asarray(values[0], jnp.int32)
    for i, value in enumerate(values[1:], 1):
        out = jnp.where(index == i, jnp.asarray(value, jnp.int32), out)
    return out


def pair_branch(roots, n, slots, pieces, b_own):
    group, sb = slots
    half = sb // 2
    blk = b_own.shape[1]
    parts = "abcdefgh"[: len(pieces)]

    def exchange(bit):
        return "row", [(r, r ^ bit) for r in range(n * group)]

    def from_chip(s):
        return (lax.axis_index("row") >> 1) ^ roots[s]

    moves = {"x": ("o", *exchange(group)), "y": ("o", *exchange(2 * group))}
    moves.update(g=("first of y", *exchange(group)), h=("last of x", *exchange(2 * group)))
    moves.update({name: ("own " + name, *exchange(1)) for name in "stuv"})
    held = dict(zip(parts, pieces), o=b_own)
    a_names = [list(parts)]
    a_table = [[0] * n for _ in roots]
    steps, brings, waits = route_of(roots, n)
    for number, (source, pairs) in enumerate(steps):
        for at, p in brings[number].items():
            a_table[roots.index(p)][at] = len(a_names)
        for part in parts:
            moves[f"{number}{part}"] = (part if source is None else f"{source}{part}", "col", pairs)
        a_names.append([f"{number}{part}" for part in parts])

    while moves:
        for name in [name for name in WRITTEN if name in moves]:
            source, axis, pairs = moves[name]
            if name == "g" and "y" in held:
                held[source] = held["y"][: half * blk]
            if name == "h" and "x" in held:
                held[source] = held["x"][half * blk :]
            if name == "s" and source not in held and all(e in held for e in ("x", "y", "g", "h", *waits.get("p", ()))):
                last = held["h"]
                if "p" in waits:
                    last = lax.optimization_barrier((last, *[held[e] for e in waits["p"]]))[0]
                halves = collect([held[e] for e in "oxy"], [held["g"], last], from_chip)
                held.update({"own " + name: x for name, x in zip("stuv", halves)})
            if all(e in held for e in (source, *waits.get(name, ()))):
                x = held[source]
                if name in waits:
                    x = lax.optimization_barrier((x, *[held[e] for e in waits[name]]))[0]
                held[name] = lax.ppermute(x, axis, pairs)
                del moves[name]

    a_sources = [[held[name] for name in names] for names in a_names]
    b_sources = [[(0, held[name])] for name in "oxy"]
    b_sources += [[(0, held[name]), (half, held[other])] for name, other in ("gh", "st", "uv")]

    def a_at(s):
        return pick(a_table[s], lax.axis_index("col"))

    def b_at(s, g):
        return jnp.where((lax.axis_index("row") & 1) == g, from_chip(s), n + s)

    early = add_early(CHUNKS, a_sources, b_sources, slots, a_at, b_at)
    return early, [arrays[-1] for arrays in a_sources[1:]]


def shards(a_vals, a_code, b_vals, b_code, panels):
    n = lax.axis_size("col")
    group = lax.axis_size("row") // n
    if group != 2 or n != 4:
        return gathered(a_vals, a_code, b_vals, b_code, panels, group)
    which, *pieces, b_own = prepare(CHUNKS, a_code, b_code, panels, as_rows(a_vals), as_rows(b_vals))
    slots = (group, b_vals.shape[0])
    branches = [functools.partial(pair_branch, pair, n, slots) for pair in itertools.combinations(range(n), 2)]
    early, a_last = lax.switch(which[0], branches, pieces, b_own)
    return add_late(*early, [pieces[-1], *a_last])


def solution(mesh):
    return jax.shard_map(
        shards,
        mesh=mesh,
        in_specs=(
            P("row", "col", None),
            P("row", "col"),
            P("row", "col", None),
            P("row", "col"),
            P(),
        ),
        out_specs=P("row", "col"),
        check_vma=False,
    )
```
